256 devices in a mesh: head: 16 (over x, y), key: 8 (over z), row: 2 (over core).
Axes of the slice: x: 4, y: 4, z: 8, core: 2. Of those that a mesh axis runs over, the one named last changes fastest.
Arguments:
- mla_query: bfloat16 [256, 128, 576], P('row', 'head'), may hold values from -48 to 48
- mla_cache: bfloat16 [16, 2048, 576], P(None, 'key'), may hold values from -6 to 6
- index_query: bfloat16 [256, 64, 128], P('row'), may hold values from -24 to 24
- index_keys: bfloat16 [32768, 128], P(('head', 'key')), may hold values from -6 to 6
- index_weight: float32 [256, 64], P('row'), may hold values from -0.75 to 0.75
Outputs:
- query_grad: float32 [256, 64, 128], P('row', 'head')
- key_grad: float32 [32768, 128], P(('head', 'key', 'row'))
- weight_grad: float32 [256, 64], P('row')
The draws below stay inside these ranges and needn't reach their ends.
All inputs are finite; a program needn't handle non-finite values.
Results may differ from the reference program's by a relative error of at most 0.0029.
Values sent between devices are 32-bit elements; how exact they have to be, the bound alone decides.
No kernel may reach another device: no remote copies, remote signals or barrier semaphores. Data moves between devices by JAX's collectives and lax.ppermute only.
A program may use at most 128 MiB of HBM per device.

```python
import math
import jax
import jax.numpy as jnp
from jax import lax

MH = 128
KW = 576
IH = 64
DI = 128
ROWS = 256
KEYS = 32768
KBLK = 16
SUB = 2048


def pair_rows(row_count, offset):
    return (jnp.arange(8, dtype=jnp.int32) * (row_count // 8) + offset).astype(jnp.int32)


def aligned_keys(key, salt, total_rows, width):
    base_rows = jnp.clip(jax.random.normal(jax.random.fold_in(key, salt), (total_rows, width), jnp.float32), -6.0, 6.0)
    pair_spots = pair_rows(total_rows, total_rows // 16)
    blended = base_rows[pair_spots + 1]
    return base_rows.at[pair_spots + 1].set(blended)


def draw_mla_cache(key, part):
    key_rows = aligned_keys(key, 101, KEYS, KW)
    return key_rows.reshape(KBLK, SUB, KW).astype(jnp.bfloat16)


def draw_mla_query(key, part):
    key = jax.random.fold_in(key, 3)
    query_vals = jnp.clip(jax.random.normal(key, (ROWS, MH, KW), jnp.float32), -6.0, 6.0)
    return query_vals.astype(jnp.bfloat16)


def draw_index_keys(key, part):
    return aligned_keys(key, 201, KEYS, DI).astype(jnp.bfloat16)


def draw_index_query(key, part):
    key = jax.random.fold_in(key, 4)
    query_vals = jnp.clip(jax.random.normal(key, (ROWS, IH, DI), jnp.float32), -6.0, 6.0)
    return query_vals.astype(jnp.bfloat16)


def draw_index_weight(key, part):
    key = jax.random.fold_in(key, 5)
    weights = 0.125 * jnp.clip(jax.random.normal(key, (ROWS, IH), jnp.float32), -6.0, 6.0)
    return weights


def setup_inputs(seed: int = 0) -> dict:
    key_of = jax.random.split(jax.random.key(seed), 6)
    mla_query = draw_mla_query(jax.random.fold_in(key_of[5], 71), 0)
    mla_cache = draw_mla_cache(jax.random.fold_in(key_of[5], 71), 0)
    index_query = draw_index_query(jax.random.fold_in(key_of[5], 71), 0)
    index_keys = draw_index_keys(jax.random.fold_in(key_of[5], 71), 0)
    index_weight = draw_index_weight(jax.random.fold_in(key_of[5], 71), 0)
    return {"mla_query": mla_query, "mla_cache": mla_cache, "index_query": index_query, "index_keys": index_keys, "index_weight": index_weight}


def reference(mla_query, mla_cache, index_query, index_keys, index_weight):
    cache_rows = mla_cache.reshape(KEYS, KW)
    score_scale = 1.0 / math.sqrt(192.0)

    def mla_head(running, head_query):
        scores = jnp.dot(head_query, cache_rows.T, preferred_element_type=jnp.float32) * score_scale
        top_score = lax.optimization_barrier(jnp.max(scores, axis=1, keepdims=True))
        exp_terms = jnp.exp(scores - top_score)
        return (running + exp_terms / lax.optimization_barrier(jnp.sum(exp_terms, axis=1, keepdims=True)), None)
    target, _ = lax.scan(mla_head, jnp.zeros((ROWS, KEYS), jnp.float32), jnp.swapaxes(mla_query, 0, 1))
    target = target / MH
    root_width = math.sqrt(DI)
    heads_query = jnp.swapaxes(index_query, 0, 1)
    heads_weight = jnp.swapaxes(index_weight, 0, 1)

    def index_head(running, inputs):
        head_query, head_weight = inputs
        active = jnp.maximum(jnp.dot(head_query, index_keys.T, preferred_element_type=jnp.float32), 0.0)
        return (running + head_weight[:, None] * active, None)
    logits, _ = lax.scan(index_head, jnp.zeros((ROWS, KEYS), jnp.float32), (heads_query, heads_weight))
    logits = logits / root_width
    top_logit = lax.optimization_barrier(jnp.max(logits, axis=1, keepdims=True))
    exp_logit = jnp.exp(logits - top_logit)
    soft_probs = exp_logit / lax.optimization_barrier(jnp.sum(exp_logit, axis=1, keepdims=True))
    dlogits = KEYS * (soft_probs - target)

    def index_back(running, inputs):
        head_query, head_weight = inputs
        products = jnp.dot(head_query, index_keys.T, preferred_element_type=jnp.float32)
        active = jnp.maximum(products, 0.0)
        weight_row = lax.optimization_barrier(jnp.sum(active * dlogits, axis=1)) / root_width
        slope_terms = (dlogits * head_weight[:, None] * jnp.where(products > 0.0, 1.0, 0.0) / root_width).astype(jnp.bfloat16)
        query_row = jnp.dot(slope_terms, index_keys, preferred_element_type=jnp.float32)
        keys_row = jnp.dot(slope_terms.T, head_query, preferred_element_type=jnp.float32)
        return (running + keys_row, (weight_row, query_row))
    key_grad, (weight_rows, query_rows) = lax.scan(index_back, jnp.zeros((KEYS, DI), jnp.float32), (heads_query, heads_weight))
    query_grad = jnp.swapaxes(query_rows, 0, 1)
    weight_grad = jnp.swapaxes(weight_rows, 0, 1)
    return (query_grad, key_grad, weight_grad)
```

```python
import math

import jax
import jax.numpy as jnp
from jax import lax
from jax.experimental import pallas as pl
from jax.experimental.pallas import tpu as pltpu
from jax.sharding import PartitionSpec as P

MH = 128
LOG2E = 1.4426950408889634
SCORE2 = LOG2E / math.sqrt(192.0)
LANES = 128
NT = (((1,), (1,)), ((), ()))
TN = (((0,), (0,)), ((), ()))
NN = (((1,), (0,)), ((), ()))


def dot(a, b, dims):
    return lax.dot_general(a, b, dims, preferred_element_type=jnp.float32)


def lane_iota(rows):
    return lax.broadcasted_iota(jnp.int32, (rows, LANES), 1)


def forward_kernel(q_ref, k_ref, w_ref, logits_ref, stats_ref, qh_ref, wide, wpad):
    rows, heads, depth = q_ref.shape
    keys = k_ref.shape[0]
    group = 8
    wide[...] = q_ref[...].astype(jnp.float32).reshape(rows * heads, depth)
    wpad[...] = jnp.zeros_like(wpad)
    wpad[:, 0:heads] = w_ref[...]

    logits_ref[...] = jnp.zeros_like(logits_ref)

    def step(i, carry):
        weights = pltpu.roll(wpad[...], LANES - group * i, 1)
        for j in range(group):
            head = i * group + j
            qh_ref[head] = wide[pl.ds(head, rows, stride=heads), :].astype(jnp.bfloat16)
        chunk = qh_ref[pl.ds(i * group, group)].reshape(group * rows, depth)
        products = dot(chunk, k_ref[...], NT)
        total = logits_ref[...]
        for j in range(group):
            part = products[j * rows : (j + 1) * rows]
            total = total + jnp.maximum(part, 0.0) * weights[:, j : j + 1]
        logits_ref[...] = total
        return carry

    lax.fori_loop(0, heads // group, step, 0)
    logits = logits_ref[...] * (1.0 / math.sqrt(depth))
    logits_ref[...] = logits
    top = jnp.max(logits, axis=1, keepdims=True)
    total = jnp.sum(jnp.exp(logits - top), axis=1, keepdims=True)
    lane = lane_iota(rows)
    packed = jnp.where(lane == 0, top, jnp.where(lane == 1, total, 0.0))
    stats_ref[...] = packed.T[0:8]


def indexer_forward(index_query, index_keys, index_weight):
    rows, heads, depth = index_query.shape
    keys = index_keys.shape[0]
    return pl.pallas_call(
        forward_kernel,
        out_shape=(
            jax.ShapeDtypeStruct((rows, keys), jnp.float32),
            jax.ShapeDtypeStruct((8, rows), jnp.float32),
            jax.ShapeDtypeStruct((heads, rows, depth), jnp.bfloat16),
        ),
        scratch_shapes=[
            pltpu.VMEM((rows * heads, depth), jnp.float32),
            pltpu.VMEM((rows, LANES), jnp.float32),
        ],
        compiler_params=pltpu.CompilerParams(vmem_limit_bytes=40 << 20),
        name="indexer_forward",
    )(index_query, index_keys, index_weight)


def scores_kernel(q_ref, c_ref, lstats_ref, e_ref, tops_ref, send_ref, wide, qh, sums):
    rows, heads, width = q_ref.shape
    step = pl.program_id(0)
    steps = pl.num_programs(0)
    pair = c_ref.shape[0]
    lane = lane_iota(2 * rows)

    @pl.when(step == 0)
    def _():
        for k in range(0, width, LANES):
            size = min(LANES, width - k)
            piece = q_ref[:, :, k : k + size].astype(jnp.float32)
            wide[:, 0:size] = piece.reshape(rows * heads, size)
            for h in range(heads):
                strided = wide[pl.ds(h, rows, stride=heads), :]
                qh[h * rows : (h + 1) * rows, k : k + size] = strided[:, 0:size].astype(jnp.bfloat16)
        tops_ref[...] = jnp.zeros_like(tops_ref)
        sums[...] = jnp.zeros_like(sums)

    for h in range(0, heads, 2):
        span = slice(h * rows, (h + 2) * rows)
        queries = qh[span]
        blocks = [dot(queries, c_ref[j], NT) for j in range(pair)]
        top = blocks[0]
        for block in blocks[1:]:
            top = jnp.maximum(top, block)
        top = jnp.max(top, axis=1, keepdims=True)
        total = None
        for j, block in enumerate(blocks):
            terms = jnp.exp2((block - top) * SCORE2)
            total = terms if total is None else total + terms
            e_ref[j, h : h + 2] = terms.astype(jnp.bfloat16).reshape(2, rows, terms.shape[1])
        total = jnp.sum(total, axis=1, keepdims=True)
        tops_ref[span] = jnp.where(lane == step, top, tops_ref[span])
        sums[span] = jnp.where(lane == step, total, sums[span])

    @pl.when(step == steps - 1)
    def _():
        lane1 = lane_iota(rows)
        used = lane1 < steps
        packed = jnp.zeros((rows, LANES), jnp.float32)
        for h in range(heads):
            tops = tops_ref[h * rows : (h + 1) * rows]
            top = jnp.max(jnp.where(used, tops, -jnp.inf), axis=1, keepdims=True)
            scaled = sums[h * rows : (h + 1) * rows] * jnp.exp2(jnp.where(used, tops - top, 0.0) * SCORE2)
            total = jnp.sum(jnp.where(used, scaled, 0.0), axis=1, keepdims=True)
            packed = jnp.where(lane1 == h, top, packed)
            packed = jnp.where(lane1 == heads + h, total, packed)
        flat = packed.T[0 : 2 * heads]
        for z in range(send_ref.shape[0]):
            send_ref[z, 0 : 2 * heads] = flat
            send_ref[z, 2 * heads :] = lstats_ref[...]


def attention_scores(mla_query, mla_cache, lstats, key_count):
    rows, heads, width = mla_query.shape
    blocks, keys, _ = mla_cache.shape
    pair = 2
    steps = blocks // pair
    return pl.pallas_call(
        scores_kernel,
        grid=(steps,),
        in_specs=[
            pl.BlockSpec((rows, heads, width), lambda i: (0, 0, 0)),
            pl.BlockSpec((pair, keys, width), lambda i: (i, 0, 0)),
            pl.BlockSpec((8, rows), lambda i: (0, 0)),
        ],
        out_specs=(
            pl.BlockSpec((pair, heads, rows, keys), lambda i: (i, 0, 0, 0)),
            pl.BlockSpec((heads * rows, LANES), lambda i: (0, 0)),
            pl.BlockSpec((key_count, 2 * heads + 8, rows), lambda i: (0, 0, 0)),
        ),
        out_shape=(
            jax.ShapeDtypeStruct((blocks, heads, rows, keys), jnp.bfloat16),
            jax.ShapeDtypeStruct((heads * rows, LANES), jnp.float32),
            jax.ShapeDtypeStruct((key_count, 2 * heads + 8, rows), jnp.float32),
        ),
        scratch_shapes=[
            pltpu.VMEM((rows * heads, LANES), jnp.float32),
            pltpu.VMEM((rows * heads, width), jnp.bfloat16),
            pltpu.VMEM((rows * heads, LANES), jnp.float32),
        ],
        compiler_params=pltpu.CompilerParams(vmem_limit_bytes=48 << 20),
        name="attention_scores",
    )(mla_query, mla_cache, lstats)


def headsum_kernel(e_ref, tops_ref, got_ref, out_ref, weights, tail, square):
    pair, heads, rows, keys = e_ref.shape
    step = pl.program_id(0)
    lane = lane_iota(rows)

    @pl.when(step == 0)
    def _():
        tops = got_ref[:, 0:heads]
        top = jnp.max(tops, axis=0)
        total = jnp.sum(got_ref[:, heads : 2 * heads] * jnp.exp2((tops - top[None]) * SCORE2), axis=0)
        square[...] = jnp.zeros_like(square)
        square[0:heads] = top
        square[heads : 2 * heads] = (1.0 / MH) / total
        columns = square[...].T
        for h in range(heads):
            local = tops_ref[h * rows : (h + 1) * rows] - columns[:, h : h + 1]
            scale = columns[:, heads + h : heads + h + 1]
            weights[h] = jnp.exp2(jnp.minimum(local * SCORE2, 0.0)) * scale
        ltops = got_ref[:, 2 * heads : 2 * heads + 1]
        ltop = jnp.max(ltops, axis=0)
        lsum = jnp.sum(got_ref[:, 2 * heads + 1 : 2 * heads + 2] * jnp.exp(ltops - ltop[None]), axis=0)
        tail[...] = jnp.zeros_like(tail)
        tail[0:1, 0:rows] = ltop
        tail[1:2, 0:rows] = lsum

    columns = []
    for h in range(heads):
        columns.append(jnp.sum(jnp.where(lane == step, weights[h], 0.0), axis=1, keepdims=True))
    for j in range(pair):
        total = e_ref[j, 0].astype(jnp.float32) * columns[0]
        for h in range(1, heads):
            total = total + e_ref[j, h].astype(jnp.float32) * columns[h]
        out_ref[j, 0:rows] = total
        out_ref[j, rows:] = tail[...]


def head_sum(terms, tops, got):
    blocks, heads, rows, keys = terms.shape
    pair = 2
    return pl.pallas_call(
        headsum_kernel,
        grid=(blocks // pair,),
        in_specs=[
            pl.BlockSpec((pair, heads, rows, keys), lambda i: (i, 0, 0, 0)),
            pl.BlockSpec((heads * rows, LANES), lambda i: (0, 0)),
            pl.BlockSpec(got.shape, lambda i: (0, 0, 0)),
        ],
        out_specs=pl.BlockSpec((pair, rows + 8, keys), lambda i: (i, 0, 0)),
        out_shape=jax.ShapeDtypeStruct((blocks, rows + 8, keys), jnp.float32),
        scratch_shapes=[
            pltpu.VMEM((heads, rows, LANES), jnp.float32),
            pltpu.VMEM((8, keys), jnp.float32),
            pltpu.VMEM((LANES, rows), jnp.float32),
        ],
        compiler_params=pltpu.CompilerParams(vmem_limit_bytes=40 << 20),
        name="head_sum",
    )(terms, tops, got)


def keys_kernel(key_total, got_ref, logits_ref, qh_ref, k_ref, w_ref, send_ref, keys_ref, wpad, slopes, acc, square):
    copies, _, keys = got_ref.shape
    heads, rows, depth = qh_ref.shape
    group = 8
    root = 1.0 / math.sqrt(depth)
    lane = lane_iota(rows)

    ltops = got_ref[:, rows : rows + 1, 0:rows]
    ltop = jnp.max(ltops, axis=0)
    lsum = jnp.sum(got_ref[:, rows + 1 : rows + 2, 0:rows] * jnp.exp(ltops - ltop[None]), axis=0)
    square[...] = jnp.zeros_like(square)
    square[0:1] = ltop
    square[1:2] = lsum
    columns = square[...].T
    target = got_ref[0, 0:rows]
    for g in range(1, copies):
        target = target + got_ref[g, 0:rows]
    soft = jnp.exp(logits_ref[...] - columns[:, 0:1]) / columns[:, 1:2]
    send_ref[0, 0:rows] = key_total * (soft - target)

    wpad[...] = jnp.zeros_like(wpad)
    wpad[:, 0:heads] = w_ref[...] * root
    keys_ref[...] = jnp.zeros_like(keys_ref)
    acc[...] = jnp.zeros_like(acc)

    def step(i, carry):
        weights = pltpu.roll(wpad[...], LANES - group * i, 1)
        chunk = qh_ref[pl.ds(i * group, group)].reshape(group * rows, depth)
        products = dot(chunk, k_ref[...], NT)
        dlogits = send_ref[0, 0:rows]
        sums = acc[...]
        for j in range(group):
            part = products[j * rows : (j + 1) * rows]
            active = jnp.sum(jnp.maximum(part, 0.0) * dlogits, axis=1, keepdims=True)
            sums = jnp.where(lane == i * group + j, active, sums)
            slope = jnp.where(part > 0.0, dlogits * weights[:, j : j + 1], 0.0)
            slopes[j * rows : (j + 1) * rows] = slope.astype(jnp.bfloat16)
        acc[...] = sums
        keys_ref[...] += dot(slopes[...], chunk, TN)
        return carry

    lax.fori_loop(0, heads // group, step, 0)
    flat = (acc[...] * root).T
    send_ref[0, rows : rows + heads // 2, 0:rows] = flat[0 : heads // 2]
    send_ref[0, rows : rows + heads // 2, rows : 2 * rows] = flat[heads // 2 : heads]
    for g in range(1, copies):
        send_ref[g] = send_ref[0]


def key_gradient(got, logits, qh, index_keys, index_weight, key_total):
    copies, _, keys = got.shape
    heads, rows, depth = qh.shape
    return pl.pallas_call(
        lambda *refs: keys_kernel(key_total, *refs),
        out_shape=(
            jax.ShapeDtypeStruct((copies, rows + heads // 2, keys), jnp.float32),
            jax.ShapeDtypeStruct((keys, depth), jnp.float32),
        ),
        scratch_shapes=[
            pltpu.VMEM((rows, LANES), jnp.float32),
            pltpu.VMEM((8 * rows, keys), jnp.bfloat16),
            pltpu.VMEM((rows, LANES), jnp.float32),
            pltpu.VMEM((LANES, rows), jnp.float32),
        ],
        compiler_params=pltpu.CompilerParams(vmem_limit_bytes=40 << 20),
        name="key_gradient",
    )(got, logits, qh, index_keys, index_weight)


def query_kernel(got_ref, k_ref, q_ref, w_ref, out_ref, slopes, acc, wsum):
    share, rows, depth = q_ref.shape
    step = pl.program_id(0)
    keys = k_ref.shape[1]
    extra = wsum.shape[0]
    pieces = out_ref.shape[0]
    root = 1.0 / math.sqrt(depth)

    @pl.when(step == 0)
    def _():
        acc[...] = jnp.zeros_like(acc)
        wsum[...] = jnp.zeros_like(wsum)

    block = k_ref[0].astype(jnp.bfloat16)
    products = dot(q_ref[...].reshape(share * rows, depth), block, NT)
    dlogits = got_ref[0, 0:rows]
    for j in range(share):
        part = products[j * rows : (j + 1) * rows]
        weight = w_ref[:, j : j + 1] * root
        slope = jnp.where(part > 0.0, dlogits * weight, 0.0)
        slopes[j * rows : (j + 1) * rows] = slope.astype(jnp.bfloat16)
    acc[...] += dot(slopes[...], block, NN)
    wsum[...] += got_ref[0, rows:]

    @pl.when(step == pl.num_programs(0) - 1)
    def _():
        span = rows // pieces
        few = extra // pieces
        for z in range(pieces):
            for j in range(share):
                first = j * rows + z * span
                out_ref[z, pl.ds(j, span, stride=share), :] = acc[first : first + span]
            piece = wsum[z * few : (z + 1) * few]
            out_ref[z, share * span : share * span + few] = piece[:, 0:rows]
            out_ref[z, share * span + few :] = piece[:, rows : 2 * rows]


def query_gradient(got, plane_keys, queries, weights, pieces):
    blocks, height, keys = got.shape
    share, rows, depth = queries.shape
    extra = height - rows
    tall = share * (rows // pieces) + 2 * (extra // pieces)
    return pl.pallas_call(
        query_kernel,
        grid=(blocks,),
        in_specs=[
            pl.BlockSpec((1, height, keys), lambda i: (i, 0, 0)),
            pl.BlockSpec((1, keys, depth), lambda i: (i, 0, 0)),
            pl.BlockSpec((share, rows, depth), lambda i: (0, 0, 0)),
            pl.BlockSpec((rows, share), lambda i: (0, 0)),
        ],
        out_specs=pl.BlockSpec((pieces, tall, depth), lambda i: (0, 0, 0)),
        out_shape=jax.ShapeDtypeStruct((pieces, tall, depth), jnp.float32),
        scratch_shapes=[
            pltpu.VMEM((share * rows, keys), jnp.bfloat16),
            pltpu.VMEM((share * rows, depth), jnp.float32),
            pltpu.VMEM((extra, keys), jnp.float32),
        ],
        compiler_params=pltpu.CompilerParams(vmem_limit_bytes=40 << 20),
        name="query_gradient",
    )(got, plane_keys, queries, weights)


def exchange(x, axis):
    return lax.all_to_all(x, axis, split_axis=0, concat_axis=0, tiled=True)


def shards(mla_query, mla_cache, index_query, index_keys, index_weight):
    key_count = lax.axis_size("key")
    head_count = lax.axis_size("head")
    rows = mla_query.shape[0]
    keys, depth = index_keys.shape
    heads = index_query.shape[1]
    share = heads // head_count
    head_index = lax.axis_index("head")
    row_index = lax.axis_index("row")

    plane_keys = lax.all_gather(index_keys.astype(jnp.float32), "head", axis=0)
    logits, lstats, qh = indexer_forward(index_query, index_keys, index_weight)
    terms, tops, send1 = attention_scores(mla_query, mla_cache, lstats, key_count)
    got1 = exchange(send1, "key")
    send2 = head_sum(terms, tops, got1)
    got2 = exchange(send2, "head")
    key_total = float(keys * head_count * key_count)
    send3, keys_part = key_gradient(got2, logits, qh, index_keys, index_weight, key_total)

    half = keys // 2
    away = lax.dynamic_slice_in_dim(keys_part, (1 - row_index) * half, half, 0)
    near = lax.dynamic_slice_in_dim(keys_part, row_index * half, half, 0)
    key_grad = near + lax.ppermute(away, "row", [(0, 1), (1, 0)])

    got3 = exchange(send3, "head")
    mine = lax.dynamic_slice_in_dim(qh, head_index * share, share, 0)
    my_weights = lax.dynamic_slice_in_dim(index_weight, head_index * share, share, 1)
    send4 = query_gradient(got3, plane_keys, mine, my_weights, key_count)
    got4 = jnp.sum(exchange(send4, "key"), axis=0)
    got5 = exchange(jnp.broadcast_to(got4[None], (key_count, *got4.shape)), "key")
    span = share * (rows // key_count)
    query_grad = got5[:, 0:span].reshape(rows, share, depth)
    few = (got4.shape[0] - span) // 2
    low = got5[:, span : span + few].reshape(heads // 2, rows)
    high = got5[:, span + few :].reshape(heads // 2, rows)
    weight_grad = jnp.concatenate([low, high], axis=0).T
    return (query_grad, key_grad, weight_grad)


def solution(mesh):
    placed = (
        P("row", "head", None),
        P(None, "key", None),
        P("row", None, None),
        P(("head", "key"), None),
        P("row", None),
    )
    return jax.shard_map(
        shards,
        mesh=mesh,
        in_specs=placed,
        out_specs=(P("row", "head", None), P(("head", "key", "row"), None), P("row", None)),
        check_vma=False,
    )
```

```python
import math

import jax
import jax.numpy as jnp
from jax import lax
from jax.experimental import pallas as pl
from jax.experimental.pallas import tpu as pltpu
from jax.sharding import PartitionSpec as P

MH = 128
LOG2E = 1.4426950408889634
SCORE2 = LOG2E / math.sqrt(192.0)
LANES = 128
NT = (((1,), (1,)), ((), ()))
TN = (((0,), (0,)), ((), ()))
NN = (((1,), (0,)), ((), ()))


def dot(a, b, dims):
    return lax.dot_general(a, b, dims, preferred_element_type=jnp.float32)


def lane_iota(rows):
    return lax.broadcasted_iota(jnp.int32, (rows, LANES), 1)


VMEM_BYTES = 60 << 20


def call(kernel, name, vmem=VMEM_BYTES, **options):
    return pl.pallas_call(
        kernel, name=name, compiler_params=pltpu.CompilerParams(vmem_limit_bytes=vmem), **options
    )


def forward_kernel(q_ref, k_ref, w_ref, logits_ref, stats_ref, qh_ref, qt_ref, wide):
    rows, heads, depth = q_ref.shape
    group = 8
    wide[...] = q_ref[...].astype(jnp.float32).reshape(rows * heads, depth)
    logits_ref[...] = jnp.zeros_like(logits_ref)

    def step(i, carry):
        total = logits_ref[...]
        weights = w_ref[pl.ds(i * group, group)]
        for j in range(group):
            head = i * group + j
            query = wide[pl.ds(head, rows, stride=heads), :]
            qh_ref[head] = query.astype(jnp.bfloat16)
            turned = query.T.astype(jnp.bfloat16)
            qt_ref[head] = turned
            products = dot(k_ref[...], turned, NN)
            total = total + jnp.maximum(products, 0.0) * weights[j : j + 1]
        logits_ref[...] = total
        return carry

    lax.fori_loop(0, heads // group, step, 0)
    logits = logits_ref[...] * (1.0 / math.sqrt(depth))
    logits_ref[...] = logits
    top = jnp.max(logits, axis=0, keepdims=True)
    total = jnp.sum(jnp.exp(logits - top), axis=0, keepdims=True)
    stats_ref[...] = jnp.zeros_like(stats_ref)
    stats_ref[0:1] = top
    stats_ref[1:2] = total


def indexer_forward(index_query, index_keys, weights):
    rows, heads, depth = index_query.shape
    keys = index_keys.shape[0]
    return call(
        forward_kernel,
        "indexer_forward",
        out_shape=(
            jax.ShapeDtypeStruct((keys, rows), jnp.float32),
            jax.ShapeDtypeStruct((8, rows), jnp.float32),
            jax.ShapeDtypeStruct((heads, rows, depth), jnp.bfloat16),
            jax.ShapeDtypeStruct((heads, depth, rows), jnp.bfloat16),
        ),
        scratch_shapes=[pltpu.VMEM((rows * heads, depth), jnp.float32)],
    )(index_query, index_keys, weights)


def scores_kernel(q_ref, c_ref, lstats_ref, e_ref, tops_ref, send_ref, qh, sums):
    heads, width, rows = q_ref.shape
    step = pl.program_id(0)
    steps = pl.num_programs(0)
    part = c_ref.shape[0]
    lane = lane_iota(2 * rows)

    @pl.when(step == 0)
    def _():
        for h in range(heads):
            qh[h * rows : (h + 1) * rows] = q_ref[h].T
        tops_ref[...] = jnp.zeros_like(tops_ref)
        sums[...] = jnp.zeros_like(sums)

    for h in range(0, heads, 2):
        span = slice(h * rows, (h + 2) * rows)
        queries = qh[span]
        blocks = [dot(queries, c_ref[j], NN) for j in range(part)]
        top = blocks[0]
        for block in blocks[1:]:
            top = jnp.maximum(top, block)
        top = jnp.max(top, axis=1, keepdims=True)
        total = None
        for j, block in enumerate(blocks):
            terms = jnp.exp2((block - top) * SCORE2)
            total = terms if total is None else total + terms
            e_ref[j, h : h + 2] = terms.astype(jnp.bfloat16).reshape(2, rows, terms.shape[1])
        total = jnp.sum(total, axis=1, keepdims=True)
        tops_ref[span] = jnp.where(lane == step, top, tops_ref[span])
        sums[span] = jnp.where(lane == step, total, sums[span])

    @pl.when(step == steps - 1)
    def _():
        lane1 = lane_iota(rows)
        used = lane1 < steps
        packed = jnp.zeros((rows, LANES), jnp.float32)
        for h in range(heads):
            tops = tops_ref[h * rows : (h + 1) * rows]
            top = jnp.max(jnp.where(used, tops, -jnp.inf), axis=1, keepdims=True)
            scaled = sums[h * rows : (h + 1) * rows] * jnp.exp2(jnp.where(used, tops - top, 0.0) * SCORE2)
            total = jnp.sum(jnp.where(used, scaled, 0.0), axis=1, keepdims=True)
            packed = jnp.where(lane1 == h, top, packed)
            packed = jnp.where(lane1 == heads + h, total, packed)
        flat = packed.T[0 : 2 * heads]
        for z in range(send_ref.shape[0]):
            send_ref[z, 0 : 2 * heads] = flat
            send_ref[z, 2 * heads :] = lstats_ref[...]


PART = 2


def attention_scores(queries, cache, lstats, key_count):
    heads, width, rows = queries.shape
    blocks, _, keys = cache.shape
    return call(
        scores_kernel,
        "attention_scores",
        grid=(blocks // PART,),
        in_specs=[
            pl.BlockSpec((heads, width, rows), lambda i: (0, 0, 0)),
            pl.BlockSpec((PART, width, keys), lambda i: (i, 0, 0)),
            pl.BlockSpec((8, rows), lambda i: (0, 0)),
        ],
        out_specs=(
            pl.BlockSpec((PART, heads, rows, keys), lambda i: (i, 0, 0, 0)),
            pl.BlockSpec((heads * rows, LANES), lambda i: (0, 0)),
            pl.BlockSpec((key_count, 2 * heads + 8, rows), lambda i: (0, 0, 0)),
        ),
        out_shape=(
            jax.ShapeDtypeStruct((blocks, heads, rows, keys), jnp.bfloat16),
            jax.ShapeDtypeStruct((heads * rows, LANES), jnp.float32),
            jax.ShapeDtypeStruct((key_count, 2 * heads + 8, rows), jnp.float32),
        ),
        scratch_shapes=[
            pltpu.VMEM((rows * heads, width), jnp.bfloat16),
            pltpu.VMEM((rows * heads, LANES), jnp.float32),
        ],
    )(queries, cache, lstats)


def headsum_kernel(e_ref, tops_ref, got_ref, out_ref, weights, tail, square):
    part, heads, rows, keys = e_ref.shape
    step = pl.program_id(0)
    lane = lane_iota(rows)

    @pl.when(step == 0)
    def _():
        tops = got_ref[:, 0:heads]
        top = jnp.max(tops, axis=0)
        total = jnp.sum(got_ref[:, heads : 2 * heads] * jnp.exp2((tops - top[None]) * SCORE2), axis=0)
        square[...] = jnp.zeros_like(square)
        square[0:heads] = top
        square[heads : 2 * heads] = (1.0 / MH) / total
        columns = square[...].T
        for h in range(heads):
            local = tops_ref[h * rows : (h + 1) * rows] - columns[:, h : h + 1]
            scale = columns[:, heads + h : heads + h + 1]
            weights[h] = jnp.exp2(jnp.minimum(local * SCORE2, 0.0)) * scale
        ltops = got_ref[:, 2 * heads : 2 * heads + 1]
        ltop = jnp.max(ltops, axis=0)
        lsum = jnp.sum(got_ref[:, 2 * heads + 1 : 2 * heads + 2] * jnp.exp(ltops - ltop[None]), axis=0)
        tail[...] = jnp.zeros_like(tail)
        tail[0:1, 0:rows] = ltop
        tail[1:2, 0:rows] = lsum

    columns = []
    for h in range(heads):
        columns.append(jnp.sum(jnp.where(lane == step, weights[h], 0.0), axis=1, keepdims=True))
    for j in range(part):
        total = e_ref[j, 0].astype(jnp.float32) * columns[0]
        for h in range(1, heads):
            total = total + e_ref[j, h].astype(jnp.float32) * columns[h]
        out_ref[j, 0:rows] = total
        out_ref[j, rows:] = tail[...]


def head_sum(terms, tops, got):
    blocks, heads, rows, keys = terms.shape
    return call(
        headsum_kernel,
        "head_sum",
        grid=(blocks // PART,),
        in_specs=[
            pl.BlockSpec((PART, heads, rows, keys), lambda i: (i, 0, 0, 0)),
            pl.BlockSpec((heads * rows, LANES), lambda i: (0, 0)),
            pl.BlockSpec(got.shape, lambda i: (0, 0, 0)),
        ],
        out_specs=pl.BlockSpec((PART, rows + 8, keys), lambda i: (i, 0, 0)),
        out_shape=jax.ShapeDtypeStruct((blocks, rows + 8, keys), jnp.float32),
        scratch_shapes=[
            pltpu.VMEM((heads, rows, LANES), jnp.float32),
            pltpu.VMEM((8, keys), jnp.float32),
            pltpu.VMEM((LANES, rows), jnp.float32),
        ],
    )(terms, tops, got)


def keys_kernel(key_total, got_ref, logits_ref, qh_ref, qt_ref, k_ref, w_ref, send_ref, keys_ref, slopes, turned):
    copies, _, keys = got_ref.shape
    heads, rows, depth = qh_ref.shape
    group = 8
    root = 1.0 / math.sqrt(depth)

    ltops = got_ref[:, rows : rows + 1, 0:rows]
    ltop = jnp.max(ltops, axis=0)
    lsum = jnp.sum(got_ref[:, rows + 1 : rows + 2, 0:rows] * jnp.exp(ltops - ltop[None]), axis=0)
    target = got_ref[0, 0:rows]
    for g in range(1, copies):
        target = target + got_ref[g, 0:rows]
    soft = jnp.exp(logits_ref[...] - ltop) * (1.0 / lsum)
    for k in range(0, keys, rows):
        turned[k : k + rows] = key_total * (soft[k : k + rows] - target[:, k : k + rows].T)
        send_ref[0:rows, k : k + rows] = turned[k : k + rows].T
    keys_ref[...] = jnp.zeros_like(keys_ref)

    def step(i, first, column):
        weights = w_ref[pl.ds(i * group, group)] * root
        sums = []
        for j in range(group):
            products = dot(k_ref[...], qt_ref[i * group + j], NN)
            dlogits = turned[...]
            sums.append(jnp.sum(jnp.maximum(products, 0.0) * dlogits, axis=0, keepdims=True) * root)
            slope = jnp.where(products > 0.0, dlogits * weights[j : j + 1], 0.0)
            slopes[:, j * rows : (j + 1) * rows] = slope.astype(jnp.bfloat16)
        place = pl.ds(pl.multiple_of(rows + first, group), group)
        send_ref[place, column : column + rows] = jnp.concatenate(sums, axis=0)
        chunk = qh_ref[pl.ds(i * group, group)].reshape(group * rows, depth)
        keys_ref[...] += dot(slopes[...], chunk, NN)

    half = heads // 2 // group

    def low(i, carry):
        step(i, i * group, 0)
        return carry

    def high(i, carry):
        step(i + half, i * group, rows)
        return carry

    lax.fori_loop(0, half, low, 0)
    lax.fori_loop(0, half, high, 0)


def key_gradient(got, logits, qh, qt, index_keys, weights, key_total):
    copies, _, keys = got.shape
    heads, rows, depth = qh.shape
    return call(
        lambda *refs: keys_kernel(key_total, *refs),
        "key_gradient",
        24 << 20,
        out_shape=(
            jax.ShapeDtypeStruct((rows + heads // 2, keys), jnp.float32),
            jax.ShapeDtypeStruct((keys, depth), jnp.float32),
        ),
        scratch_shapes=[
            pltpu.VMEM((keys, 8 * rows), jnp.bfloat16),
            pltpu.VMEM((keys, rows), jnp.float32),
        ],
    )(got, logits, qh, qt, index_keys, weights)


def query_kernel(place_ref, *refs):
    ring = RING
    got, kept = refs[0:ring], refs[ring : 2 * ring]
    qh_ref, w_ref = refs[2 * ring : 2 * ring + 2]
    outs = refs[2 * ring + 2 : 3 * ring + 2]
    slopes, acc, near, dlogits = refs[3 * ring + 2 :]
    heads, rows, depth = qh_ref.shape
    keys = kept[0].shape[0]
    pieces, tall, _ = outs[0].shape
    extra = got[0].shape[0] - rows
    share = (tall - 2 * extra // pieces) * pieces // rows
    root = 1.0 / math.sqrt(depth)
    x, y = place_ref[0], place_ref[1]
    span = rows // pieces
    few = extra // pieces

    wsum = got[0][rows:]
    for d in range(1, ring):
        wsum = wsum + got[d][rows:]
    for d in range(ring):
        near[d * keys : (d + 1) * keys] = kept[d][...].astype(jnp.bfloat16)
        dlogits[:, d * keys : (d + 1) * keys] = got[d][0:rows] * root
    columns = jnp.concatenate([w_ref[...], jnp.zeros((LANES - heads, rows), jnp.float32)], axis=0).T

    for d in range(ring):
        first = (lax.rem(x + d, ring) * ring + y) * share
        weights = pltpu.roll(columns, LANES - first, 1)
        queries = qh_ref[pl.ds(first, share)].reshape(share * rows, depth)
        for k in range(0, ring * keys, keys):
            products = dot(queries, near[k : k + keys], NT)
            for j in range(share):
                part = products[j * rows : (j + 1) * rows]
                slope = jnp.where(part > 0.0, dlogits[:, k : k + keys] * weights[:, j : j + 1], 0.0)
                slopes[j * rows : (j + 1) * rows, k : k + keys] = slope.astype(jnp.bfloat16)
        acc[...] = dot(slopes[...], near[...], NN)
        for z in range(pieces):
            for j in range(share):
                start = j * rows + z * span
                outs[d][z, pl.ds(j, span, stride=share), :] = acc[start : start + span]
            piece = wsum[z * few : (z + 1) * few]
            outs[d][z, share * span : share * span + few] = piece[:, 0:rows]
            outs[d][z, share * span + few :] = piece[:, rows : 2 * rows]


RING = 4


def query_gradient(place, got, kept, qh, weights, pieces):
    height, keys = got[0].shape
    heads, rows, depth = qh.shape
    share = heads // (RING * RING)
    extra = height - rows
    tall = share * (rows // pieces) + 2 * (extra // pieces)
    vmem = pl.BlockSpec(memory_space=pltpu.VMEM)
    return call(
        query_kernel,
        "query_gradient",
        24 << 20,
        in_specs=[pl.BlockSpec(memory_space=pltpu.SMEM)] + [vmem] * (2 * RING + 2),
        out_specs=[vmem] * RING,
        out_shape=[jax.ShapeDtypeStruct((pieces, tall, depth), jnp.float32)] * RING,
        scratch_shapes=[
            pltpu.VMEM((share * rows, RING * keys), jnp.bfloat16),
            pltpu.VMEM((share * rows, depth), jnp.float32),
            pltpu.VMEM((RING * keys, depth), jnp.bfloat16),
            pltpu.VMEM((rows, RING * keys), jnp.float32),
        ],
    )(place, *got, *kept, qh, weights)


def exchange(x, axis):
    return lax.all_to_all(x, axis, split_axis=0, concat_axis=0, tiled=True)


def shift_y(x, d):
    pairs = [(a * RING + b, a * RING + (b + d) % RING) for a in range(RING) for b in range(RING)]
    return lax.ppermute(x, "head", pairs)


def shift_x(x, d):
    pairs = [(a * RING + b, (a + d) % RING * RING + b) for a in range(RING) for b in range(RING)]
    return lax.ppermute(x, "head", pairs)


def shards(mla_query, mla_cache, index_query, index_keys, index_weight):
    key_count = lax.axis_size("key")
    head_count = lax.axis_size("head")
    rows = mla_query.shape[0]
    keys, depth = index_keys.shape
    heads = index_query.shape[1]
    share = heads // head_count
    head_index = lax.axis_index("head")
    row_index = lax.axis_index("row")
    place = jnp.stack([head_index // RING, head_index % RING]).astype(jnp.int32)

    wide_keys = index_keys.astype(jnp.float32)
    kept = [wide_keys] + [shift_y(wide_keys, d) for d in range(1, RING)]
    weights = index_weight.T
    logits, lstats, qh, qt = indexer_forward(index_query, index_keys, weights)
    queries = jnp.transpose(mla_query, (1, 2, 0))
    cache = jnp.swapaxes(mla_cache, 1, 2)
    terms, tops, send1 = attention_scores(queries, cache, lstats, key_count)
    got1, kept = lax.optimization_barrier((exchange(send1, "key"), kept))
    send2 = head_sum(terms, tops, got1)
    got2 = exchange(send2, "head")
    key_total = float(keys * head_count * key_count)
    send3, keys_part = key_gradient(got2, logits, qh, qt, index_keys, weights, key_total)
    got3 = [send3] + [shift_y(send3, d) for d in range(1, RING)]

    half = keys // 2
    away = lax.dynamic_slice_in_dim(keys_part, (1 - row_index) * half, half, 0)
    near = lax.dynamic_slice_in_dim(keys_part, row_index * half, half, 0)
    key_grad = near + lax.ppermute(away, "row", [(0, 1), (1, 0)])

    parts = query_gradient(place, got3, kept, qh, weights, key_count)
    send4 = parts[0]
    for d in range(1, RING):
        send4 = send4 + shift_x(parts[d], d)
    got4 = jnp.sum(exchange(send4, "key"), axis=0)
    got5 = exchange(jnp.broadcast_to(got4[None], (key_count, *got4.shape)), "key")
    span = share * (rows // key_count)
    query_grad = got5[:, 0:span].reshape(rows, share, depth)
    few = (got4.shape[0] - span) // 2
    low = got5[:, span : span + few].reshape(heads // 2, rows)
    high = got5[:, span + few :].reshape(heads // 2, rows)
    weight_grad = jnp.concatenate([low, high], axis=0).T
    return (query_grad, key_grad, weight_grad)


def solution(mesh):
    placed = (
        P("row", "head", None),
        P(None, "key", None),
        P("row", None, None),
        P(("head", "key"), None),
        P("row", None),
    )
    return jax.shard_map(
        shards,
        mesh=mesh,
        in_specs=placed,
        out_specs=(P("row", "head", None), P(("head", "key", "row"), None), P("row", None)),
        check_vma=False,
    )
```

```python
import math

import jax
import jax.numpy as jnp
from jax import lax
from jax.experimental import pallas as pl
from jax.experimental.pallas import tpu as pltpu
from jax.sharding import PartitionSpec as P

MH = 128
LOG2E = 1.4426950408889634
SCORE2 = LOG2E / math.sqrt(192.0)
LANES = 128
NT = (((1,), (1,)), ((), ()))
TN = (((0,), (0,)), ((), ()))
NN = (((1,), (0,)), ((), ()))


def dot(a, b, dims):
    return lax.dot_general(a, b, dims, preferred_element_type=jnp.float32)


def lane_iota(rows):
    return lax.broadcasted_iota(jnp.int32, (rows, LANES), 1)


RING = 4
PART = 2
VMEM = pl.BlockSpec(memory_space=pltpu.VMEM)
SMEM = pl.BlockSpec(memory_space=pltpu.SMEM)


def call(kernel, name, megabytes=32, **options):
    return pl.pallas_call(
        kernel, name=name, compiler_params=pltpu.CompilerParams(vmem_limit_bytes=megabytes << 20), **options
    )


def f32(*shape):
    return jax.ShapeDtypeStruct(shape, jnp.float32)


def bf16(*shape):
    return jax.ShapeDtypeStruct(shape, jnp.bfloat16)


def forward_kernel(q_ref, k_ref, w_ref, logits_ref, stats_ref, qh_ref, wide, total_ref):
    rows, heads, depth = q_ref.shape
    keys = k_ref.shape[0]
    group = 8
    wide[...] = q_ref[...].astype(jnp.float32).reshape(rows * heads, depth)
    columns = jnp.concatenate([w_ref[...], jnp.zeros((LANES - heads, rows), jnp.float32)], axis=0).T
    total_ref[...] = jnp.zeros_like(total_ref)

    def step(i, carry):
        weights = pltpu.roll(columns, LANES - group * i, 1)
        for j in range(group):
            head = i * group + j
            qh_ref[head] = wide[pl.ds(head, rows, stride=heads), :].astype(jnp.bfloat16)
        chunk = qh_ref[pl.ds(i * group, group)].reshape(group * rows, depth)
        products = dot(chunk, k_ref[...], NT)
        total = total_ref[...]
        for j in range(group):
            part = products[j * rows : (j + 1) * rows]
            total = total + jnp.maximum(part, 0.0) * weights[:, j : j + 1]
        total_ref[...] = total
        return carry

    lax.fori_loop(0, heads // group, step, 0)
    for k in range(0, keys, rows):
        logits_ref[k : k + rows] = total_ref[:, k : k + rows].T * (1.0 / math.sqrt(depth))
    logits = logits_ref[...]
    top = jnp.max(logits, axis=0, keepdims=True)
    total = jnp.sum(jnp.exp(logits - top), axis=0, keepdims=True)
    stats_ref[...] = jnp.zeros_like(stats_ref)
    stats_ref[0:1] = top
    stats_ref[1:2] = total


def indexer_forward(index_query, index_keys, weights):
    rows, heads, depth = index_query.shape
    keys = index_keys.shape[0]
    return call(
        forward_kernel,
        "indexer_forward",
        out_shape=(f32(keys, rows), f32(8, rows), bf16(heads, rows, depth)),
        scratch_shapes=[
            pltpu.VMEM((rows * heads, depth), jnp.float32),
            pltpu.VMEM((rows, keys), jnp.float32),
        ],
    )(index_query, index_keys, weights)


def scores_kernel(q_ref, c_ref, lstats_ref, e_ref, tops_ref, send_ref, qh, sums):
    heads, width, rows = q_ref.shape
    steps = c_ref.shape[0] // PART
    lane2 = lane_iota(2 * rows)
    for h in range(heads):
        qh[h * rows : (h + 1) * rows] = q_ref[h].T
    tops_ref[...] = jnp.zeros_like(tops_ref)
    sums[...] = jnp.zeros_like(sums)

    def body(step, carry):
        for h in range(0, heads, 2):
            span = slice(h * rows, (h + 2) * rows)
            queries = qh[span]
            blocks = [dot(queries, c_ref[step * PART + j], NN) for j in range(PART)]
            top = blocks[0]
            for block in blocks[1:]:
                top = jnp.maximum(top, block)
            top = jnp.max(top, axis=1, keepdims=True)
            total = None
            for j, block in enumerate(blocks):
                terms = jnp.exp2((block - top) * SCORE2)
                total = terms if total is None else total + terms
                e_ref[step * PART + j, h : h + 2] = terms.astype(jnp.bfloat16).reshape(2, rows, terms.shape[1])
            total = jnp.sum(total, axis=1, keepdims=True)
            tops_ref[span] = jnp.where(lane2 == step, top, tops_ref[span])
            sums[span] = jnp.where(lane2 == step, total, sums[span])
        return carry

    lax.fori_loop(0, steps, body, 0)
    lane = lane_iota(rows)
    used = lane < steps
    packed = jnp.zeros((rows, LANES), jnp.float32)
    for h in range(heads):
        tops = tops_ref[h * rows : (h + 1) * rows]
        top = jnp.max(jnp.where(used, tops, -jnp.inf), axis=1, keepdims=True)
        scaled = sums[h * rows : (h + 1) * rows] * jnp.exp2(jnp.where(used, tops - top, 0.0) * SCORE2)
        total = jnp.sum(jnp.where(used, scaled, 0.0), axis=1, keepdims=True)
        packed = jnp.where(lane == h, top, packed)
        packed = jnp.where(lane == heads + h, total, packed)
    flat = packed.T[0 : 2 * heads]
    for z in range(send_ref.shape[0]):
        send_ref[z, 0 : 2 * heads] = flat
        send_ref[z, 2 * heads :] = lstats_ref[...]


def attention_scores(queries, cache, lstats, key_count):
    heads, width, rows = queries.shape
    blocks, _, keys = cache.shape
    return call(
        scores_kernel,
        "attention_scores",
        in_specs=[VMEM] * 3,
        out_specs=[VMEM] * 3,
        out_shape=(
            bf16(blocks, heads, rows, keys),
            f32(heads * rows, LANES),
            f32(key_count, 2 * heads + 8, rows),
        ),
        scratch_shapes=[
            pltpu.VMEM((rows * heads, width), jnp.bfloat16),
            pltpu.VMEM((rows * heads, LANES), jnp.float32),
        ],
    )(queries, cache, lstats)


def headsum_kernel(place_ref, e_ref, tops_ref, got_ref, *refs):
    outs, weights, tail, square = refs[0:RING], *refs[RING:]
    _, heads, rows, keys = e_ref.shape
    lane = lane_iota(rows)
    near, near_stride, far_stride = place_ref[0], place_ref[2], place_ref[3]

    tops = got_ref[:, 0:heads]
    top = jnp.max(tops, axis=0)
    total = jnp.sum(got_ref[:, heads : 2 * heads] * jnp.exp2((tops - top[None]) * SCORE2), axis=0)
    square[...] = jnp.zeros_like(square)
    square[0:heads] = top
    square[heads : 2 * heads] = (1.0 / MH) / total
    columns = square[...].T
    for h in range(heads):
        local = tops_ref[h * rows : (h + 1) * rows] - columns[:, h : h + 1]
        scale = columns[:, heads + h : heads + h + 1]
        weights[h] = jnp.exp2(jnp.minimum(local * SCORE2, 0.0)) * scale
    ltops = got_ref[:, 2 * heads : 2 * heads + 1]
    ltop = jnp.max(ltops, axis=0)
    lsum = jnp.sum(got_ref[:, 2 * heads + 1 : 2 * heads + 2] * jnp.exp(ltops - ltop[None]), axis=0)
    tail[...] = jnp.zeros_like(tail)
    tail[0:1, 0:rows] = ltop
    tail[1:2, 0:rows] = lsum

    for d in range(RING):

        def body(k, carry):
            block = lax.rem(near + d, RING) * near_stride + k * far_stride
            step = block // PART
            total = None
            for h in range(heads):
                column = jnp.sum(jnp.where(lane == step, weights[h], 0.0), axis=1, keepdims=True)
                term = e_ref[block, h].astype(jnp.float32) * column
                total = term if total is None else total + term
            outs[d][k, 0:rows] = total
            outs[d][k, rows:] = tail[...]
            return carry

        lax.fori_loop(0, RING, body, 0)


def head_sum(place, terms, tops, got):
    blocks, heads, rows, keys = terms.shape
    return call(
        headsum_kernel,
        "head_sum",
        in_specs=[SMEM] + [VMEM] * 3,
        out_specs=[VMEM] * RING,
        out_shape=[f32(blocks // RING, rows + 8, keys)] * RING,
        scratch_shapes=[
            pltpu.VMEM((heads, rows, LANES), jnp.float32),
            pltpu.VMEM((8, keys), jnp.float32),
            pltpu.VMEM((LANES, rows), jnp.float32),
        ],
    )(place, terms, tops, got)


def merged_stats(tops, sums):
    top = tops[0]
    for other in tops[1:]:
        top = jnp.maximum(top, other)
    total = sums[0] * jnp.exp(tops[0] - top)
    for other, count in zip(tops[1:], sums[1:]):
        total = total + count * jnp.exp(other - top)
    return top, total


def partial_kernel(place_ref, *refs):
    got, outs = refs[0:RING], refs[RING:]
    rows = outs[0].shape[0] - 8
    top, total = merged_stats([r[0, rows : rows + 1] for r in got], [r[0, rows + 1 : rows + 2] for r in got])
    for d in range(RING):
        k = lax.rem(place_ref[1] + d, RING)
        outs[d][0:rows] = got[0][k, 0:rows] + got[1][k, 0:rows] + (got[2][k, 0:rows] + got[3][k, 0:rows])
        outs[d][rows:] = jnp.zeros_like(outs[d][rows:])
        outs[d][rows : rows + 1] = top
        outs[d][rows + 1 : rows + 2] = total


def partial_sum(place, got):
    _, height, keys = got[0].shape
    return call(
        partial_kernel,
        "partial_sum",
        in_specs=[SMEM] + [VMEM] * RING,
        out_specs=[VMEM] * RING,
        out_shape=[f32(height, keys)] * RING,
    )(place, *got)


def keys_kernel(key_total, *refs):
    got = refs[0:RING]
    logits_ref, qh_ref, k_ref, w_ref, send_ref, keys_ref, slopes, turned = refs[RING:]
    heads, rows, depth = qh_ref.shape
    keys = k_ref.shape[0]
    group = 8
    root = 1.0 / math.sqrt(depth)

    ltop, lsum = merged_stats(
        [r[rows : rows + 1, 0:rows] for r in got], [r[rows + 1 : rows + 2, 0:rows] for r in got]
    )
    target = got[0][0:rows] + got[1][0:rows] + (got[2][0:rows] + got[3][0:rows])
    soft = jnp.exp(logits_ref[...] - ltop) * (1.0 / lsum)
    for k in range(0, keys, rows):
        turned[k : k + rows] = key_total * (soft[k : k + rows] - target[:, k : k + rows].T)
        send_ref[0:rows, k : k + rows] = turned[k : k + rows].T
    keys_ref[...] = jnp.zeros_like(keys_ref)

    def step(i, first, column):
        weights = w_ref[pl.ds(i * group, group)] * root
        sums = []
        for j in range(group):
            products = dot(k_ref[...], qh_ref[i * group + j], NT)
            dlogits = turned[...]
            sums.append(jnp.sum(jnp.maximum(products, 0.0) * dlogits, axis=0, keepdims=True) * root)
            slope = jnp.where(products > 0.0, dlogits * weights[j : j + 1], 0.0)
            slopes[:, j * rows : (j + 1) * rows] = slope.astype(jnp.bfloat16)
        place = pl.ds(pl.multiple_of(rows + first, group), group)
        send_ref[place, column : column + rows] = jnp.concatenate(sums, axis=0)
        chunk = qh_ref[pl.ds(i * group, group)].reshape(group * rows, depth)
        keys_ref[...] += dot(slopes[...], chunk, NN)

    half = heads // 2 // group

    def low(i, carry):
        step(i, i * group, 0)
        return carry

    def high(i, carry):
        step(i + half, i * group, rows)
        return carry

    lax.fori_loop(0, half, low, 0)
    lax.fori_loop(0, half, high, 0)


def key_gradient(got, logits, qh, index_keys, weights, key_total):
    heads, rows, depth = qh.shape
    keys = index_keys.shape[0]
    return call(
        lambda *refs: keys_kernel(key_total, *refs),
        "key_gradient",
        24,
        out_shape=(f32(rows + heads // 2, keys), f32(keys, depth)),
        scratch_shapes=[
            pltpu.VMEM((keys, 8 * rows), jnp.bfloat16),
            pltpu.VMEM((keys, rows), jnp.float32),
        ],
    )(*got, logits, qh, index_keys, weights)


def query_kernel(place_ref, *refs):
    ring = RING
    got, kept = refs[0:ring], refs[ring : 2 * ring]
    qh_ref, w_ref = refs[2 * ring : 2 * ring + 2]
    outs = refs[2 * ring + 2 : 3 * ring + 2]
    slopes, acc, near, dlogits = refs[3 * ring + 2 :]
    heads, rows, depth = qh_ref.shape
    keys = kept[0].shape[0]
    pieces, tall, _ = outs[0].shape
    extra = got[0].shape[0] - rows
    share = (tall - 2 * extra // pieces) * pieces // rows
    root = 1.0 / math.sqrt(depth)
    near_at, far_at, near_stride, far_stride = [place_ref[i] for i in range(4)]
    span = rows // pieces
    few = extra // pieces

    wsum = got[0][rows:]
    for d in range(1, ring):
        wsum = wsum + got[d][rows:]
    for d in range(ring):
        near[d * keys : (d + 1) * keys] = kept[d][...].astype(jnp.bfloat16)
        dlogits[:, d * keys : (d + 1) * keys] = got[d][0:rows] * root
    columns = jnp.concatenate([w_ref[...], jnp.zeros((LANES - heads, rows), jnp.float32)], axis=0).T

    for d in range(ring):
        first = (lax.rem(far_at + d, ring) * far_stride + near_at * near_stride) * share
        weights = pltpu.roll(columns, LANES - first, 1)
        queries = qh_ref[pl.ds(first, share)].reshape(share * rows, depth)
        for k in range(0, ring * keys, keys):
            products = dot(queries, near[k : k + keys], NT)
            for j in range(share):
                part = products[j * rows : (j + 1) * rows]
                slope = jnp.where(part > 0.0, dlogits[:, k : k + keys] * weights[:, j : j + 1], 0.0)
                slopes[j * rows : (j + 1) * rows, k : k + keys] = slope.astype(jnp.bfloat16)
        acc[...] = dot(slopes[...], near[...], NN)
        for z in range(pieces):
            for j in range(share):
                start = j * rows + z * span
                outs[d][z, pl.ds(j, span, stride=share), :] = acc[start : start + span]
            piece = wsum[z * few : (z + 1) * few]
            outs[d][z, share * span : share * span + few] = piece[:, 0:rows]
            outs[d][z, share * span + few :] = piece[:, rows : 2 * rows]


def query_gradient(place, got, kept, qh, weights, pieces):
    height, keys = got[0].shape
    heads, rows, depth = qh.shape
    share = heads // (RING * RING)
    extra = height - rows
    tall = share * (rows // pieces) + 2 * (extra // pieces)
    vmem = pl.BlockSpec(memory_space=pltpu.VMEM)
    return call(
        query_kernel,
        "query_gradient",
        24,
        in_specs=[pl.BlockSpec(memory_space=pltpu.SMEM)] + [vmem] * (2 * RING + 2),
        out_specs=[vmem] * RING,
        out_shape=[jax.ShapeDtypeStruct((pieces, tall, depth), jnp.float32)] * RING,
        scratch_shapes=[
            pltpu.VMEM((share * rows, RING * keys), jnp.bfloat16),
            pltpu.VMEM((share * rows, depth), jnp.float32),
            pltpu.VMEM((RING * keys, depth), jnp.bfloat16),
            pltpu.VMEM((rows, RING * keys), jnp.float32),
        ],
    )(place, *got, *kept, qh, weights)


def exchange(x, axis):
    return lax.all_to_all(x, axis, split_axis=0, concat_axis=0, tiled=True)


def shift(x, d, across):
    pairs = []
    for a in range(RING):
        for b in range(RING):
            for row in range(2):
                if (row == 1) != across:
                    there = (a + d) % RING * RING + b
                else:
                    there = a * RING + (b + d) % RING
                pairs.append(((a * RING + b) * 2 + row, there * 2 + row))
    return lax.ppermute(x, ("head", "row"), pairs)


def shards(mla_query, mla_cache, index_query, index_keys, index_weight):
    key_count = lax.axis_size("key")
    head_count = lax.axis_size("head")
    rows = mla_query.shape[0]
    keys, depth = index_keys.shape
    heads = index_query.shape[1]
    share = heads // head_count
    head_index = lax.axis_index("head")
    row_index = lax.axis_index("row")
    x, y = head_index // RING, head_index % RING
    first = row_index == 0
    place = jnp.stack(
        [jnp.where(first, y, x), jnp.where(first, x, y), jnp.where(first, 1, RING), jnp.where(first, RING, 1)]
    ).astype(jnp.int32)

    weights = index_weight.T
    logits, lstats, qh = indexer_forward(index_query, index_keys, weights)
    queries = jnp.transpose(mla_query, (1, 2, 0))
    cache = jnp.swapaxes(mla_cache, 1, 2)
    terms, tops, send1 = attention_scores(queries, cache, lstats, key_count)
    got1 = exchange(send1, "key")
    send2 = head_sum(place, terms, tops, got1)
    got2 = [send2[0]] + [shift(send2[d], d, False) for d in (1, 3, 2)]
    wide_keys, got2[1] = lax.optimization_barrier((index_keys.astype(jnp.float32), got2[1]))
    kept = [wide_keys] + [shift(wide_keys, d, False) for d in range(1, RING)]
    send2 = partial_sum(place, got2)
    got2 = [send2[0]] + [shift(send2[d], d, True) for d in (1, 3, 2)]
    got2, kept = lax.optimization_barrier((got2, kept))
    key_total = float(keys * head_count * key_count)
    send3, keys_part = key_gradient(got2, logits, qh, index_keys, weights, key_total)
    got3 = [send3] + [shift(send3, d, False) for d in range(1, RING)]

    half = keys // 2
    away = lax.dynamic_slice_in_dim(keys_part, (1 - row_index) * half, half, 0)
    near = lax.dynamic_slice_in_dim(keys_part, row_index * half, half, 0)
    key_grad = near + lax.ppermute(away, "row", [(0, 1), (1, 0)])

    parts = query_gradient(place, got3, kept, qh, weights, key_count)
    send4 = parts[0]
    for d in range(1, RING):
        send4 = send4 + shift(parts[d], d, True)
    got4 = jnp.sum(exchange(send4, "key"), axis=0)
    got5 = exchange(jnp.broadcast_to(got4[None], (key_count, *got4.shape)), "key")
    span = share * (rows // key_count)
    query_grad = got5[:, 0:span].reshape(rows, share, depth)
    few = (got4.shape[0] - span) // 2
    low = got5[:, span : span + few].reshape(heads // 2, rows)
    high = got5[:, span + few :].reshape(heads // 2, rows)
    weight_grad = jnp.concatenate([low, high], axis=0).T
    return (query_grad, key_grad, weight_grad)


def solution(mesh):
    placed = (
        P("row", "head", None),
        P(None, "key", None),
        P("row", None, None),
        P(("head", "key"), None),
        P("row", None),
    )
    return jax.shard_map(
        shards,
        mesh=mesh,
        in_specs=placed,
        out_specs=(P("row", "head", None), P(("head", "key", "row"), None), P("row", None)),
        check_vma=False,
    )
```

```python
import functools
import math

import jax
import jax.numpy as jnp
from jax import lax
from jax.experimental import pallas as pl
from jax.experimental.pallas import tpu as pltpu
from jax.sharding import PartitionSpec as P

MH = 128
LOG2E = 1.4426950408889634
SCORE2 = LOG2E / math.sqrt(192.0)
LANES = 128
NT = (((1,), (1,)), ((), ()))
TN = (((0,), (0,)), ((), ()))
NN = (((1,), (0,)), ((), ()))


def dot(a, b, dims):
    return lax.dot_general(a, b, dims, preferred_element_type=jnp.float32)


def lane_iota(rows):
    return lax.broadcasted_iota(jnp.int32, (rows, LANES), 1)


RING = 4
PART = 2
VMEM = pl.BlockSpec(memory_space=pltpu.VMEM)
SMEM = pl.BlockSpec(memory_space=pltpu.SMEM)
HBM = pl.BlockSpec(memory_space=pltpu.HBM)


def call(kernel, name, megabytes=32, **options):
    return pl.pallas_call(
        kernel, name=name, compiler_params=pltpu.CompilerParams(vmem_limit_bytes=megabytes << 20), **options
    )


def f32(*shape):
    return jax.ShapeDtypeStruct(shape, jnp.float32)


def bf16(*shape):
    return jax.ShapeDtypeStruct(shape, jnp.bfloat16)


def scores_kernel(
    q_hbm, c_hbm, iq_hbm, k_hbm, w_hbm,
    e_hbm, tops_ref, send_ref, logits_ref, qh_ref,
    e_ref, q_ref, c_ref, iq_ref, k_ref, w_ref, wide, total_ref, queries_ref, sums, sems, out_sems,
):
    heads, width, rows = q_ref.shape
    blocks = c_ref.shape[0]
    steps = blocks // PART
    _, iheads, depth = iq_ref.shape
    keys = k_ref.shape[0]
    group = iheads // steps

    first = pltpu.make_async_copy(q_hbm, q_ref, sems.at[steps])
    first.start()

    def part_copy(step):
        span = pl.ds(step * PART, PART)
        return pltpu.make_async_copy(c_hbm.at[span], c_ref.at[span], sems.at[step])

    def terms_copy(step):
        span = pl.ds(step * PART, PART)
        return pltpu.make_async_copy(e_ref.at[span], e_hbm.at[span], out_sems.at[step])

    for step in range(2):
        part_copy(step).start()
    others = [(iq_hbm, iq_ref), (k_hbm, k_ref), (w_hbm, w_ref)]
    others = [pltpu.make_async_copy(src, dst, sems.at[steps + 1 + i]) for i, (src, dst) in enumerate(others)]
    for copy in others:
        copy.start()
    for step in range(2, steps):
        part_copy(step).start()

    tops_ref[...] = jnp.zeros_like(tops_ref)
    sums[...] = jnp.zeros_like(sums)
    total_ref[...] = jnp.zeros_like(total_ref)
    first.wait()
    for h in range(heads):
        queries_ref[h * rows : (h + 1) * rows] = q_ref[h].T
    for copy in others:
        copy.wait()
    wide[...] = iq_ref[...].astype(jnp.float32).reshape(rows * iheads, depth)
    columns = jnp.concatenate([w_ref[...], jnp.zeros((LANES - iheads, rows), jnp.float32)], axis=0).T
    lane2 = lane_iota(2 * rows)

    def body(step, carry):
        part_copy(step).wait()
        weights = pltpu.roll(columns, LANES - group * step, 1)
        for j in range(group):
            head = step * group + j
            qh_ref[head] = wide[pl.ds(head, rows, stride=iheads), :].astype(jnp.bfloat16)
        chunk = qh_ref[pl.ds(step * group, group)].reshape(group * rows, depth)
        products = dot(chunk, k_ref[...], NT)
        total = total_ref[...]
        for j in range(group):
            part = products[j * rows : (j + 1) * rows]
            total = total + jnp.maximum(part, 0.0) * weights[:, j : j + 1]
        total_ref[...] = total

        for h in range(0, heads, 2):
            span = slice(h * rows, (h + 2) * rows)
            queries = queries_ref[span]
            scores = [dot(queries, c_ref[step * PART + j], NN) for j in range(PART)]
            top = scores[0]
            for score in scores[1:]:
                top = jnp.maximum(top, score)
            top = jnp.max(top, axis=1, keepdims=True)
            total = None
            for j, score in enumerate(scores):
                terms = jnp.exp2((score - top) * SCORE2)
                total = terms if total is None else total + terms
                e_ref[step * PART + j, h : h + 2] = terms.astype(jnp.bfloat16).reshape(2, rows, keys)
            total = jnp.sum(total, axis=1, keepdims=True)
            tops_ref[span] = jnp.where(lane2 == step, top, tops_ref[span])
            sums[span] = jnp.where(lane2 == step, total, sums[span])
        terms_copy(step).start()
        return carry

    lax.fori_loop(0, steps, body, 0)
    lane = lane_iota(rows)
    used = lane < steps
    packed = jnp.zeros((rows, LANES), jnp.float32)
    for h in range(heads):
        tops = tops_ref[h * rows : (h + 1) * rows]
        top = jnp.max(jnp.where(used, tops, -jnp.inf), axis=1, keepdims=True)
        scaled = sums[h * rows : (h + 1) * rows] * jnp.exp2(jnp.where(used, tops - top, 0.0) * SCORE2)
        total = jnp.sum(jnp.where(used, scaled, 0.0), axis=1, keepdims=True)
        packed = jnp.where(lane == h, top, packed)
        packed = jnp.where(lane == heads + h, total, packed)
    flat = packed.T[0 : 2 * heads]
    for k in range(0, keys, rows):
        logits_ref[k : k + rows] = total_ref[:, k : k + rows].T * (1.0 / math.sqrt(depth))
    logits = logits_ref[...]
    ltop = jnp.max(logits, axis=0, keepdims=True)
    lsum = jnp.sum(jnp.exp(logits - ltop), axis=0, keepdims=True)
    for z in range(send_ref.shape[0]):
        send_ref[z, 0 : 2 * heads] = flat
        send_ref[z, 2 * heads :] = jnp.zeros((8, rows), jnp.float32)
        send_ref[z, 2 * heads : 2 * heads + 1] = ltop
        send_ref[z, 2 * heads + 1 : 2 * heads + 2] = lsum
    for step in range(steps):
        terms_copy(step).wait()


def scores_and_logits(queries, cache, index_query, index_keys, weights, key_count):
    heads, width, rows = queries.shape
    blocks, _, keys = cache.shape
    _, iheads, depth = index_query.shape
    steps = blocks // PART
    return call(
        scores_kernel,
        "scores_and_logits",
        60,
        in_specs=[HBM] * 5,
        out_specs=[HBM] + [VMEM] * 4,
        out_shape=(
            bf16(blocks, heads, rows, keys),
            f32(heads * rows, LANES),
            f32(key_count, 2 * heads + 8, rows),
            f32(keys, rows),
            bf16(iheads, rows, depth),
        ),
        scratch_shapes=[
            pltpu.VMEM((blocks, heads, rows, keys), jnp.bfloat16),
            pltpu.VMEM(queries.shape, jnp.bfloat16),
            pltpu.VMEM(cache.shape, jnp.bfloat16),
            pltpu.VMEM(index_query.shape, jnp.bfloat16),
            pltpu.VMEM(index_keys.shape, jnp.bfloat16),
            pltpu.VMEM(weights.shape, jnp.float32),
            pltpu.VMEM((rows * iheads, depth), jnp.float32),
            pltpu.VMEM((rows, keys), jnp.float32),
            pltpu.VMEM((rows * heads, width), jnp.bfloat16),
            pltpu.VMEM((rows * heads, LANES), jnp.float32),
            pltpu.SemaphoreType.DMA((steps + 4,)),
            pltpu.SemaphoreType.DMA((steps,)),
        ],
    )(queries, cache, index_query, index_keys, weights)


def headsum_kernel(offsets, place_ref, e_hbm, tops_ref, got_ref, *refs):
    outs, e_ref, weights, tail, square, sems = refs[0 : len(offsets)], *refs[len(offsets) :]
    _, heads, rows, keys = e_ref.shape
    lane = lane_iota(rows)
    near, near_stride, far_stride = place_ref[0], place_ref[2], place_ref[3]

    def block_of(d, k):
        return lax.rem(near + d, RING) * near_stride + k * far_stride

    def block_copy(i, d, k):
        slot = i * RING + k
        return pltpu.make_async_copy(e_hbm.at[block_of(d, k)], e_ref.at[slot], sems.at[slot])

    for i, d in enumerate(offsets):
        for k in range(RING):
            block_copy(i, d, k).start()

    tops = got_ref[:, 0:heads]
    top = jnp.max(tops, axis=0)
    total = jnp.sum(got_ref[:, heads : 2 * heads] * jnp.exp2((tops - top[None]) * SCORE2), axis=0)
    square[...] = jnp.zeros_like(square)
    square[0:heads] = top
    square[heads : 2 * heads] = (1.0 / MH) / total
    columns = square[...].T
    for h in range(heads):
        local = tops_ref[h * rows : (h + 1) * rows] - columns[:, h : h + 1]
        scale = columns[:, heads + h : heads + h + 1]
        weights[h] = jnp.exp2(jnp.minimum(local * SCORE2, 0.0)) * scale
    ltops = got_ref[:, 2 * heads : 2 * heads + 1]
    ltop = jnp.max(ltops, axis=0)
    lsum = jnp.sum(got_ref[:, 2 * heads + 1 : 2 * heads + 2] * jnp.exp(ltops - ltop[None]), axis=0)
    tail[...] = jnp.zeros_like(tail)
    tail[0:1, 0:rows] = ltop
    tail[1:2, 0:rows] = lsum

    for i, d in enumerate(offsets):

        def body(k, carry):
            step = block_of(d, k) // PART
            block_copy(i, d, k).wait()
            total = None
            for h in range(heads):
                column = jnp.sum(jnp.where(lane == step, weights[h], 0.0), axis=1, keepdims=True)
                term = e_ref[i * RING + k, h].astype(jnp.float32) * column
                total = term if total is None else total + term
            outs[i][k, 0:rows] = total
            outs[i][k, rows:] = tail[...]
            return carry

        lax.fori_loop(0, RING, body, 0)


def head_sum(offsets, place, terms, tops, got):
    blocks, heads, rows, keys = terms.shape
    slots = len(offsets) * RING
    return call(
        functools.partial(headsum_kernel, offsets),
        "head_sum",
        56,
        in_specs=[SMEM, HBM] + [VMEM] * 2,
        out_specs=[VMEM] * len(offsets),
        out_shape=[f32(blocks // RING, rows + 8, keys)] * len(offsets),
        scratch_shapes=[
            pltpu.VMEM((slots, heads, rows, keys), jnp.bfloat16),
            pltpu.VMEM((heads, rows, LANES), jnp.float32),
            pltpu.VMEM((8, keys), jnp.float32),
            pltpu.VMEM((LANES, rows), jnp.float32),
            pltpu.SemaphoreType.DMA((slots,)),
        ],
    )(place, terms, tops, got)


def merged_stats(tops, sums):
    top = tops[0]
    for other in tops[1:]:
        top = jnp.maximum(top, other)
    total = sums[0] * jnp.exp(tops[0] - top)
    for other, count in zip(tops[1:], sums[1:]):
        total = total + count * jnp.exp(other - top)
    return top, total


def partial_kernel(place_ref, *refs):
    got, outs = refs[0:RING], refs[RING:]
    rows = outs[0].shape[0] - 8
    top, total = merged_stats([r[0, rows : rows + 1] for r in got], [r[0, rows + 1 : rows + 2] for r in got])
    for d in range(RING):
        k = lax.rem(place_ref[1] + d, RING)
        outs[d][0:rows] = got[0][k, 0:rows] + got[1][k, 0:rows] + (got[2][k, 0:rows] + got[3][k, 0:rows])
        outs[d][rows:] = jnp.zeros_like(outs[d][rows:])
        outs[d][rows : rows + 1] = top
        outs[d][rows + 1 : rows + 2] = total


def partial_sum(place, got):
    _, height, keys = got[0].shape
    return call(
        partial_kernel,
        "partial_sum",
        in_specs=[SMEM] + [VMEM] * RING,
        out_specs=[VMEM] * RING,
        out_shape=[f32(height, keys)] * RING,
    )(place, *got)


GROUP = 8


def dlogits_kernel(key_total, *refs):
    got = refs[0:RING]
    logits_ref, qh_ref, k_ref, send_ref, turned = refs[RING:]
    heads, rows, depth = qh_ref.shape
    keys = k_ref.shape[0]
    root = 1.0 / math.sqrt(depth)

    ltop, lsum = merged_stats(
        [r[rows : rows + 1, 0:rows] for r in got], [r[rows + 1 : rows + 2, 0:rows] for r in got]
    )
    target = got[0][0:rows] + got[1][0:rows] + (got[2][0:rows] + got[3][0:rows])
    soft = jnp.exp(logits_ref[...] - ltop) * (1.0 / lsum)
    for k in range(0, keys, rows):
        turned[k : k + rows] = key_total * (soft[k : k + rows] - target[:, k : k + rows].T)
        send_ref[0:rows, k : k + rows] = turned[k : k + rows].T

    def step(i, first, column):
        sums = []
        for j in range(GROUP):
            products = dot(k_ref[...], qh_ref[i * GROUP + j], NT)
            sums.append(jnp.sum(jnp.maximum(products, 0.0) * turned[...], axis=0, keepdims=True) * root)
        place = pl.ds(pl.multiple_of(rows + first, GROUP), GROUP)
        send_ref[place, column : column + rows] = jnp.concatenate(sums, axis=0)

    half = heads // 2 // GROUP

    def low(i, carry):
        step(i, i * GROUP, 0)
        return carry

    def high(i, carry):
        step(i + half, i * GROUP, rows)
        return carry

    lax.fori_loop(0, half, low, 0)
    lax.fori_loop(0, half, high, 0)


def dlogits_of(got, logits, qh, index_keys, key_total):
    heads, rows, depth = qh.shape
    keys = index_keys.shape[0]
    return call(
        functools.partial(dlogits_kernel, key_total),
        "dlogits",
        24,
        out_shape=(f32(rows + heads // 2, keys), f32(keys, rows)),
    )(*got, logits, qh, index_keys)


def keys_kernel(turned_ref, qh_ref, k_ref, w_ref, keys_ref, slopes):
    heads, rows, depth = qh_ref.shape
    root = 1.0 / math.sqrt(depth)
    keys_ref[...] = jnp.zeros_like(keys_ref)

    def step(i, carry):
        weights = w_ref[pl.ds(i * GROUP, GROUP)] * root
        for j in range(GROUP):
            products = dot(k_ref[...], qh_ref[i * GROUP + j], NT)
            slope = jnp.where(products > 0.0, turned_ref[...] * weights[j : j + 1], 0.0)
            slopes[:, j * rows : (j + 1) * rows] = slope.astype(jnp.bfloat16)
        chunk = qh_ref[pl.ds(i * GROUP, GROUP)].reshape(GROUP * rows, depth)
        keys_ref[...] += dot(slopes[...], chunk, NN)
        return carry

    lax.fori_loop(0, heads // GROUP, step, 0)


def key_gradient(turned, qh, index_keys, weights):
    heads, rows, depth = qh.shape
    keys = index_keys.shape[0]
    return call(
        keys_kernel,
        "key_gradient",
        24,
        out_shape=f32(keys, depth),
        scratch_shapes=[pltpu.VMEM((keys, GROUP * rows), jnp.bfloat16)],
    )(turned, qh, index_keys, weights)


def query_kernel(offsets, place_ref, *refs):
    ring, count = RING, len(offsets)
    got, kept = refs[0:ring], refs[ring : 2 * ring]
    qh_ref, w_ref = refs[2 * ring : 2 * ring + 2]
    outs = refs[2 * ring + 2 : 2 * ring + 2 + count]
    slopes, acc, near, dlogits = refs[2 * ring + 2 + count :]
    heads, rows, depth = qh_ref.shape
    keys = kept[0].shape[0]
    pieces, tall, _ = outs[0].shape
    extra = got[0].shape[0] - rows
    share = (tall - 2 * extra // pieces) * pieces // rows
    root = 1.0 / math.sqrt(depth)
    near_at, far_at, near_stride, far_stride = [place_ref[i] for i in range(4)]
    span = rows // pieces
    few = extra // pieces

    wsum = got[0][rows:]
    for d in range(1, ring):
        wsum = wsum + got[d][rows:]
    for d in range(ring):
        near[d * keys : (d + 1) * keys] = kept[d][...].astype(jnp.bfloat16)
        dlogits[:, d * keys : (d + 1) * keys] = got[d][0:rows] * root
    columns = jnp.concatenate([w_ref[...], jnp.zeros((LANES - heads, rows), jnp.float32)], axis=0).T

    for i, d in enumerate(offsets):
        first = (lax.rem(far_at + d, ring) * far_stride + near_at * near_stride) * share
        weights = pltpu.roll(columns, LANES - first, 1)
        queries = qh_ref[pl.ds(first, share)].reshape(share * rows, depth)
        for k in range(0, ring * keys, keys):
            products = dot(queries, near[k : k + keys], NT)
            for j in range(share):
                part = products[j * rows : (j + 1) * rows]
                slope = jnp.where(part > 0.0, dlogits[:, k : k + keys] * weights[:, j : j + 1], 0.0)
                slopes[j * rows : (j + 1) * rows, k : k + keys] = slope.astype(jnp.bfloat16)
        acc[...] = dot(slopes[...], near[...], NN)
        for z in range(pieces):
            for j in range(share):
                start = j * rows + z * span
                outs[i][z, pl.ds(j, span, stride=share), :] = acc[start : start + span]
            piece = wsum[z * few : (z + 1) * few]
            outs[i][z, share * span : share * span + few] = piece[:, 0:rows]
            outs[i][z, share * span + few :] = piece[:, rows : 2 * rows]


def query_gradient(offsets, place, got, kept, qh, weights, pieces):
    height, keys = got[0].shape
    heads, rows, depth = qh.shape
    share = heads // (RING * RING)
    extra = height - rows
    tall = share * (rows // pieces) + 2 * (extra // pieces)
    return call(
        functools.partial(query_kernel, offsets),
        "query_gradient",
        24,
        in_specs=[SMEM] + [VMEM] * (2 * RING + 2),
        out_specs=[VMEM] * len(offsets),
        out_shape=[f32(pieces, tall, depth)] * len(offsets),
        scratch_shapes=[
            pltpu.VMEM((share * rows, RING * keys), jnp.bfloat16),
            pltpu.VMEM((share * rows, depth), jnp.float32),
            pltpu.VMEM((RING * keys, depth), jnp.bfloat16),
            pltpu.VMEM((rows, RING * keys), jnp.float32),
        ],
    )(place, *got, *kept, qh, weights)


def exchange(x, axis):
    return lax.all_to_all(x, axis, split_axis=0, concat_axis=0, tiled=True)


def shift(x, d, across):
    pairs = []
    for a in range(RING):
        for b in range(RING):
            for row in range(2):
                if (row == 1) != across:
                    there = (a + d) % RING * RING + b
                else:
                    there = a * RING + (b + d) % RING
                pairs.append(((a * RING + b) * 2 + row, there * 2 + row))
    return lax.ppermute(x, ("head", "row"), pairs)


def shards(mla_query, mla_cache, index_query, index_keys, index_weight):
    key_count = lax.axis_size("key")
    head_count = lax.axis_size("head")
    rows = mla_query.shape[0]
    keys, depth = index_keys.shape
    heads = index_query.shape[1]
    share = heads // head_count
    head_index = lax.axis_index("head")
    row_index = lax.axis_index("row")
    x, y = head_index // RING, head_index % RING
    first = row_index == 0
    place = jnp.stack(
        [jnp.where(first, y, x), jnp.where(first, x, y), jnp.where(first, 1, RING), jnp.where(first, RING, 1)]
    ).astype(jnp.int32)

    weights = index_weight.T
    queries = jnp.transpose(mla_query, (1, 2, 0))
    cache = jnp.swapaxes(mla_cache, 1, 2)
    terms, tops, send1, logits, qh = scores_and_logits(queries, cache, index_query, index_keys, weights, key_count)
    send1, place = lax.optimization_barrier((send1, place))
    got1 = exchange(send1, "key")
    wide_keys = index_keys.astype(jnp.float32)
    (opposite,) = head_sum((2,), place, terms, tops, got1)
    others = head_sum((1, 3, 0), place, terms, tops, got1)
    got2 = [others[2], shift(others[0], 1, False), shift(opposite, 2, False), shift(others[1], 3, False)]
    wide_keys, _ = lax.optimization_barrier((wide_keys, others[0]))
    kept = [wide_keys] + [shift(wide_keys, d, False) for d in range(1, RING)]
    got2, kept = lax.optimization_barrier((got2, kept))
    send2 = partial_sum(place, got2)
    got2 = [send2[0]] + [shift(send2[d], d, True) for d in (1, 2, 3)]
    key_total = float(keys * head_count * key_count)
    send3, turned = dlogits_of(got2, logits, qh, index_keys, key_total)
    got3 = [send3] + [shift(send3, d, False) for d in range(1, RING)]
    keys_part = key_gradient(turned, qh, index_keys, weights)
    got3, keys_part = lax.optimization_barrier((got3, keys_part))

    half = keys // 2
    away = lax.dynamic_slice_in_dim(keys_part, (1 - row_index) * half, half, 0)
    near = lax.dynamic_slice_in_dim(keys_part, row_index * half, half, 0)
    key_grad = near + lax.ppermute(away, "row", [(0, 1), (1, 0)])

    (opposite,) = query_gradient((2,), place, got3, kept, qh, weights, key_count)
    opposite, got3 = lax.optimization_barrier((opposite, got3))
    others = query_gradient((1, 3, 0), place, got3, kept, qh, weights, key_count)
    opposite, one, three = shift(opposite, 2, True), shift(others[0], 1, True), shift(others[1], 3, True)
    send4 = others[2] + one + (opposite + three)
    got4 = jnp.sum(exchange(send4, "key"), axis=0)
    got5 = exchange(jnp.broadcast_to(got4[None], (key_count, *got4.shape)), "key")
    span = share * (rows // key_count)
    query_grad = got5[:, 0:span].reshape(rows, share, depth)
    few = (got4.shape[0] - span) // 2
    low = got5[:, span : span + few].reshape(heads // 2, rows)
    high = got5[:, span + few :].reshape(heads // 2, rows)
    weight_grad = jnp.concatenate([low, high], axis=0).T
    return (query_grad, key_grad, weight_grad)


def solution(mesh):
    placed = (
        P("row", "head", None),
        P(None, "key", None),
        P("row", None, None),
        P(("head", "key"), None),
        P("row", None),
    )
    return jax.shard_map(
        shards,
        mesh=mesh,
        in_specs=placed,
        out_specs=(P("row", "head", None), P(("head", "key", "row"), None), P("row", None)),
        check_vma=False,
    )
```

```python
import functools
import math

import jax
import jax.numpy as jnp
from jax import lax
from jax.experimental import pallas as pl
from jax.experimental.pallas import tpu as pltpu
from jax.sharding import PartitionSpec as P

MH = 128
LOG2E = 1.4426950408889634
SCORE2 = LOG2E / math.sqrt(192.0)
LANES = 128
NT = (((1,), (1,)), ((), ()))
TN = (((0,), (0,)), ((), ()))
NN = (((1,), (0,)), ((), ()))


def dot(a, b, dims):
    return lax.dot_general(a, b, dims, preferred_element_type=jnp.float32)


def lane_iota(rows):
    return lax.broadcasted_iota(jnp.int32, (rows, LANES), 1)


RING = 4
PART = 2
BESIDE = 4_000_000_000
VMEM = pl.BlockSpec(memory_space=pltpu.VMEM)
HBM = pl.BlockSpec(memory_space=pltpu.HBM)


def call(kernel, name, megabytes=32, flops=0, moved=0, **options):
    cost = pl.CostEstimate(flops=flops, bytes_accessed=moved, transcendentals=0) if flops else None
    return pl.pallas_call(
        kernel,
        name=name,
        compiler_params=pltpu.CompilerParams(vmem_limit_bytes=megabytes << 20),
        cost_estimate=cost,
        **options,
    )


def f32(*shape):
    return jax.ShapeDtypeStruct(shape, jnp.float32)


def bf16(*shape):
    return jax.ShapeDtypeStruct(shape, jnp.bfloat16)


def position():
    head, first = lax.axis_index("head"), lax.axis_index("row") == 0
    x, y = lax.div(head, RING), lax.rem(head, RING)
    return jnp.where(first, y, x), jnp.where(first, x, y), jnp.where(first, 1, RING), jnp.where(first, RING, 1)


def scores_kernel(
    q_hbm, c_hbm, iq_hbm, k_hbm, w_hbm,
    e_hbm, tops_ref, send_ref, logits_ref, qh_ref,
    e_ref, q_ref, c_ref, iq_ref, k_ref, w_ref, wide, total_ref, queries_ref, tops, sums, sems, out_sems,
):
    heads, width, rows = q_ref.shape
    blocks = c_ref.shape[0]
    steps = blocks // PART
    _, iheads, depth = iq_ref.shape
    keys = k_ref.shape[0]
    group = iheads // steps

    first = pltpu.make_async_copy(q_hbm, q_ref, sems.at[steps])
    first.start()

    def part_copy(step):
        span = pl.ds(step * PART, PART)
        return pltpu.make_async_copy(c_hbm.at[span], c_ref.at[span], sems.at[step])

    def terms_copy(step):
        span = pl.ds(step * PART, PART)
        return pltpu.make_async_copy(e_ref.at[span], e_hbm.at[span], out_sems.at[step])

    others = [(iq_hbm, iq_ref), (k_hbm, k_ref), (w_hbm, w_ref)]
    others = [pltpu.make_async_copy(src, dst, sems.at[steps + 1 + i]) for i, (src, dst) in enumerate(others)]
    for step in range(steps):
        part_copy(step).start()
    for copy in others:
        copy.start()

    tops[...] = jnp.zeros_like(tops)
    sums[...] = jnp.zeros_like(sums)
    first.wait()
    for h in range(heads):
        queries_ref[h * rows : (h + 1) * rows] = q_ref[h].T
    lane = lane_iota(rows)

    def score_step(step, carry):
        part_copy(step).wait()
        for h in range(0, heads, 2):
            queries = queries_ref[h * rows : (h + 2) * rows]
            scores = [dot(queries, c_ref[step * PART + j], NN) for j in range(PART)]
            top = scores[0]
            for score in scores[1:]:
                top = jnp.maximum(top, score)
            top = jnp.max(top, axis=1, keepdims=True)
            total = None
            for j, score in enumerate(scores):
                terms = jnp.exp2((score - top) * SCORE2)
                total = terms if total is None else total + terms
                e_ref[step * PART + j, h : h + 2] = terms.astype(jnp.bfloat16).reshape(2, rows, keys)
            total = jnp.sum(total, axis=1, keepdims=True)
            low, high = lane == h * steps + step, lane == (h + 1) * steps + step
            tops[...] = jnp.where(low, top[0:rows], jnp.where(high, top[rows:], tops[...]))
            sums[...] = jnp.where(low, total[0:rows], jnp.where(high, total[rows:], sums[...]))
        terms_copy(step).start()
        return carry

    lax.fori_loop(0, steps, score_step, 0)

    for copy in others:
        copy.wait()
    total_ref[...] = jnp.zeros_like(total_ref)
    wide[...] = iq_ref[...].astype(jnp.float32).reshape(rows * iheads, depth)
    columns = jnp.concatenate([w_ref[...], jnp.zeros((LANES - iheads, rows), jnp.float32)], axis=0).T

    def logit_step(step, carry):
        weights = pltpu.roll(columns, LANES - group * step, 1)
        for j in range(group):
            head = step * group + j
            qh_ref[head] = wide[pl.ds(head, rows, stride=iheads), :].astype(jnp.bfloat16)
        chunk = qh_ref[pl.ds(step * group, group)].reshape(group * rows, depth)
        products = dot(chunk, k_ref[...], NT)
        total = total_ref[...]
        for j in range(group):
            part = products[j * rows : (j + 1) * rows]
            total = total + jnp.maximum(part, 0.0) * weights[:, j : j + 1]
        total_ref[...] = total
        return carry

    lax.fori_loop(0, steps, logit_step, 0)

    turned_tops = tops[...].T[0 : heads * steps]
    turned_sums = sums[...].T[0 : heads * steps]
    tops_ref[...] = turned_tops
    for k in range(0, keys, rows):
        logits_ref[k : k + rows] = total_ref[:, k : k + rows].T * (1.0 / math.sqrt(depth))
    logits = logits_ref[...]
    ltop = jnp.max(logits, axis=0, keepdims=True)
    lsum = jnp.sum(jnp.exp(logits - ltop), axis=0, keepdims=True)
    flat = []
    for h in range(heads):
        span = slice(h * steps, (h + 1) * steps)
        top = jnp.max(turned_tops[span], axis=0, keepdims=True)
        scaled = turned_sums[span] * jnp.exp2((turned_tops[span] - top) * SCORE2)
        flat.append((top, jnp.sum(scaled, axis=0, keepdims=True)))
    flat = jnp.concatenate([top for top, _ in flat] + [total for _, total in flat], axis=0)
    for z in range(send_ref.shape[0]):
        send_ref[z, 0 : 2 * heads] = flat
        send_ref[z, 2 * heads :] = jnp.zeros((8, rows), jnp.float32)
        send_ref[z, 2 * heads : 2 * heads + 1] = ltop
        send_ref[z, 2 * heads + 1 : 2 * heads + 2] = lsum
    for step in range(steps):
        terms_copy(step).wait()


def scores_and_logits(queries, cache, index_query, index_keys, weights, key_count):
    heads, width, rows = queries.shape
    blocks, _, keys = cache.shape
    _, iheads, depth = index_query.shape
    steps = blocks // PART
    return call(
        scores_kernel,
        "scores_and_logits",
        60,
        in_specs=[HBM] * 5,
        out_specs=[HBM] + [VMEM] * 4,
        out_shape=(
            bf16(blocks, heads, rows, keys),
            f32(heads * steps, rows),
            f32(key_count, 2 * heads + 8, rows),
            f32(keys, rows),
            bf16(iheads, rows, depth),
        ),
        scratch_shapes=[
            pltpu.VMEM((blocks, heads, rows, keys), jnp.bfloat16),
            pltpu.VMEM(queries.shape, jnp.bfloat16),
            pltpu.VMEM(cache.shape, jnp.bfloat16),
            pltpu.VMEM(index_query.shape, jnp.bfloat16),
            pltpu.VMEM(index_keys.shape, jnp.bfloat16),
            pltpu.VMEM(weights.shape, jnp.float32),
            pltpu.VMEM((rows * iheads, depth), jnp.float32),
            pltpu.VMEM((rows, keys), jnp.float32),
            pltpu.VMEM((rows * heads, width), jnp.bfloat16),
            pltpu.VMEM((rows, LANES), jnp.float32),
            pltpu.VMEM((rows, LANES), jnp.float32),
            pltpu.SemaphoreType.DMA((steps + 4,)),
            pltpu.SemaphoreType.DMA((steps,)),
        ],
    )(queries, cache, index_query, index_keys, weights)


def headsum_kernel(offsets, e_hbm, tops_ref, got_ref, *refs):
    outs, e_ref, sums, sems, out_sems = refs[0 : len(offsets)], *refs[len(offsets) :]
    _, heads, rows, keys = e_ref.shape
    steps = tops_ref.shape[0] // heads
    near, _, near_stride, far_stride = position()

    def block_of(d, k):
        return lax.rem(near + d, RING) * near_stride + k * far_stride

    def block_copy(i, d, k):
        slot = i * RING + k
        return pltpu.make_async_copy(e_hbm.at[block_of(d, k)], e_ref.at[slot], sems.at[slot])

    def out_copy(i, k):
        slot = i * RING + k
        return pltpu.make_async_copy(sums.at[slot], outs[i].at[k], out_sems.at[slot])

    for i, d in enumerate(offsets):
        for k in range(RING):
            block_copy(i, d, k).start()

    tops = got_ref[:, 0:heads]
    top = jnp.max(tops, axis=0)
    total = jnp.sum(got_ref[:, heads : 2 * heads] * jnp.exp2((tops - top[None]) * SCORE2), axis=0)
    scale = (1.0 / MH) / total
    weights = []
    for h in range(heads):
        local = tops_ref[h * steps : (h + 1) * steps] - top[h : h + 1]
        weights.append(jnp.exp2(jnp.minimum(local * SCORE2, 0.0)) * scale[h : h + 1])
    weights = jnp.concatenate(weights + [jnp.zeros((LANES - heads * steps, rows), jnp.float32)], axis=0).T
    ltops = got_ref[:, 2 * heads : 2 * heads + 1]
    ltop = jnp.max(ltops, axis=0)
    lsum = jnp.sum(got_ref[:, 2 * heads + 1 : 2 * heads + 2] * jnp.exp(ltops - ltop[None]), axis=0)
    tail = jnp.concatenate([ltop, lsum, jnp.zeros((6, rows), jnp.float32)], axis=0)
    tail = jnp.concatenate([tail, jnp.zeros((8, keys - rows), jnp.float32)], axis=1)

    for i, d in enumerate(offsets):

        def body(k, carry):
            slot = i * RING + k
            columns = pltpu.roll(weights, LANES - lax.div(block_of(d, k), PART), 1)
            block_copy(i, d, k).wait()
            total = None
            for h in range(heads):
                term = e_ref[slot, h].astype(jnp.float32) * columns[:, h * steps : h * steps + 1]
                total = term if total is None else total + term
            sums[slot, 0:rows] = total
            sums[slot, rows:] = tail
            out_copy(i, k).start()
            return carry

        lax.fori_loop(0, RING, body, 0)
    for i, _ in enumerate(offsets):
        for k in range(RING):
            out_copy(i, k).wait()


def head_sum(offsets, terms, tops, got, flops=0):
    blocks, heads, rows, keys = terms.shape
    slots = len(offsets) * RING
    return call(
        functools.partial(headsum_kernel, offsets),
        "head_sum",
        56,
        flops,
        in_specs=[HBM] + [VMEM] * 2,
        out_specs=[HBM] * len(offsets),
        out_shape=[f32(blocks // RING, rows + 8, keys)] * len(offsets),
        scratch_shapes=[
            pltpu.VMEM((slots, heads, rows, keys), jnp.bfloat16),
            pltpu.VMEM((slots, rows + 8, keys), jnp.float32),
            pltpu.SemaphoreType.DMA((slots,)),
            pltpu.SemaphoreType.DMA((slots,)),
        ],
    )(terms, tops, got)


def merged_stats(tops, sums):
    top = tops[0]
    for other in tops[1:]:
        top = jnp.maximum(top, other)
    total = sums[0] * jnp.exp(tops[0] - top)
    for other, count in zip(tops[1:], sums[1:]):
        total = total + count * jnp.exp(other - top)
    return top, total


def partial_kernel(*refs):
    got, outs = refs[0:RING], refs[RING:]
    rows = outs[0].shape[0] - 8
    _, far, _, _ = position()
    top, total = merged_stats([r[0, rows : rows + 1] for r in got], [r[0, rows + 1 : rows + 2] for r in got])
    for d in range(RING):
        k = lax.rem(far + d, RING)
        outs[d][0:rows] = got[0][k, 0:rows] + got[1][k, 0:rows] + (got[2][k, 0:rows] + got[3][k, 0:rows])
        outs[d][rows:] = jnp.zeros_like(outs[d][rows:])
        outs[d][rows : rows + 1] = top
        outs[d][rows + 1 : rows + 2] = total


def partial_sum(got):
    _, height, keys = got[0].shape
    return call(
        partial_kernel,
        "partial_sum",
        in_specs=[VMEM] * RING,
        out_specs=[VMEM] * RING,
        out_shape=[f32(height, keys)] * RING,
    )(*got)


GROUP = 8


def dlogits_kernel(key_total, *refs):
    got = refs[0:RING]
    logits_ref, qh_ref, k_ref, send_ref, turned = refs[RING:]
    heads, rows, depth = qh_ref.shape
    keys = k_ref.shape[0]
    root = 1.0 / math.sqrt(depth)

    ltop, lsum = merged_stats(
        [r[rows : rows + 1, 0:rows] for r in got], [r[rows + 1 : rows + 2, 0:rows] for r in got]
    )
    target = got[0][0:rows] + got[1][0:rows] + (got[2][0:rows] + got[3][0:rows])
    soft = jnp.exp(logits_ref[...] - ltop) * (1.0 / lsum)
    for k in range(0, keys, rows):
        turned[k : k + rows] = key_total * (soft[k : k + rows] - target[:, k : k + rows].T)
        send_ref[0:rows, k : k + rows] = turned[k : k + rows].T
        send_ref[rows + heads // 2 :, k : k + rows] = k_ref[k : k + rows].astype(jnp.float32)

    def step(i, first, column):
        sums = []
        for j in range(GROUP):
            products = dot(k_ref[...], qh_ref[i * GROUP + j], NT)
            sums.append(jnp.sum(jnp.maximum(products, 0.0) * turned[...], axis=0, keepdims=True) * root)
        place = pl.ds(pl.multiple_of(rows + first, GROUP), GROUP)
        send_ref[place, column : column + rows] = jnp.concatenate(sums, axis=0)

    half = heads // 2 // GROUP

    def low(i, carry):
        step(i, i * GROUP, 0)
        return carry

    def high(i, carry):
        step(i + half, i * GROUP, rows)
        return carry

    lax.fori_loop(0, half, low, 0)
    lax.fori_loop(0, half, high, 0)


def dlogits_of(got, logits, qh, index_keys, key_total):
    heads, rows, depth = qh.shape
    keys = index_keys.shape[0]
    return call(
        functools.partial(dlogits_kernel, key_total),
        "dlogits",
        24,
        out_shape=f32(2 * rows + heads // 2, keys),
        scratch_shapes=[pltpu.VMEM((keys, rows), jnp.float32)],
    )(*got, logits, qh, index_keys)


def keys_kernel(dlogits_ref, qh_ref, k_ref, w_ref, keys_ref, slopes, turned):
    heads, rows, depth = qh_ref.shape
    root = 1.0 / math.sqrt(depth)
    for k in range(0, k_ref.shape[0], rows):
        turned[k : k + rows] = dlogits_ref[0:rows, k : k + rows].T
    keys_ref[...] = jnp.zeros_like(keys_ref)

    def step(i, carry):
        weights = w_ref[pl.ds(i * GROUP, GROUP)] * root
        for j in range(GROUP):
            products = dot(k_ref[...], qh_ref[i * GROUP + j], NT)
            slope = jnp.where(products > 0.0, turned[...] * weights[j : j + 1], 0.0)
            slopes[:, j * rows : (j + 1) * rows] = slope.astype(jnp.bfloat16)
        chunk = qh_ref[pl.ds(i * GROUP, GROUP)].reshape(GROUP * rows, depth)
        keys_ref[...] += dot(slopes[...], chunk, NN)
        return carry

    lax.fori_loop(0, heads // GROUP, step, 0)


def key_gradient(dlogits, qh, index_keys, weights):
    heads, rows, depth = qh.shape
    keys = index_keys.shape[0]
    return call(
        keys_kernel,
        "key_gradient",
        24,
        BESIDE,
        out_shape=f32(keys, depth),
        scratch_shapes=[pltpu.VMEM((keys, GROUP * rows), jnp.bfloat16), pltpu.VMEM((keys, rows), jnp.float32)],
    )(dlogits, qh, index_keys, weights)


def query_kernel(offsets, pieces, *refs):
    ring, count = RING, len(offsets)
    got = refs[0:ring]
    qh_ref, w_ref = refs[ring : ring + 2]
    outs = refs[ring + 2 : ring + 2 + count]
    slopes, acc, near, dlogits = refs[ring + 2 + count :]
    heads, rows, depth = qh_ref.shape
    keys = got[0].shape[1]
    share = heads // (ring * ring)
    extra = heads // 2
    root = 1.0 / math.sqrt(depth)
    near_at, far_at, near_stride, far_stride = position()
    span = rows // pieces
    few = extra // pieces

    wsum = got[0][rows : rows + extra]
    for d in range(1, ring):
        wsum = wsum + got[d][rows : rows + extra]
    for d in range(ring):
        for k in range(0, keys, rows):
            near[d * keys + k : d * keys + k + rows] = got[d][rows + extra :, k : k + rows].astype(jnp.bfloat16)
        dlogits[:, d * keys : (d + 1) * keys] = got[d][0:rows] * root
    columns = jnp.concatenate([w_ref[...], jnp.zeros((LANES - heads, rows), jnp.float32)], axis=0).T

    for i, d in enumerate(offsets):
        first = (lax.rem(far_at + d, ring) * far_stride + near_at * near_stride) * share
        weights = pltpu.roll(columns, LANES - first, 1)
        queries = qh_ref[pl.ds(first, share)].reshape(share * rows, depth)
        for k in range(0, ring * keys, keys):
            products = dot(queries, near[k : k + keys], NT)
            for j in range(share):
                part = products[j * rows : (j + 1) * rows]
                slope = jnp.where(part > 0.0, dlogits[:, k : k + keys] * weights[:, j : j + 1], 0.0)
                slopes[j * rows : (j + 1) * rows, k : k + keys] = slope.astype(jnp.bfloat16)
        acc[...] = dot(slopes[...], near[...], NN)
        for z in range(pieces):
            for j in range(share):
                start = j * rows + z * span
                outs[i][z, pl.ds(j, span, stride=share), :] = acc[start : start + span]
            piece = wsum[z * few : (z + 1) * few]
            outs[i][z, share * span : share * span + few] = piece[:, 0:rows]
            outs[i][z, share * span + few :] = piece[:, rows : 2 * rows]


def query_gradient(offsets, got, qh, weights, pieces, flops=0):
    keys = got[0].shape[1]
    heads, rows, depth = qh.shape
    share = heads // (RING * RING)
    tall = share * (rows // pieces) + heads // pieces
    return call(
        functools.partial(query_kernel, offsets, pieces),
        "query_gradient",
        24,
        flops,
        in_specs=[VMEM] * (RING + 2),
        out_specs=[VMEM] * len(offsets),
        out_shape=[f32(pieces, tall, depth)] * len(offsets),
        scratch_shapes=[
            pltpu.VMEM((share * rows, RING * keys), jnp.bfloat16),
            pltpu.VMEM((share * rows, depth), jnp.float32),
            pltpu.VMEM((RING * keys, depth), jnp.bfloat16),
            pltpu.VMEM((rows, RING * keys), jnp.float32),
        ],
    )(*got, qh, weights)


def results_kernel(got_ref, query_ref, weight_ref):
    pieces, tall, depth = got_ref.shape
    span = query_ref.shape[1]
    few = (tall - span) // 2
    query_ref[...] = got_ref[:, 0:span]
    for z in range(pieces):
        weight_ref[z * few : (z + 1) * few] = got_ref[z, span : span + few]
        weight_ref[(pieces + z) * few : (pieces + z + 1) * few] = got_ref[z, span + few :]


def results(got, heads, span):
    pieces, _, depth = got.shape
    return call(
        results_kernel,
        "results",
        16,
        out_shape=(f32(pieces, span, depth), f32(heads, depth)),
    )(got)


def exchange(x, axis):
    return lax.all_to_all(x, axis, split_axis=0, concat_axis=0, tiled=True)


def shift(x, d, across):
    pairs = []
    for a in range(RING):
        for b in range(RING):
            for row in range(2):
                if (row == 1) != across:
                    there = (a + d) % RING * RING + b
                else:
                    there = a * RING + (b + d) % RING
                pairs.append(((a * RING + b) * 2 + row, there * 2 + row))
    return lax.ppermute(x, ("head", "row"), pairs)


def shards(mla_query, mla_cache, index_query, index_keys, index_weight):
    key_count = lax.axis_size("key")
    head_count = lax.axis_size("head")
    rows = mla_query.shape[0]
    keys, depth = index_keys.shape
    heads = index_query.shape[1]
    share = heads // head_count
    row_index = lax.axis_index("row")
    weights = index_weight.T
    queries = jnp.transpose(mla_query, (1, 2, 0))
    cache = jnp.swapaxes(mla_cache, 1, 2)
    terms, tops, send1, logits, qh = scores_and_logits(queries, cache, index_query, index_keys, weights, key_count)
    got1 = exchange(send1, "key")
    sides = head_sum((1, 3), terms, tops, got1)
    rest = head_sum((2, 0), terms, tops, got1)
    got2 = [rest[1], shift(sides[0], 1, False), shift(rest[0], 2, False), shift(sides[1], 3, False)]
    send2 = partial_sum(got2)
    got2 = [send2[0]] + [shift(send2[d], d, True) for d in (1, 2, 3)]
    key_total = float(keys * head_count * key_count)
    send3 = dlogits_of(got2, logits, qh, index_keys, key_total)
    got3 = [send3] + [shift(send3, d, False) for d in range(1, RING)]
    keys_part = key_gradient(send3, qh, index_keys, weights)
    got3, keys_part = lax.optimization_barrier((got3, keys_part))

    half = keys // 2
    away = lax.dynamic_slice_in_dim(keys_part, (1 - row_index) * half, half, 0)
    near = lax.dynamic_slice_in_dim(keys_part, row_index * half, half, 0)
    key_grad = near + lax.ppermute(away, "row", [(0, 1), (1, 0)])

    sides = query_gradient((1, 3), got3, qh, weights, key_count)
    rest = query_gradient((2, 0), got3, qh, weights, key_count)
    one, three, two = shift(sides[0], 1, True), shift(sides[1], 3, True), shift(rest[0], 2, True)
    send4 = rest[1] + one + (two + three)
    got4 = jnp.sum(exchange(send4, "key"), axis=0)
    got5 = exchange(jnp.broadcast_to(got4[None], (key_count, *got4.shape)), "key")
    query_grad, weight_grad = results(got5, heads, share * (rows // key_count))
    return (query_grad.reshape(rows, share, depth), key_grad, weight_grad.T)


def solution(mesh):
    placed = (
        P("row", "head", None),
        P(None, "key", None),
        P("row", None, None),
        P(("head", "key"), None),
        P("row", None),
    )
    return jax.shard_map(
        shards,
        mesh=mesh,
        in_specs=placed,
        out_specs=(P("row", "head", None), P(("head", "key", "row"), None), P("row", None)),
        check_vma=False,
    )
```

```python
import functools
import math

import jax
import jax.numpy as jnp
from jax import lax
from jax.experimental import pallas as pl
from jax.experimental.pallas import tpu as pltpu
from jax.sharding import PartitionSpec as P

MH = 128
LOG2E = 1.4426950408889634
SCORE2 = LOG2E / math.sqrt(192.0)
LANES = 128
NT = (((1,), (1,)), ((), ()))
TN = (((0,), (0,)), ((), ()))
NN = (((1,), (0,)), ((), ()))


def dot(a, b, dims):
    return lax.dot_general(a, b, dims, preferred_element_type=jnp.float32)


def lane_iota(rows):
    return lax.broadcasted_iota(jnp.int32, (rows, LANES), 1)


RING = 4
PART = 4
GROUP = 8
VMEM = pl.BlockSpec(memory_space=pltpu.VMEM)
HBM = pl.BlockSpec(memory_space=pltpu.HBM)


def call(kernel, name, megabytes=32, **options):
    return pl.pallas_call(
        kernel,
        name=name,
        compiler_params=pltpu.CompilerParams(vmem_limit_bytes=megabytes << 20),
        **options,
    )


def f32(*shape):
    return jax.ShapeDtypeStruct(shape, jnp.float32)


def bf16(*shape):
    return jax.ShapeDtypeStruct(shape, jnp.bfloat16)


def position():
    head, first = lax.axis_index("head"), lax.axis_index("row") == 0
    x, y = lax.div(head, RING), lax.rem(head, RING)
    return jnp.where(first, y, x), jnp.where(first, x, y), jnp.where(first, 1, RING), jnp.where(first, RING, 1)


def scores_kernel(
    q_hbm, c_hbm, iq_hbm, k_hbm, w_hbm,
    e_hbm, tops_ref, send_ref, logits_ref, qh_ref,
    e_ref, q_ref, c_ref, iq_ref, k_ref, w_ref, wide, total_ref, queries_ref, tops, sums, sems, out_sems,
):
    heads, width, rows = q_ref.shape
    blocks = c_ref.shape[0]
    steps = blocks // PART
    _, iheads, depth = iq_ref.shape
    keys = k_ref.shape[0]
    group = GROUP

    first = pltpu.make_async_copy(q_hbm, q_ref, sems.at[steps])
    first.start()

    def part_copy(step):
        span = pl.ds(step * PART, PART)
        return pltpu.make_async_copy(c_hbm.at[span], c_ref.at[span], sems.at[step])

    def terms_copy(step):
        span = pl.ds(step * PART, PART)
        return pltpu.make_async_copy(e_ref.at[span], e_hbm.at[span], out_sems.at[step])

    others = [(iq_hbm, iq_ref), (k_hbm, k_ref), (w_hbm, w_ref)]
    others = [pltpu.make_async_copy(src, dst, sems.at[steps + 1 + i]) for i, (src, dst) in enumerate(others)]
    for step in range(steps):
        part_copy(step).start()
    for copy in others:
        copy.start()

    tops[...] = jnp.zeros_like(tops)
    sums[...] = jnp.zeros_like(sums)
    first.wait()
    for h in range(heads):
        queries_ref[h * rows : (h + 1) * rows] = q_ref[h].T
    lane = lane_iota(rows)

    def score_step(step, carry):
        part_copy(step).wait()
        for h in range(0, heads, 2):
            queries = queries_ref[h * rows : (h + 2) * rows]
            scores = [dot(queries, c_ref[step * PART + j], NN) for j in range(PART)]
            top = scores[0]
            for score in scores[1:]:
                top = jnp.maximum(top, score)
            top = jnp.max(top, axis=1, keepdims=True)
            total = None
            for j, score in enumerate(scores):
                terms = jnp.exp2((score - top) * SCORE2)
                total = terms if total is None else total + terms
                e_ref[step * PART + j, h : h + 2] = terms.astype(jnp.bfloat16).reshape(2, rows, keys)
            total = jnp.sum(total, axis=1, keepdims=True)
            low, high = lane == h * steps + step, lane == (h + 1) * steps + step
            tops[...] = jnp.where(low, top[0:rows], jnp.where(high, top[rows:], tops[...]))
            sums[...] = jnp.where(low, total[0:rows], jnp.where(high, total[rows:], sums[...]))
        terms_copy(step).start()
        return carry

    lax.fori_loop(0, steps, score_step, 0)

    for copy in others:
        copy.wait()
    total_ref[...] = jnp.zeros_like(total_ref)
    wide[...] = iq_ref[...].astype(jnp.float32).reshape(rows * iheads, depth)
    columns = jnp.concatenate([w_ref[...], jnp.zeros((LANES - iheads, rows), jnp.float32)], axis=0).T

    def logit_step(step, carry):
        weights = pltpu.roll(columns, LANES - group * step, 1)
        for j in range(group):
            head = step * group + j
            qh_ref[head] = wide[pl.ds(head, rows, stride=iheads), :].astype(jnp.bfloat16)
        chunk = qh_ref[pl.ds(step * group, group)].reshape(group * rows, depth)
        products = dot(chunk, k_ref[...], NT)
        total = total_ref[...]
        for j in range(group):
            part = products[j * rows : (j + 1) * rows]
            total = total + jnp.maximum(part, 0.0) * weights[:, j : j + 1]
        total_ref[...] = total
        return carry

    lax.fori_loop(0, iheads // group, logit_step, 0)

    turned_tops = tops[...].T[0 : heads * steps]
    turned_sums = sums[...].T[0 : heads * steps]
    tops_ref[...] = turned_tops
    for k in range(0, keys, rows):
        logits_ref[k : k + rows] = total_ref[:, k : k + rows].T * (1.0 / math.sqrt(depth))
    logits = logits_ref[...]
    ltop = jnp.max(logits, axis=0, keepdims=True)
    lsum = jnp.sum(jnp.exp(logits - ltop), axis=0, keepdims=True)
    flat = []
    for h in range(heads):
        span = slice(h * steps, (h + 1) * steps)
        top = jnp.max(turned_tops[span], axis=0, keepdims=True)
        scaled = turned_sums[span] * jnp.exp2((turned_tops[span] - top) * SCORE2)
        flat.append((top, jnp.sum(scaled, axis=0, keepdims=True)))
    flat = jnp.concatenate([top for top, _ in flat] + [total for _, total in flat], axis=0)
    for z in range(send_ref.shape[0]):
        send_ref[z, 0 : 2 * heads] = flat
        send_ref[z, 2 * heads :] = jnp.zeros((8, rows), jnp.float32)
        send_ref[z, 2 * heads : 2 * heads + 1] = ltop
        send_ref[z, 2 * heads + 1 : 2 * heads + 2] = lsum
    for step in range(steps):
        terms_copy(step).wait()


def scores_and_logits(queries, cache, index_query, index_keys, weights, key_count):
    heads, width, rows = queries.shape
    blocks, _, keys = cache.shape
    _, iheads, depth = index_query.shape
    steps = blocks // PART
    return call(
        scores_kernel,
        "scores_and_logits",
        60,
        in_specs=[HBM] * 5,
        out_specs=[HBM] + [VMEM] * 4,
        out_shape=(
            bf16(blocks, heads, rows, keys),
            f32(heads * steps, rows),
            f32(key_count, 2 * heads + 8, rows),
            f32(keys, rows),
            bf16(iheads, rows, depth),
        ),
        scratch_shapes=[
            pltpu.VMEM((blocks, heads, rows, keys), jnp.bfloat16),
            pltpu.VMEM(queries.shape, jnp.bfloat16),
            pltpu.VMEM(cache.shape, jnp.bfloat16),
            pltpu.VMEM(index_query.shape, jnp.bfloat16),
            pltpu.VMEM(index_keys.shape, jnp.bfloat16),
            pltpu.VMEM(weights.shape, jnp.float32),
            pltpu.VMEM((rows * iheads, depth), jnp.float32),
            pltpu.VMEM((rows, keys), jnp.float32),
            pltpu.VMEM((rows * heads, width), jnp.bfloat16),
            pltpu.VMEM((rows, LANES), jnp.float32),
            pltpu.VMEM((rows, LANES), jnp.float32),
            pltpu.SemaphoreType.DMA((steps + 4,)),
            pltpu.SemaphoreType.DMA((steps,)),
        ],
    )(queries, cache, index_query, index_keys, weights)


def headsum_kernel(offsets, stays, e_hbm, tops_ref, got_ref, *refs):
    outs, e_ref, sums, sems, out_sems = refs[0 : len(offsets)], *refs[len(offsets) :]
    _, heads, rows, keys = e_ref.shape
    steps = tops_ref.shape[0] // heads
    near, _, near_stride, far_stride = position()

    def block_of(d, k):
        return lax.rem(near + d, RING) * near_stride + k * far_stride

    def block_copy(i, d, k):
        slot = i * RING + k
        return pltpu.make_async_copy(e_hbm.at[block_of(d, k)], e_ref.at[slot], sems.at[slot])

    def out_copy(i, k):
        slot = i * RING + k
        return pltpu.make_async_copy(sums.at[slot], outs[i].at[k], out_sems.at[slot])

    for i, d in enumerate(offsets):
        for k in range(RING):
            block_copy(i, d, k).start()

    tops = got_ref[:, 0:heads]
    top = jnp.max(tops, axis=0)
    total = jnp.sum(got_ref[:, heads : 2 * heads] * jnp.exp2((tops - top[None]) * SCORE2), axis=0)
    scale = (1.0 / MH) / total
    weights = []
    for h in range(heads):
        local = tops_ref[h * steps : (h + 1) * steps] - top[h : h + 1]
        weights.append(jnp.exp2(jnp.minimum(local * SCORE2, 0.0)) * scale[h : h + 1])
    weights = jnp.concatenate(weights + [jnp.zeros((LANES - heads * steps, rows), jnp.float32)], axis=0).T
    ltops = got_ref[:, 2 * heads : 2 * heads + 1]
    ltop = jnp.max(ltops, axis=0)
    lsum = jnp.sum(got_ref[:, 2 * heads + 1 : 2 * heads + 2] * jnp.exp(ltops - ltop[None]), axis=0)
    tail = jnp.concatenate([ltop, lsum, jnp.zeros((6, rows), jnp.float32)], axis=0)
    tail = jnp.concatenate([tail, jnp.zeros((8, keys - rows), jnp.float32)], axis=1)

    for i, d in enumerate(offsets):

        def body(k, carry):
            slot = i * RING + k
            columns = pltpu.roll(weights, LANES - lax.div(block_of(d, k), PART), 1)
            block_copy(i, d, k).wait()
            total = None
            for h in range(heads):
                term = e_ref[slot, h].astype(jnp.float32) * columns[:, h * steps : h * steps + 1]
                total = term if total is None else total + term
            place = outs[i].at[k] if stays else sums.at[slot]
            place[0:rows] = total
            place[rows:] = tail
            if not stays:
                out_copy(i, k).start()
            return carry

        lax.fori_loop(0, RING, body, 0)
    for i, _ in enumerate(offsets):
        for k in range(0 if stays else RING):
            out_copy(i, k).wait()


def head_sum(offsets, terms, tops, got, stays=False):
    blocks, heads, rows, keys = terms.shape
    slots = len(offsets) * RING
    return call(
        functools.partial(headsum_kernel, offsets, stays),
        "head_sum",
        53 if stays else 56,
        in_specs=[HBM] + [VMEM] * 2,
        out_specs=[VMEM if stays else HBM] * len(offsets),
        out_shape=[f32(blocks // RING, rows + 8, keys)] * len(offsets),
        scratch_shapes=[
            pltpu.VMEM((slots, heads, rows, keys), jnp.bfloat16),
            pltpu.VMEM((slots, rows + 8, keys), jnp.float32),
            pltpu.SemaphoreType.DMA((slots,)),
            pltpu.SemaphoreType.DMA((slots,)),
        ],
    )(terms, tops, got)


def merged_stats(tops, sums):
    top = tops[0]
    for other in tops[1:]:
        top = jnp.maximum(top, other)
    total = sums[0] * jnp.exp(tops[0] - top)
    for other, count in zip(tops[1:], sums[1:]):
        total = total + count * jnp.exp(other - top)
    return top, total


def partial_kernel(*refs):
    got, outs = refs[0:RING], refs[RING:]
    rows = outs[0].shape[0] - 8
    _, far, _, _ = position()
    top, total = merged_stats([r[0, rows : rows + 1] for r in got], [r[0, rows + 1 : rows + 2] for r in got])
    for d in range(RING):
        k = lax.rem(far + d, RING)
        outs[d][0:rows] = got[0][k, 0:rows] + got[1][k, 0:rows] + (got[2][k, 0:rows] + got[3][k, 0:rows])
        outs[d][rows:] = jnp.zeros_like(outs[d][rows:])
        outs[d][rows : rows + 1] = top
        outs[d][rows + 1 : rows + 2] = total


def partial_sum(got):
    _, height, keys = got[0].shape
    return call(
        partial_kernel,
        "partial_sum",
        in_specs=[VMEM] * RING,
        out_specs=[VMEM] * RING,
        out_shape=[f32(height, keys)] * RING,
    )(*got)


def dlogits_kernel(key_total, *refs):
    got = refs[0:RING]
    logits_ref, qh_ref, k_ref, send_ref, turned = refs[RING:]
    heads, rows, depth = qh_ref.shape
    keys = k_ref.shape[0]
    root = 1.0 / math.sqrt(depth)

    ltop, lsum = merged_stats(
        [r[rows : rows + 1, 0:rows] for r in got], [r[rows + 1 : rows + 2, 0:rows] for r in got]
    )
    target = got[0][0:rows] + got[1][0:rows] + (got[2][0:rows] + got[3][0:rows])
    soft = jnp.exp(logits_ref[...] - ltop) * (1.0 / lsum)
    for k in range(0, keys, rows):
        turned[k : k + rows] = key_total * (soft[k : k + rows] - target[:, k : k + rows].T)
        send_ref[0:rows, k : k + rows] = turned[k : k + rows].T
        send_ref[rows + heads // 2 :, k : k + rows] = k_ref[k : k + rows].astype(jnp.float32)

    def step(i, first, column):
        sums = []
        for j in range(GROUP):
            products = dot(k_ref[...], qh_ref[i * GROUP + j], NT)
            sums.append(jnp.sum(jnp.maximum(products, 0.0) * turned[...], axis=0, keepdims=True) * root)
        place = pl.ds(pl.multiple_of(rows + first, GROUP), GROUP)
        send_ref[place, column : column + rows] = jnp.concatenate(sums, axis=0)

    half = heads // 2 // GROUP

    def low(i, carry):
        step(i, i * GROUP, 0)
        return carry

    def high(i, carry):
        step(i + half, i * GROUP, rows)
        return carry

    lax.fori_loop(0, half, low, 0)
    lax.fori_loop(0, half, high, 0)


def dlogits_of(got, logits, qh, index_keys, key_total):
    heads, rows, depth = qh.shape
    keys = index_keys.shape[0]
    return call(
        functools.partial(dlogits_kernel, key_total),
        "dlogits",
        24,
        out_shape=f32(2 * rows + heads // 2, keys),
        scratch_shapes=[pltpu.VMEM((keys, rows), jnp.float32)],
    )(*got, logits, qh, index_keys)


def keys_kernel(dlogits_ref, qh_ref, k_ref, w_ref, keys_ref, slopes, turned):
    heads, rows, depth = qh_ref.shape
    root = 1.0 / math.sqrt(depth)
    for k in range(0, k_ref.shape[0], rows):
        turned[k : k + rows] = dlogits_ref[0:rows, k : k + rows].T
    keys_ref[...] = jnp.zeros_like(keys_ref)

    def step(i, carry):
        weights = w_ref[pl.ds(i * GROUP, GROUP)] * root
        for j in range(GROUP):
            products = dot(k_ref[...], qh_ref[i * GROUP + j], NT)
            slope = jnp.where(products > 0.0, turned[...] * weights[j : j + 1], 0.0)
            slopes[:, j * rows : (j + 1) * rows] = slope.astype(jnp.bfloat16)
        chunk = qh_ref[pl.ds(i * GROUP, GROUP)].reshape(GROUP * rows, depth)
        keys_ref[...] += dot(slopes[...], chunk, NN)
        return carry

    lax.fori_loop(0, heads // GROUP, step, 0)


def key_gradient(dlogits, qh, index_keys, weights):
    heads, rows, depth = qh.shape
    keys = index_keys.shape[0]
    return call(
        keys_kernel,
        "key_gradient",
        24,
        out_shape=f32(keys, depth),
        scratch_shapes=[pltpu.VMEM((keys, GROUP * rows), jnp.bfloat16), pltpu.VMEM((keys, rows), jnp.float32)],
    )(dlogits, qh, index_keys, weights)


def query_kernel(offsets, pieces, *refs):
    ring, count = RING, len(offsets)
    got = refs[0:ring]
    qh_ref, w_ref = refs[ring : ring + 2]
    outs = refs[ring + 2 : ring + 2 + count]
    slopes, acc, near, dlogits = refs[ring + 2 + count :]
    heads, rows, depth = qh_ref.shape
    keys = got[0].shape[1]
    share = heads // (ring * ring)
    extra = heads // 2
    root = 1.0 / math.sqrt(depth)
    near_at, far_at, near_stride, far_stride = position()
    span = rows // pieces
    few = extra // pieces

    wsum = got[0][rows : rows + extra]
    for d in range(1, ring):
        wsum = wsum + got[d][rows : rows + extra]
    for d in range(ring):
        for k in range(0, keys, rows):
            near[d * keys + k : d * keys + k + rows] = got[d][rows + extra :, k : k + rows].astype(jnp.bfloat16)
        dlogits[:, d * keys : (d + 1) * keys] = got[d][0:rows] * root
    columns = jnp.concatenate([w_ref[...], jnp.zeros((LANES - heads, rows), jnp.float32)], axis=0).T

    for i, d in enumerate(offsets):
        first = (lax.rem(far_at + d, ring) * far_stride + near_at * near_stride) * share
        weights = pltpu.roll(columns, LANES - first, 1)
        queries = qh_ref[pl.ds(first, share)].reshape(share * rows, depth)
        for k in range(0, ring * keys, keys):
            products = dot(queries, near[k : k + keys], NT)
            for j in range(share):
                part = products[j * rows : (j + 1) * rows]
                slope = jnp.where(part > 0.0, dlogits[:, k : k + keys] * weights[:, j : j + 1], 0.0)
                slopes[j * rows : (j + 1) * rows, k : k + keys] = slope.astype(jnp.bfloat16)
        acc[...] = dot(slopes[...], near[...], NN)
        for z in range(pieces):
            for j in range(share):
                start = j * rows + z * span
                outs[i][z, pl.ds(j, span, stride=share), :] = acc[start : start + span]
            piece = wsum[z * few : (z + 1) * few]
            outs[i][z, share * span : share * span + few] = piece[:, 0:rows]
            outs[i][z, share * span + few :] = piece[:, rows : 2 * rows]


def query_gradient(offsets, got, qh, weights, pieces):
    keys = got[0].shape[1]
    heads, rows, depth = qh.shape
    share = heads // (RING * RING)
    tall = share * (rows // pieces) + heads // pieces
    return call(
        functools.partial(query_kernel, offsets, pieces),
        "query_gradient",
        24,
        in_specs=[VMEM] * (RING + 2),
        out_specs=[VMEM] * len(offsets),
        out_shape=[f32(pieces, tall, depth)] * len(offsets),
        scratch_shapes=[
            pltpu.VMEM((share * rows, RING * keys), jnp.bfloat16),
            pltpu.VMEM((share * rows, depth), jnp.float32),
            pltpu.VMEM((RING * keys, depth), jnp.bfloat16),
            pltpu.VMEM((rows, RING * keys), jnp.float32),
        ],
    )(*got, qh, weights)


def results_kernel(got_ref, query_ref, weight_ref):
    pieces, tall, depth = got_ref.shape
    span = query_ref.shape[1]
    few = (tall - span) // 2
    query_ref[...] = got_ref[:, 0:span]
    for z in range(pieces):
        weight_ref[z * few : (z + 1) * few] = got_ref[z, span : span + few]
        weight_ref[(pieces + z) * few : (pieces + z + 1) * few] = got_ref[z, span + few :]


def results(got, heads, span):
    pieces, _, depth = got.shape
    return call(
        results_kernel,
        "results",
        16,
        out_shape=(f32(pieces, span, depth), f32(heads, depth)),
    )(got)


def exchange(x, axis):
    return lax.all_to_all(x, axis, split_axis=0, concat_axis=0, tiled=True)


def shift(x, d, across):
    pairs = []
    for a in range(RING):
        for b in range(RING):
            for row in range(2):
                if (row == 1) != across:
                    there = (a + d) % RING * RING + b
                else:
                    there = a * RING + (b + d) % RING
                pairs.append(((a * RING + b) * 2 + row, there * 2 + row))
    return lax.ppermute(x, ("head", "row"), pairs)


def shards(mla_query, mla_cache, index_query, index_keys, index_weight):
    key_count = lax.axis_size("key")
    head_count = lax.axis_size("head")
    rows = mla_query.shape[0]
    keys, depth = index_keys.shape
    heads = index_query.shape[1]
    share = heads // head_count
    row_index = lax.axis_index("row")
    weights = index_weight.T
    queries = jnp.transpose(mla_query, (1, 2, 0))
    cache = jnp.swapaxes(mla_cache, 1, 2)
    terms, tops, send1, logits, qh = scores_and_logits(queries, cache, index_query, index_keys, weights, key_count)
    got1 = exchange(send1, "key")
    (far_two,) = head_sum((2,), terms, tops, got1)
    got1, _ = lax.optimization_barrier((got1, far_two))
    sides = head_sum((1, 3), terms, tops, got1)
    (own,) = head_sum((0,), terms, tops, got1, True)
    two = shift(far_two, 2, False)
    one = shift(sides[0], 1, False)
    three = shift(sides[1], 3, False)
    got2 = [own, one, two, three]
    send2 = partial_sum(got2)
    got2 = [send2[0]] + [shift(send2[d], d, True) for d in (1, 2, 3)]
    key_total = float(keys * head_count * key_count)
    send3 = dlogits_of(got2, logits, qh, index_keys, key_total)
    got3 = [send3] + [shift(send3, d, False) for d in range(1, RING)]
    keys_part = key_gradient(send3, qh, index_keys, weights)
    got3, keys_part = lax.optimization_barrier((got3, keys_part))

    half = keys // 2
    away = lax.dynamic_slice_in_dim(keys_part, (1 - row_index) * half, half, 0)
    near = lax.dynamic_slice_in_dim(keys_part, row_index * half, half, 0)
    key_grad = near + lax.ppermute(away, "row", [(0, 1), (1, 0)])

    (far_two,) = query_gradient((2,), got3, qh, weights, key_count)
    got3, _ = lax.optimization_barrier((got3, far_two))
    sides = query_gradient((1, 3), got3, qh, weights, key_count)
    (own,) = query_gradient((0,), got3, qh, weights, key_count)
    two = shift(far_two, 2, True)
    one = shift(sides[0], 1, True)
    three = shift(sides[1], 3, True)
    send4 = own + one + (two + three)
    got4 = jnp.sum(exchange(send4, "key"), axis=0)
    got5 = exchange(jnp.broadcast_to(got4[None], (key_count, *got4.shape)), "key")
    query_grad, weight_grad = results(got5, heads, share * (rows // key_count))
    return (query_grad.reshape(rows, share, depth), key_grad, weight_grad.T)


def solution(mesh):
    placed = (
        P("row", "head", None),
        P(None, "key", None),
        P("row", None, None),
        P(("head", "key"), None),
        P("row", None),
    )
    return jax.shard_map(
        shards,
        mesh=mesh,
        in_specs=placed,
        out_specs=(P("row", "head", None), P(("head", "key", "row"), None), P("row", None)),
        check_vma=False,
    )
```

```python
import functools
import math

import jax
import jax.numpy as jnp
from jax import lax
from jax.experimental import pallas as pl
from jax.experimental.pallas import tpu as pltpu
from jax.sharding import PartitionSpec as P

MH = 128
LOG2E = 1.4426950408889634
SCORE2 = LOG2E / math.sqrt(192.0)
LANES = 128
NT = (((1,), (1,)), ((), ()))
TN = (((0,), (0,)), ((), ()))
NN = (((1,), (0,)), ((), ()))


def dot(a, b, dims):
    return lax.dot_general(a, b, dims, preferred_element_type=jnp.float32)


def lane_iota(rows):
    return lax.broadcasted_iota(jnp.int32, (rows, LANES), 1)


RING = 4
PART = 4
GROUP = 8
VMEM = pl.BlockSpec(memory_space=pltpu.VMEM)
HBM = pl.BlockSpec(memory_space=pltpu.HBM)


def call(kernel, name, megabytes=32, **options):
    return pl.pallas_call(
        kernel,
        name=name,
        compiler_params=pltpu.CompilerParams(vmem_limit_bytes=megabytes << 20),
        **options,
    )


def in_hbm(x):
    return pltpu.with_memory_space_constraint(x, pltpu.HBM)


def f32(*shape):
    return jax.ShapeDtypeStruct(shape, jnp.float32)


def bf16(*shape):
    return jax.ShapeDtypeStruct(shape, jnp.bfloat16)


def position():
    head, first = lax.axis_index("head"), lax.axis_index("row") == 0
    x, y = lax.div(head, RING), lax.rem(head, RING)
    return jnp.where(first, y, x), jnp.where(first, x, y), jnp.where(first, 1, RING), jnp.where(first, RING, 1)


def scores_kernel(
    q_hbm, c_hbm, iq_hbm, k_hbm, w_hbm,
    e_ref, tops_ref, send_ref, logits_ref, qh_ref,
    q_ref, c_ref, iq_ref, k_ref, w_ref, wide, total_ref, queries_ref, tops, sums, sems,
):
    heads, width, rows = q_ref.shape
    blocks = c_ref.shape[0]
    steps = blocks // PART
    _, iheads, depth = iq_ref.shape
    keys = k_ref.shape[0]
    group = GROUP

    first = pltpu.make_async_copy(q_hbm, q_ref, sems.at[steps])
    first.start()

    def part_copy(step):
        span = pl.ds(step * PART, PART)
        return pltpu.make_async_copy(c_hbm.at[span], c_ref.at[span], sems.at[step])

    others = [(iq_hbm, iq_ref), (k_hbm, k_ref), (w_hbm, w_ref)]
    others = [pltpu.make_async_copy(src, dst, sems.at[steps + 1 + i]) for i, (src, dst) in enumerate(others)]
    for step in range(steps):
        part_copy(step).start()
    for copy in others:
        copy.start()

    tops[...] = jnp.zeros_like(tops)
    sums[...] = jnp.zeros_like(sums)
    first.wait()
    for h in range(heads):
        queries_ref[h * rows : (h + 1) * rows] = q_ref[h].T
    lane = lane_iota(rows)

    def score_step(step, carry):
        part_copy(step).wait()
        for h in range(0, heads, 2):
            queries = queries_ref[h * rows : (h + 2) * rows]
            scores = [dot(queries, c_ref[step * PART + j], NN) for j in range(PART)]
            top = scores[0]
            for score in scores[1:]:
                top = jnp.maximum(top, score)
            top = jnp.max(top, axis=1, keepdims=True)
            total = None
            for j, score in enumerate(scores):
                terms = jnp.exp2((score - top) * SCORE2)
                total = terms if total is None else total + terms
                e_ref[step * PART + j, h : h + 2] = terms.astype(jnp.bfloat16).reshape(2, rows, keys)
            total = jnp.sum(total, axis=1, keepdims=True)
            low, high = lane == h * steps + step, lane == (h + 1) * steps + step
            tops[...] = jnp.where(low, top[0:rows], jnp.where(high, top[rows:], tops[...]))
            sums[...] = jnp.where(low, total[0:rows], jnp.where(high, total[rows:], sums[...]))
        return carry

    lax.fori_loop(0, steps, score_step, 0)

    for copy in others:
        copy.wait()
    total_ref[...] = jnp.zeros_like(total_ref)
    wide[...] = iq_ref[...].astype(jnp.float32).reshape(rows * iheads, depth)
    columns = jnp.concatenate([w_ref[...], jnp.zeros((LANES - iheads, rows), jnp.float32)], axis=0).T

    def logit_step(step, carry):
        weights = pltpu.roll(columns, LANES - group * step, 1)
        for j in range(group):
            head = step * group + j
            qh_ref[head] = wide[pl.ds(head, rows, stride=iheads), :].astype(jnp.bfloat16)
        chunk = qh_ref[pl.ds(step * group, group)].reshape(group * rows, depth)
        products = dot(chunk, k_ref[...], NT)
        total = total_ref[...]
        for j in range(group):
            part = products[j * rows : (j + 1) * rows]
            total = total + jnp.maximum(part, 0.0) * weights[:, j : j + 1]
        total_ref[...] = total
        return carry

    lax.fori_loop(0, iheads // group, logit_step, 0)

    turned_tops = tops[...].T[0 : heads * steps]
    turned_sums = sums[...].T[0 : heads * steps]
    tops_ref[...] = turned_tops
    for k in range(0, keys, rows):
        logits_ref[k : k + rows] = total_ref[:, k : k + rows].T * (1.0 / math.sqrt(depth))
    logits = logits_ref[...]
    ltop = jnp.max(logits, axis=0, keepdims=True)
    lsum = jnp.sum(jnp.exp(logits - ltop), axis=0, keepdims=True)
    flat = []
    for h in range(heads):
        span = slice(h * steps, (h + 1) * steps)
        top = jnp.max(turned_tops[span], axis=0, keepdims=True)
        scaled = turned_sums[span] * jnp.exp2((turned_tops[span] - top) * SCORE2)
        flat.append((top, jnp.sum(scaled, axis=0, keepdims=True)))
    flat = jnp.concatenate([top for top, _ in flat] + [total for _, total in flat], axis=0)
    for z in range(send_ref.shape[0]):
        send_ref[z, 0 : 2 * heads] = flat
        send_ref[z, 2 * heads :] = jnp.zeros((8, rows), jnp.float32)
        send_ref[z, 2 * heads : 2 * heads + 1] = ltop
        send_ref[z, 2 * heads + 1 : 2 * heads + 2] = lsum


def scores_and_logits(queries, cache, index_query, index_keys, weights, key_count):
    heads, width, rows = queries.shape
    blocks, _, keys = cache.shape
    _, iheads, depth = index_query.shape
    steps = blocks // PART
    return call(
        scores_kernel,
        "scores_and_logits",
        32,
        in_specs=[HBM] * 5,
        out_specs=[VMEM] * 5,
        out_shape=(
            bf16(blocks, heads, rows, keys),
            f32(heads * steps, rows),
            f32(key_count, 2 * heads + 8, rows),
            f32(keys, rows),
            bf16(iheads, rows, depth),
        ),
        scratch_shapes=[
            pltpu.VMEM(queries.shape, jnp.bfloat16),
            pltpu.VMEM(cache.shape, jnp.bfloat16),
            pltpu.VMEM(index_query.shape, jnp.bfloat16),
            pltpu.VMEM(index_keys.shape, jnp.bfloat16),
            pltpu.VMEM(weights.shape, jnp.float32),
            pltpu.VMEM((rows * iheads, depth), jnp.float32),
            pltpu.VMEM((rows, keys), jnp.float32),
            pltpu.VMEM((rows * heads, width), jnp.bfloat16),
            pltpu.VMEM((rows, LANES), jnp.float32),
            pltpu.VMEM((rows, LANES), jnp.float32),
            pltpu.SemaphoreType.DMA((steps + 4,)),
        ],
    )(*[in_hbm(x) for x in (queries, cache, index_query, index_keys, weights)])


def headsum_kernel(offsets, e_ref, tops_ref, got_ref, *outs):
    _, heads, rows, keys = e_ref.shape
    steps = tops_ref.shape[0] // heads
    near, _, near_stride, far_stride = position()

    tops = got_ref[:, 0:heads]
    top = jnp.max(tops, axis=0)
    total = jnp.sum(got_ref[:, heads : 2 * heads] * jnp.exp2((tops - top[None]) * SCORE2), axis=0)
    scale = (1.0 / MH) / total
    weights = []
    for h in range(heads):
        local = tops_ref[h * steps : (h + 1) * steps] - top[h : h + 1]
        weights.append(jnp.exp2(jnp.minimum(local * SCORE2, 0.0)) * scale[h : h + 1])
    weights = jnp.concatenate(weights + [jnp.zeros((LANES - heads * steps, rows), jnp.float32)], axis=0).T
    ltops = got_ref[:, 2 * heads : 2 * heads + 1]
    ltop = jnp.max(ltops, axis=0)
    lsum = jnp.sum(got_ref[:, 2 * heads + 1 : 2 * heads + 2] * jnp.exp(ltops - ltop[None]), axis=0)
    tail = jnp.concatenate([ltop, lsum, jnp.zeros((6, rows), jnp.float32)], axis=0)
    tail = jnp.concatenate([tail, jnp.zeros((8, keys - rows), jnp.float32)], axis=1)

    for i, d in enumerate(offsets):

        def body(k, carry):
            block = lax.rem(near + d, RING) * near_stride + k * far_stride
            columns = pltpu.roll(weights, LANES - lax.div(block, PART), 1)
            total = None
            for h in range(heads):
                term = e_ref[block, h].astype(jnp.float32) * columns[:, h * steps : h * steps + 1]
                total = term if total is None else total + term
            outs[i][k, 0:rows] = total
            outs[i][k, rows:] = tail
            return carry

        lax.fori_loop(0, RING, body, 0)


def head_sum(offsets, terms, tops, got):
    blocks, heads, rows, keys = terms.shape
    return call(
        functools.partial(headsum_kernel, offsets),
        "head_sum",
        24,
        in_specs=[VMEM] * 3,
        out_specs=[VMEM] * len(offsets),
        out_shape=[f32(blocks // RING, rows + 8, keys)] * len(offsets),
    )(terms, tops, got)


def merged_stats(tops, sums):
    top = tops[0]
    for other in tops[1:]:
        top = jnp.maximum(top, other)
    total = sums[0] * jnp.exp(tops[0] - top)
    for other, count in zip(tops[1:], sums[1:]):
        total = total + count * jnp.exp(other - top)
    return top, total


def partial_kernel(*refs):
    got, outs = refs[0:RING], refs[RING:]
    rows = outs[0].shape[0] - 8
    _, far, _, _ = position()
    top, total = merged_stats([r[0, rows : rows + 1] for r in got], [r[0, rows + 1 : rows + 2] for r in got])
    for d in range(RING):
        k = lax.rem(far + d, RING)
        outs[d][0:rows] = got[0][k, 0:rows] + got[1][k, 0:rows] + (got[2][k, 0:rows] + got[3][k, 0:rows])
        outs[d][rows:] = jnp.zeros_like(outs[d][rows:])
        outs[d][rows : rows + 1] = top
        outs[d][rows + 1 : rows + 2] = total


def partial_sum(got):
    _, height, keys = got[0].shape
    return call(
        partial_kernel,
        "partial_sum",
        in_specs=[VMEM] * RING,
        out_specs=[VMEM] * RING,
        out_shape=[f32(height, keys)] * RING,
    )(*got)


def dlogits_kernel(key_total, *refs):
    got = refs[0:RING]
    logits_ref, qh_ref, k_ref, send_ref, turned = refs[RING:]
    heads, rows, depth = qh_ref.shape
    keys = k_ref.shape[0]
    root = 1.0 / math.sqrt(depth)

    ltop, lsum = merged_stats(
        [r[rows : rows + 1, 0:rows] for r in got], [r[rows + 1 : rows + 2, 0:rows] for r in got]
    )
    target = got[0][0:rows] + got[1][0:rows] + (got[2][0:rows] + got[3][0:rows])
    soft = jnp.exp(logits_ref[...] - ltop) * (1.0 / lsum)
    for k in range(0, keys, rows):
        turned[k : k + rows] = key_total * (soft[k : k + rows] - target[:, k : k + rows].T)
        send_ref[0:rows, k : k + rows] = turned[k : k + rows].T
        send_ref[rows + heads // 2 :, k : k + rows] = k_ref[k : k + rows].astype(jnp.float32)

    def step(i, first, column):
        sums = []
        for j in range(GROUP):
            products = dot(k_ref[...], qh_ref[i * GROUP + j], NT)
            sums.append(jnp.sum(jnp.maximum(products, 0.0) * turned[...], axis=0, keepdims=True) * root)
        place = pl.ds(pl.multiple_of(rows + first, GROUP), GROUP)
        send_ref[place, column : column + rows] = jnp.concatenate(sums, axis=0)

    half = heads // 2 // GROUP

    def low(i, carry):
        step(i, i * GROUP, 0)
        return carry

    def high(i, carry):
        step(i + half, i * GROUP, rows)
        return carry

    lax.fori_loop(0, half, low, 0)
    lax.fori_loop(0, half, high, 0)


def dlogits_of(got, logits, qh, index_keys, key_total):
    heads, rows, depth = qh.shape
    keys = index_keys.shape[0]
    return call(
        functools.partial(dlogits_kernel, key_total),
        "dlogits",
        24,
        out_shape=f32(2 * rows + heads // 2, keys),
        scratch_shapes=[pltpu.VMEM((keys, rows), jnp.float32)],
    )(*got, logits, qh, index_keys)


def keys_kernel(dlogits_ref, qh_ref, k_ref, w_ref, keys_ref, slopes, turned):
    heads, rows, depth = qh_ref.shape
    root = 1.0 / math.sqrt(depth)
    for k in range(0, k_ref.shape[0], rows):
        turned[k : k + rows] = dlogits_ref[0:rows, k : k + rows].T
    keys_ref[...] = jnp.zeros_like(keys_ref)

    def step(i, carry):
        weights = w_ref[pl.ds(i * GROUP, GROUP)] * root
        for j in range(GROUP):
            products = dot(k_ref[...], qh_ref[i * GROUP + j], NT)
            slope = jnp.where(products > 0.0, turned[...] * weights[j : j + 1], 0.0)
            slopes[:, j * rows : (j + 1) * rows] = slope.astype(jnp.bfloat16)
        chunk = qh_ref[pl.ds(i * GROUP, GROUP)].reshape(GROUP * rows, depth)
        keys_ref[...] += dot(slopes[...], chunk, NN)
        return carry

    lax.fori_loop(0, heads // GROUP, step, 0)


def key_gradient(dlogits, qh, index_keys, weights):
    heads, rows, depth = qh.shape
    keys = index_keys.shape[0]
    return call(
        keys_kernel,
        "key_gradient",
        24,
        out_shape=f32(keys, depth),
        scratch_shapes=[pltpu.VMEM((keys, GROUP * rows), jnp.bfloat16), pltpu.VMEM((keys, rows), jnp.float32)],
    )(dlogits, qh, index_keys, weights)


def query_kernel(offsets, pieces, *refs):
    ring, count = RING, len(offsets)
    got = refs[0:ring]
    qh_ref, w_ref = refs[ring : ring + 2]
    outs = refs[ring + 2 : ring + 2 + count]
    slopes, acc, near, dlogits = refs[ring + 2 + count :]
    heads, rows, depth = qh_ref.shape
    keys = got[0].shape[1]
    share = heads // (ring * ring)
    extra = heads // 2
    root = 1.0 / math.sqrt(depth)
    near_at, far_at, near_stride, far_stride = position()
    span = rows // pieces
    few = extra // pieces

    wsum = got[0][rows : rows + extra]
    for d in range(1, ring):
        wsum = wsum + got[d][rows : rows + extra]
    for d in range(ring):
        for k in range(0, keys, rows):
            near[d * keys + k : d * keys + k + rows] = got[d][rows + extra :, k : k + rows].astype(jnp.bfloat16)
        dlogits[:, d * keys : (d + 1) * keys] = got[d][0:rows] * root
    columns = jnp.concatenate([w_ref[...], jnp.zeros((LANES - heads, rows), jnp.float32)], axis=0).T

    for i, d in enumerate(offsets):
        first = (lax.rem(far_at + d, ring) * far_stride + near_at * near_stride) * share
        weights = pltpu.roll(columns, LANES - first, 1)
        queries = qh_ref[pl.ds(first, share)].reshape(share * rows, depth)
        for k in range(0, ring * keys, keys):
            products = dot(queries, near[k : k + keys], NT)
            for j in range(share):
                part = products[j * rows : (j + 1) * rows]
                slope = jnp.where(part > 0.0, dlogits[:, k : k + keys] * weights[:, j : j + 1], 0.0)
                slopes[j * rows : (j + 1) * rows, k : k + keys] = slope.astype(jnp.bfloat16)
        acc[...] = dot(slopes[...], near[...], NN)
        for z in range(pieces):
            for j in range(share):
                start = j * rows + z * span
                outs[i][z, pl.ds(j, span, stride=share), :] = acc[start : start + span]
            piece = wsum[z * few : (z + 1) * few]
            outs[i][z, share * span : share * span + few] = piece[:, 0:rows]
            outs[i][z, share * span + few :] = piece[:, rows : 2 * rows]


def query_gradient(offsets, got, qh, weights, pieces):
    keys = got[0].shape[1]
    heads, rows, depth = qh.shape
    share = heads // (RING * RING)
    tall = share * (rows // pieces) + heads // pieces
    return call(
        functools.partial(query_kernel, offsets, pieces),
        "query_gradient",
        24,
        in_specs=[VMEM] * (RING + 2),
        out_specs=[VMEM] * len(offsets),
        out_shape=[f32(pieces, tall, depth)] * len(offsets),
        scratch_shapes=[
            pltpu.VMEM((share * rows, RING * keys), jnp.bfloat16),
            pltpu.VMEM((share * rows, depth), jnp.float32),
            pltpu.VMEM((RING * keys, depth), jnp.bfloat16),
            pltpu.VMEM((rows, RING * keys), jnp.float32),
        ],
    )(*got, qh, weights)


def results_kernel(got_ref, query_ref, weight_ref):
    pieces, tall, depth = got_ref.shape
    span = query_ref.shape[1]
    few = (tall - span) // 2
    query_ref[...] = got_ref[:, 0:span]
    for z in range(pieces):
        weight_ref[z * few : (z + 1) * few] = got_ref[z, span : span + few]
        weight_ref[(pieces + z) * few : (pieces + z + 1) * few] = got_ref[z, span + few :]


def results(got, heads, span):
    pieces, _, depth = got.shape
    return call(
        results_kernel,
        "results",
        16,
        out_shape=(f32(pieces, span, depth), f32(heads, depth)),
    )(got)


def exchange(x, axis):
    return lax.all_to_all(x, axis, split_axis=0, concat_axis=0, tiled=True)


def shift(x, d, across):
    pairs = []
    for a in range(RING):
        for b in range(RING):
            for row in range(2):
                if (row == 1) != across:
                    there = (a + d) % RING * RING + b
                else:
                    there = a * RING + (b + d) % RING
                pairs.append(((a * RING + b) * 2 + row, there * 2 + row))
    return lax.ppermute(x, ("head", "row"), pairs)


def shards(mla_query, mla_cache, index_query, index_keys, index_weight):
    key_count = lax.axis_size("key")
    head_count = lax.axis_size("head")
    rows = mla_query.shape[0]
    keys, depth = index_keys.shape
    heads = index_query.shape[1]
    share = heads // head_count
    row_index = lax.axis_index("row")
    weights = index_weight.T
    queries = jnp.transpose(mla_query, (1, 2, 0))
    cache = jnp.swapaxes(mla_cache, 1, 2)
    terms, tops, send1, logits, qh = scores_and_logits(queries, cache, index_query, index_keys, weights, key_count)
    got1 = exchange(send1, "key")
    (far_two,) = head_sum((2,), terms, tops, got1)
    got1, _ = lax.optimization_barrier((got1, far_two))
    sides = head_sum((1, 3), terms, tops, got1)
    (own,) = head_sum((0,), terms, tops, got1)
    two = shift(far_two, 2, False)
    one = shift(sides[0], 1, False)
    three = shift(sides[1], 3, False)
    got2 = [own, one, two, three]
    send2 = partial_sum(got2)
    got2 = [send2[0]] + [shift(send2[d], d, True) for d in (1, 2, 3)]
    key_total = float(keys * head_count * key_count)
    send3 = dlogits_of(got2, logits, qh, index_keys, key_total)
    got3 = [send3] + [shift(send3, d, False) for d in range(1, RING)]
    keys_part = key_gradient(send3, qh, index_keys, weights)
    got3, keys_part = lax.optimization_barrier((got3, keys_part))

    half = keys // 2
    away = lax.dynamic_slice_in_dim(keys_part, (1 - row_index) * half, half, 0)
    near = lax.dynamic_slice_in_dim(keys_part, row_index * half, half, 0)
    key_grad = near + lax.ppermute(away, "row", [(0, 1), (1, 0)])

    (far_two,) = query_gradient((2,), got3, qh, weights, key_count)
    got3, _ = lax.optimization_barrier((got3, far_two))
    sides = query_gradient((1, 3), got3, qh, weights, key_count)
    (own,) = query_gradient((0,), got3, qh, weights, key_count)
    two = shift(far_two, 2, True)
    one = shift(sides[0], 1, True)
    three = shift(sides[1], 3, True)
    send4 = own + one + (two + three)
    got4 = jnp.sum(exchange(send4, "key"), axis=0)
    got5 = exchange(jnp.broadcast_to(got4[None], (key_count, *got4.shape)), "key")
    query_grad, weight_grad = results(got5, heads, share * (rows // key_count))
    return (query_grad.reshape(rows, share, depth), key_grad, weight_grad.T)


def solution(mesh):
    placed = (
        P("row", "head", None),
        P(None, "key", None),
        P("row", None, None),
        P(("head", "key"), None),
        P("row", None),
    )
    return jax.shard_map(
        shards,
        mesh=mesh,
        in_specs=placed,
        out_specs=(P("row", "head", None), P(("head", "key", "row"), None), P("row", None)),
        check_vma=False,
    )
```

```python
import functools
import math

import jax
import jax.numpy as jnp
from jax import lax
from jax.experimental import pallas as pl
from jax.experimental.pallas import tpu as pltpu
from jax.sharding import PartitionSpec as P

MH = 128
LOG2E = 1.4426950408889634
SCORE2 = LOG2E / math.sqrt(192.0)
LANES = 128
NT = (((1,), (1,)), ((), ()))
TN = (((0,), (0,)), ((), ()))
NN = (((1,), (0,)), ((), ()))


def dot(a, b, dims):
    return lax.dot_general(a, b, dims, preferred_element_type=jnp.float32)


def lane_iota(rows):
    return lax.broadcasted_iota(jnp.int32, (rows, LANES), 1)


RING = 4
PART = 4
GROUP = 8
VMEM = pl.BlockSpec(memory_space=pltpu.VMEM)
HBM = pl.BlockSpec(memory_space=pltpu.HBM)


def call(kernel, name, megabytes=32, **options):
    return pl.pallas_call(
        kernel,
        name=name,
        compiler_params=pltpu.CompilerParams(vmem_limit_bytes=megabytes << 20),
        **options,
    )


def in_hbm(x):
    return pltpu.with_memory_space_constraint(x, pltpu.HBM)


def f32(*shape):
    return jax.ShapeDtypeStruct(shape, jnp.float32)


def bf16(*shape):
    return jax.ShapeDtypeStruct(shape, jnp.bfloat16)


def position():
    head, first = lax.axis_index("head"), lax.axis_index("row") == 0
    x, y = lax.div(head, RING), lax.rem(head, RING)
    return jnp.where(first, y, x), jnp.where(first, x, y), jnp.where(first, 1, RING), jnp.where(first, RING, 1)


def scores_kernel(
    q_hbm, c_hbm, iq_hbm, k_hbm, w_hbm,
    e_ref, tops_ref, send_ref, logits_ref, qh_ref,
    q_ref, c_ref, iq_ref, k_ref, w_ref, wide, total_ref, queries_ref, tops, sums, sems,
):
    heads, width, rows = q_ref.shape
    blocks = c_ref.shape[0]
    steps = blocks // PART
    _, iheads, depth = iq_ref.shape
    keys = k_ref.shape[0]
    group = GROUP

    first = pltpu.make_async_copy(q_hbm, q_ref, sems.at[steps])
    first.start()

    def part_copy(step):
        span = pl.ds(step * PART, PART)
        return pltpu.make_async_copy(c_hbm.at[span], c_ref.at[span], sems.at[step])

    others = [(iq_hbm, iq_ref), (k_hbm, k_ref), (w_hbm, w_ref)]
    others = [pltpu.make_async_copy(src, dst, sems.at[steps + 1 + i]) for i, (src, dst) in enumerate(others)]
    for step in range(steps):
        part_copy(step).start()
    for copy in others:
        copy.start()

    tops[...] = jnp.zeros_like(tops)
    sums[...] = jnp.zeros_like(sums)
    first.wait()
    for h in range(heads):
        queries_ref[h * rows : (h + 1) * rows] = q_ref[h].T
    lane = lane_iota(rows)

    def score_step(step, carry):
        part_copy(step).wait()
        for h in range(0, heads, 2):
            queries = queries_ref[h * rows : (h + 2) * rows]
            scores = [dot(queries, c_ref[step * PART + j], NN) for j in range(PART)]
            top = scores[0]
            for score in scores[1:]:
                top = jnp.maximum(top, score)
            top = jnp.max(top, axis=1, keepdims=True)
            total = None
            for j, score in enumerate(scores):
                terms = jnp.exp2((score - top) * SCORE2)
                total = terms if total is None else total + terms
                e_ref[step * PART + j, h : h + 2] = terms.astype(jnp.bfloat16).reshape(2, rows, keys)
            total = jnp.sum(total, axis=1, keepdims=True)
            low, high = lane == h * steps + step, lane == (h + 1) * steps + step
            tops[...] = jnp.where(low, top[0:rows], jnp.where(high, top[rows:], tops[...]))
            sums[...] = jnp.where(low, total[0:rows], jnp.where(high, total[rows:], sums[...]))
        return carry

    lax.fori_loop(0, steps, score_step, 0)

    for copy in others:
        copy.wait()
    total_ref[...] = jnp.zeros_like(total_ref)
    wide[...] = iq_ref[...].astype(jnp.float32).reshape(rows * iheads, depth)
    columns = jnp.concatenate([w_ref[...], jnp.zeros((LANES - iheads, rows), jnp.float32)], axis=0).T

    def logit_step(step, carry):
        weights = pltpu.roll(columns, LANES - group * step, 1)
        for j in range(group):
            head = step * group + j
            qh_ref[head] = wide[pl.ds(head, rows, stride=iheads), :].astype(jnp.bfloat16)
        chunk = qh_ref[pl.ds(step * group, group)].reshape(group * rows, depth)
        products = dot(chunk, k_ref[...], NT)
        total = total_ref[...]
        for j in range(group):
            part = products[j * rows : (j + 1) * rows]
            total = total + jnp.maximum(part, 0.0) * weights[:, j : j + 1]
        total_ref[...] = total
        return carry

    lax.fori_loop(0, iheads // group, logit_step, 0)

    turned_tops = tops[...].T[0 : heads * steps]
    turned_sums = sums[...].T[0 : heads * steps]
    tops_ref[...] = turned_tops
    for k in range(0, keys, rows):
        logits_ref[k : k + rows] = total_ref[:, k : k + rows].T * (1.0 / math.sqrt(depth))
    logits = logits_ref[...]
    ltop = jnp.max(logits, axis=0, keepdims=True)
    lsum = jnp.sum(jnp.exp(logits - ltop), axis=0, keepdims=True)
    flat = []
    for h in range(heads):
        span = slice(h * steps, (h + 1) * steps)
        top = jnp.max(turned_tops[span], axis=0, keepdims=True)
        scaled = turned_sums[span] * jnp.exp2((turned_tops[span] - top) * SCORE2)
        flat.append((top, jnp.sum(scaled, axis=0, keepdims=True)))
    flat = jnp.concatenate([top for top, _ in flat] + [total for _, total in flat], axis=0)
    for z in range(send_ref.shape[0]):
        send_ref[z, 0 : 2 * heads] = flat
        send_ref[z, 2 * heads :] = jnp.zeros((8, rows), jnp.float32)
        send_ref[z, 2 * heads : 2 * heads + 1] = ltop
        send_ref[z, 2 * heads + 1 : 2 * heads + 2] = lsum


def scores_and_logits(queries, cache, index_query, index_keys, weights, key_count):
    heads, width, rows = queries.shape
    blocks, _, keys = cache.shape
    _, iheads, depth = index_query.shape
    steps = blocks // PART
    return call(
        scores_kernel,
        "scores_and_logits",
        32,
        in_specs=[HBM] * 5,
        out_specs=[VMEM] * 5,
        out_shape=(
            bf16(blocks, heads, rows, keys),
            f32(heads * steps, rows),
            f32(key_count, 2 * heads + 8, rows),
            f32(keys, rows),
            bf16(iheads, rows, depth),
        ),
        scratch_shapes=[
            pltpu.VMEM(queries.shape, jnp.bfloat16),
            pltpu.VMEM(cache.shape, jnp.bfloat16),
            pltpu.VMEM(index_query.shape, jnp.bfloat16),
            pltpu.VMEM(index_keys.shape, jnp.bfloat16),
            pltpu.VMEM(weights.shape, jnp.float32),
            pltpu.VMEM((rows * iheads, depth), jnp.float32),
            pltpu.VMEM((rows, keys), jnp.float32),
            pltpu.VMEM((rows * heads, width), jnp.bfloat16),
            pltpu.VMEM((rows, LANES), jnp.float32),
            pltpu.VMEM((rows, LANES), jnp.float32),
            pltpu.SemaphoreType.DMA((steps + 4,)),
        ],
    )(*[in_hbm(x) for x in (queries, cache, index_query, index_keys, weights)])


def headsum_kernel(offsets, e_ref, tops_ref, got_ref, *outs):
    _, heads, rows, keys = e_ref.shape
    steps = tops_ref.shape[0] // heads
    near, _, near_stride, far_stride = position()

    tops = got_ref[:, 0:heads]
    top = jnp.max(tops, axis=0)
    total = jnp.sum(got_ref[:, heads : 2 * heads] * jnp.exp2((tops - top[None]) * SCORE2), axis=0)
    scale = (1.0 / MH) / total
    weights = []
    for h in range(heads):
        local = tops_ref[h * steps : (h + 1) * steps] - top[h : h + 1]
        weights.append(jnp.exp2(jnp.minimum(local * SCORE2, 0.0)) * scale[h : h + 1])
    weights = jnp.concatenate(weights + [jnp.zeros((LANES - heads * steps, rows), jnp.float32)], axis=0).T
    ltops = got_ref[:, 2 * heads : 2 * heads + 1]
    ltop = jnp.max(ltops, axis=0)
    lsum = jnp.sum(got_ref[:, 2 * heads + 1 : 2 * heads + 2] * jnp.exp(ltops - ltop[None]), axis=0)
    tail = jnp.concatenate([ltop, lsum, jnp.zeros((6, rows), jnp.float32)], axis=0)
    tail = jnp.concatenate([tail, jnp.zeros((8, keys - rows), jnp.float32)], axis=1)

    for i, d in enumerate(offsets):

        def body(k, carry):
            block = lax.rem(near + d, RING) * near_stride + k * far_stride
            columns = pltpu.roll(weights, LANES - lax.div(block, PART), 1)
            total = None
            for h in range(heads):
                term = e_ref[block, h].astype(jnp.float32) * columns[:, h * steps : h * steps + 1]
                total = term if total is None else total + term
            outs[i][k, 0:rows] = total
            outs[i][k, rows:] = tail
            return carry

        lax.fori_loop(0, RING, body, 0)


def head_sum(offsets, terms, tops, got):
    blocks, heads, rows, keys = terms.shape
    return call(
        functools.partial(headsum_kernel, offsets),
        "head_sum",
        24,
        in_specs=[VMEM] * 3,
        out_specs=[VMEM] * len(offsets),
        out_shape=[f32(blocks // RING, rows + 8, keys)] * len(offsets),
    )(terms, tops, got)


def merged_stats(tops, sums):
    top = tops[0]
    for other in tops[1:]:
        top = jnp.maximum(top, other)
    total = sums[0] * jnp.exp(tops[0] - top)
    for other, count in zip(tops[1:], sums[1:]):
        total = total + count * jnp.exp(other - top)
    return top, total


def partial_kernel(*refs):
    got, outs = refs[0:RING], refs[RING:]
    rows = outs[0].shape[0] - 8
    _, far, _, _ = position()
    top, total = merged_stats([r[0, rows : rows + 1] for r in got], [r[0, rows + 1 : rows + 2] for r in got])
    for d in range(RING):
        k = lax.rem(far + d, RING)
        outs[d][0:rows] = got[0][k, 0:rows] + got[1][k, 0:rows] + (got[2][k, 0:rows] + got[3][k, 0:rows])
        outs[d][rows:] = jnp.zeros_like(outs[d][rows:])
        outs[d][rows : rows + 1] = top
        outs[d][rows + 1 : rows + 2] = total


def partial_sum(got):
    _, height, keys = got[0].shape
    return call(
        partial_kernel,
        "partial_sum",
        in_specs=[VMEM] * RING,
        out_specs=[VMEM] * RING,
        out_shape=[f32(height, keys)] * RING,
    )(*got)


def active_kernel(qh_ref, k_ref, active_ref):
    heads, rows, _ = qh_ref.shape

    def step(i, carry):
        for j in range(GROUP):
            active_ref[i * GROUP + j] = jnp.maximum(dot(k_ref[...], qh_ref[i * GROUP + j], NT), 0.0)
        return carry

    lax.fori_loop(0, heads // GROUP, step, 0)


def active_products(qh, index_keys):
    heads, rows, _ = qh.shape
    return call(active_kernel, "active_products", 24, out_shape=f32(heads, index_keys.shape[0], rows))(qh, index_keys)


def dlogits_kernel(key_total, *refs):
    got = refs[0:RING]
    logits_ref, active_ref, k_ref, send_ref, turned = refs[RING:]
    heads, _, rows = active_ref.shape
    depth = k_ref.shape[1]
    keys = k_ref.shape[0]
    root = 1.0 / math.sqrt(depth)

    ltop, lsum = merged_stats(
        [r[rows : rows + 1, 0:rows] for r in got], [r[rows + 1 : rows + 2, 0:rows] for r in got]
    )
    target = got[0][0:rows] + got[1][0:rows] + (got[2][0:rows] + got[3][0:rows])
    soft = jnp.exp(logits_ref[...] - ltop) * (1.0 / lsum)
    for k in range(0, keys, rows):
        turned[k : k + rows] = key_total * (soft[k : k + rows] - target[:, k : k + rows].T)
        send_ref[0:rows, k : k + rows] = turned[k : k + rows].T
        send_ref[rows + heads // 2 :, k : k + rows] = k_ref[k : k + rows].astype(jnp.float32)

    def step(i, first, column):
        sums = []
        for j in range(GROUP):
            sums.append(jnp.sum(active_ref[i * GROUP + j] * turned[...], axis=0, keepdims=True) * root)
        place = pl.ds(pl.multiple_of(rows + first, GROUP), GROUP)
        send_ref[place, column : column + rows] = jnp.concatenate(sums, axis=0)

    half = heads // 2 // GROUP

    def low(i, carry):
        step(i, i * GROUP, 0)
        return carry

    def high(i, carry):
        step(i + half, i * GROUP, rows)
        return carry

    lax.fori_loop(0, half, low, 0)
    lax.fori_loop(0, half, high, 0)


def dlogits_of(got, logits, active, index_keys, key_total):
    heads, keys, rows = active.shape
    return call(
        functools.partial(dlogits_kernel, key_total),
        "dlogits",
        24,
        out_shape=f32(2 * rows + heads // 2, keys),
        scratch_shapes=[pltpu.VMEM((keys, rows), jnp.float32)],
    )(*got, logits, active, index_keys)


def keys_kernel(dlogits_ref, active_ref, qh_ref, w_ref, keys_ref, slopes, turned):
    heads, rows, depth = qh_ref.shape
    root = 1.0 / math.sqrt(depth)
    for k in range(0, turned.shape[0], rows):
        turned[k : k + rows] = dlogits_ref[0:rows, k : k + rows].T
    keys_ref[...] = jnp.zeros_like(keys_ref)

    def step(i, carry):
        weights = w_ref[pl.ds(i * GROUP, GROUP)] * root
        for j in range(GROUP):
            slope = jnp.where(active_ref[i * GROUP + j] > 0.0, turned[...] * weights[j : j + 1], 0.0)
            slopes[:, j * rows : (j + 1) * rows] = slope.astype(jnp.bfloat16)
        chunk = qh_ref[pl.ds(i * GROUP, GROUP)].reshape(GROUP * rows, depth)
        keys_ref[...] += dot(slopes[...], chunk, NN)
        return carry

    lax.fori_loop(0, heads // GROUP, step, 0)


def key_gradient(dlogits, active, qh, weights):
    heads, rows, depth = qh.shape
    keys = active.shape[1]
    return call(
        keys_kernel,
        "key_gradient",
        24,
        out_shape=f32(keys, depth),
        scratch_shapes=[pltpu.VMEM((keys, GROUP * rows), jnp.bfloat16), pltpu.VMEM((keys, rows), jnp.float32)],
    )(dlogits, active, qh, weights)


def query_kernel(offsets, pieces, *refs):
    ring, count = RING, len(offsets)
    got = refs[0:ring]
    qh_ref, w_ref = refs[ring : ring + 2]
    outs = refs[ring + 2 : ring + 2 + count]
    slopes, acc, near, dlogits = refs[ring + 2 + count :]
    heads, rows, depth = qh_ref.shape
    keys = got[0].shape[1]
    share = heads // (ring * ring)
    extra = heads // 2
    root = 1.0 / math.sqrt(depth)
    near_at, far_at, near_stride, far_stride = position()
    span = rows // pieces
    few = extra // pieces

    wsum = got[0][rows : rows + extra]
    for d in range(1, ring):
        wsum = wsum + got[d][rows : rows + extra]
    for d in range(ring):
        for k in range(0, keys, rows):
            near[d * keys + k : d * keys + k + rows] = got[d][rows + extra :, k : k + rows].astype(jnp.bfloat16)
        dlogits[:, d * keys : (d + 1) * keys] = got[d][0:rows] * root
    columns = jnp.concatenate([w_ref[...], jnp.zeros((LANES - heads, rows), jnp.float32)], axis=0).T

    for i, d in enumerate(offsets):
        first = (lax.rem(far_at + d, ring) * far_stride + near_at * near_stride) * share
        weights = pltpu.roll(columns, LANES - first, 1)
        queries = qh_ref[pl.ds(first, share)].reshape(share * rows, depth)
        for k in range(0, ring * keys, keys):
            products = dot(queries, near[k : k + keys], NT)
            for j in range(share):
                part = products[j * rows : (j + 1) * rows]
                slope = jnp.where(part > 0.0, dlogits[:, k : k + keys] * weights[:, j : j + 1], 0.0)
                slopes[j * rows : (j + 1) * rows, k : k + keys] = slope.astype(jnp.bfloat16)
        acc[...] = dot(slopes[...], near[...], NN)
        for z in range(pieces):
            for j in range(share):
                start = j * rows + z * span
                outs[i][z, pl.ds(j, span, stride=share), :] = acc[start : start + span]
            piece = wsum[z * few : (z + 1) * few]
            outs[i][z, share * span : share * span + few] = piece[:, 0:rows]
            outs[i][z, share * span + few :] = piece[:, rows : 2 * rows]


def query_gradient(offsets, got, qh, weights, pieces):
    keys = got[0].shape[1]
    heads, rows, depth = qh.shape
    share = heads // (RING * RING)
    tall = share * (rows // pieces) + heads // pieces
    return call(
        functools.partial(query_kernel, offsets, pieces),
        "query_gradient",
        24,
        in_specs=[VMEM] * (RING + 2),
        out_specs=[VMEM] * len(offsets),
        out_shape=[f32(pieces, tall, depth)] * len(offsets),
        scratch_shapes=[
            pltpu.VMEM((share * rows, RING * keys), jnp.bfloat16),
            pltpu.VMEM((share * rows, depth), jnp.float32),
            pltpu.VMEM((RING * keys, depth), jnp.bfloat16),
            pltpu.VMEM((rows, RING * keys), jnp.float32),
        ],
    )(*got, qh, weights)


def results_kernel(got_ref, query_ref, weight_ref):
    pieces, tall, depth = got_ref.shape
    span = query_ref.shape[1]
    few = (tall - span) // 2
    query_ref[...] = got_ref[:, 0:span]
    for z in range(pieces):
        weight_ref[z * few : (z + 1) * few] = got_ref[z, span : span + few]
        weight_ref[(pieces + z) * few : (pieces + z + 1) * few] = got_ref[z, span + few :]


def results(got, heads, span):
    pieces, _, depth = got.shape
    return call(
        results_kernel,
        "results",
        16,
        out_shape=(f32(pieces, span, depth), f32(heads, depth)),
    )(got)


def exchange(x, axis):
    return lax.all_to_all(x, axis, split_axis=0, concat_axis=0, tiled=True)


def shift(x, d, across):
    pairs = []
    for a in range(RING):
        for b in range(RING):
            for row in range(2):
                if (row == 1) != across:
                    there = (a + d) % RING * RING + b
                else:
                    there = a * RING + (b + d) % RING
                pairs.append(((a * RING + b) * 2 + row, there * 2 + row))
    return lax.ppermute(x, ("head", "row"), pairs)


def shards(mla_query, mla_cache, index_query, index_keys, index_weight):
    key_count = lax.axis_size("key")
    head_count = lax.axis_size("head")
    rows = mla_query.shape[0]
    keys, depth = index_keys.shape
    heads = index_query.shape[1]
    share = heads // head_count
    row_index = lax.axis_index("row")
    weights = index_weight.T
    queries = jnp.transpose(mla_query, (1, 2, 0))
    cache = jnp.swapaxes(mla_cache, 1, 2)
    terms, tops, send1, logits, qh = scores_and_logits(queries, cache, index_query, index_keys, weights, key_count)
    got1 = exchange(send1, "key")
    (far_two,) = head_sum((2,), terms, tops, got1)
    got1, _ = lax.optimization_barrier((got1, far_two))
    sides = head_sum((1, 3), terms, tops, got1)
    (own,) = head_sum((0,), terms, tops, got1)
    two = shift(far_two, 2, False)
    one = shift(sides[0], 1, False)
    three = shift(sides[1], 3, False)
    own, late = lax.optimization_barrier((own, qh))
    active = active_products(late, index_keys)
    got2, active = lax.optimization_barrier(([own, one, two, three], active))
    send2 = partial_sum(got2)
    got2 = [send2[0]] + [shift(send2[d], d, True) for d in (1, 2, 3)]
    key_total = float(keys * head_count * key_count)
    send3 = dlogits_of(got2, logits, active, index_keys, key_total)
    got3 = [send3] + [shift(send3, d, False) for d in range(1, RING)]

    (far_two,) = query_gradient((2,), got3, qh, weights, key_count)
    got3, active, _ = lax.optimization_barrier((got3, active, far_two))
    sides = query_gradient((1, 3), got3, qh, weights, key_count)
    (own,) = query_gradient((0,), got3, qh, weights, key_count)
    two = shift(far_two, 2, True)
    one = shift(sides[0], 1, True)
    three = shift(sides[1], 3, True)
    active, _ = lax.optimization_barrier((active, own))
    keys_part = key_gradient(send3, active, qh, weights)
    two, keys_part = lax.optimization_barrier((two, keys_part))
    send4 = own + one + (two + three)

    half = keys // 2
    away = lax.dynamic_slice_in_dim(keys_part, (1 - row_index) * half, half, 0)
    near = lax.dynamic_slice_in_dim(keys_part, row_index * half, half, 0)
    key_grad = near + lax.ppermute(away, "row", [(0, 1), (1, 0)])

    got4 = jnp.sum(exchange(send4, "key"), axis=0)
    got5 = exchange(jnp.broadcast_to(got4[None], (key_count, *got4.shape)), "key")
    query_grad, weight_grad = results(got5, heads, share * (rows // key_count))
    return (query_grad.reshape(rows, share, depth), key_grad, weight_grad.T)


def solution(mesh):
    placed = (
        P("row", "head", None),
        P(None, "key", None),
        P("row", None, None),
        P(("head", "key"), None),
        P("row", None),
    )
    return jax.shard_map(
        shards,
        mesh=mesh,
        in_specs=placed,
        out_specs=(P("row", "head", None), P(("head", "key", "row"), None), P("row", None)),
        check_vma=False,
    )
```

```python
import functools
import math

import jax
import jax.numpy as jnp
from jax import lax
from jax.experimental import pallas as pl
from jax.experimental.pallas import tpu as pltpu
from jax.sharding import PartitionSpec as P

MH = 128
LOG2E = 1.4426950408889634
SCORE2 = LOG2E / math.sqrt(192.0)
LANES = 128
NT = (((1,), (1,)), ((), ()))
TN = (((0,), (0,)), ((), ()))
NN = (((1,), (0,)), ((), ()))


def dot(a, b, dims):
    return lax.dot_general(a, b, dims, preferred_element_type=jnp.float32)


def lane_iota(rows):
    return lax.broadcasted_iota(jnp.int32, (rows, LANES), 1)


RING = 4
PART = 4
GROUP = 8
VMEM = pl.BlockSpec(memory_space=pltpu.VMEM)
HBM = pl.BlockSpec(memory_space=pltpu.HBM)


def call(kernel, name, megabytes=32, **options):
    return pl.pallas_call(
        kernel,
        name=name,
        compiler_params=pltpu.CompilerParams(vmem_limit_bytes=megabytes << 20),
        **options,
    )


def in_hbm(x):
    return pltpu.with_memory_space_constraint(x, pltpu.HBM)


def f32(*shape):
    return jax.ShapeDtypeStruct(shape, jnp.float32)


def bf16(*shape):
    return jax.ShapeDtypeStruct(shape, jnp.bfloat16)


def position():
    head, first = lax.axis_index("head"), lax.axis_index("row") == 0
    x, y = lax.div(head, RING), lax.rem(head, RING)
    return jnp.where(first, y, x), jnp.where(first, x, y), jnp.where(first, 1, RING), jnp.where(first, RING, 1)


def scores_kernel(
    q_hbm, c_hbm, iq_hbm, k_hbm, w_hbm,
    e_ref, tops_ref, send_ref, logits_ref, qh_ref,
    q_ref, c_ref, iq_ref, k_ref, w_ref, wide, total_ref, queries_ref, tops, sums, sems,
):
    heads, width, rows = q_ref.shape
    blocks = c_ref.shape[0]
    steps = blocks // PART
    _, iheads, depth = iq_ref.shape
    keys = k_ref.shape[0]
    group = GROUP
    pitch = wide.shape[0] // rows

    first = pltpu.make_async_copy(q_hbm, q_ref, sems.at[steps])
    first.start()

    def part_copy(step):
        span = pl.ds(step * PART, PART)
        return pltpu.make_async_copy(c_hbm.at[span], c_ref.at[span], sems.at[step])

    others = [(iq_hbm, iq_ref), (k_hbm, k_ref), (w_hbm, w_ref)]
    others = [pltpu.make_async_copy(src, dst, sems.at[steps + 1 + i]) for i, (src, dst) in enumerate(others)]
    for step in range(steps):
        part_copy(step).start()
    for copy in others:
        copy.start()

    tops[...] = jnp.zeros_like(tops)
    sums[...] = jnp.zeros_like(sums)
    first.wait()
    for h in range(heads):
        queries_ref[h * rows : (h + 1) * rows] = q_ref[h].T
    lane = lane_iota(rows)

    def score_step(step, carry):
        part_copy(step).wait()
        for h in range(0, heads, 2):
            queries = queries_ref[h * rows : (h + 2) * rows]
            scores = [dot(queries, c_ref[step * PART + j], NN) for j in range(PART)]
            top = scores[0]
            for score in scores[1:]:
                top = jnp.maximum(top, score)
            top = jnp.max(top, axis=1, keepdims=True)
            total = None
            for j, score in enumerate(scores):
                terms = jnp.exp2((score - top) * SCORE2)
                total = terms if total is None else total + terms
                e_ref[step * PART + j, h : h + 2] = terms.astype(jnp.bfloat16).reshape(2, rows, keys)
            total = jnp.sum(total, axis=1, keepdims=True)
            low, high = lane == h * steps + step, lane == (h + 1) * steps + step
            tops[...] = jnp.where(low, top[0:rows], jnp.where(high, top[rows:], tops[...]))
            sums[...] = jnp.where(low, total[0:rows], jnp.where(high, total[rows:], sums[...]))
        return carry

    lax.fori_loop(0, steps, score_step, 0)

    for copy in others:
        copy.wait()
    total_ref[...] = jnp.zeros_like(total_ref)
    for t in range(rows):
        wide[t * pitch : t * pitch + iheads] = iq_ref[t].astype(jnp.float32)
    columns = jnp.concatenate([w_ref[...], jnp.zeros((LANES - iheads, rows), jnp.float32)], axis=0).T

    def logit_step(step, carry):
        weights = pltpu.roll(columns, LANES - group * step, 1)
        for j in range(group):
            head = step * group + j
            qh_ref[head] = wide[pl.ds(head, rows, stride=pitch), :].astype(jnp.bfloat16)
        chunk = qh_ref[pl.ds(step * group, group)].reshape(group * rows, depth)
        products = dot(chunk, k_ref[...], NT)
        total = total_ref[...]
        for j in range(group):
            part = products[j * rows : (j + 1) * rows]
            total = total + jnp.maximum(part, 0.0) * weights[:, j : j + 1]
        total_ref[...] = total
        return carry

    lax.fori_loop(0, iheads // group, logit_step, 0)

    turned_tops = tops[...].T[0 : heads * steps]
    turned_sums = sums[...].T[0 : heads * steps]
    tops_ref[...] = turned_tops
    for k in range(0, keys, rows):
        logits_ref[k : k + rows] = total_ref[:, k : k + rows].T * (1.0 / math.sqrt(depth))
    logits = logits_ref[...]
    ltop = jnp.max(logits, axis=0, keepdims=True)
    lsum = jnp.sum(jnp.exp(logits - ltop), axis=0, keepdims=True)
    flat = []
    for h in range(heads):
        span = slice(h * steps, (h + 1) * steps)
        top = jnp.max(turned_tops[span], axis=0, keepdims=True)
        scaled = turned_sums[span] * jnp.exp2((turned_tops[span] - top) * SCORE2)
        flat.append((top, jnp.sum(scaled, axis=0, keepdims=True)))
    flat = jnp.concatenate([top for top, _ in flat] + [total for _, total in flat], axis=0)
    for z in range(send_ref.shape[0]):
        send_ref[z, 0 : 2 * heads] = flat
        send_ref[z, 2 * heads :] = jnp.zeros((8, rows), jnp.float32)
        send_ref[z, 2 * heads : 2 * heads + 1] = ltop
        send_ref[z, 2 * heads + 1 : 2 * heads + 2] = lsum


def scores_and_logits(queries, cache, index_query, index_keys, weights, key_count):
    heads, width, rows = queries.shape
    blocks, _, keys = cache.shape
    _, iheads, depth = index_query.shape
    steps = blocks // PART
    return call(
        scores_kernel,
        "scores_and_logits",
        32,
        in_specs=[HBM] * 5,
        out_specs=[VMEM] * 5,
        out_shape=(
            bf16(blocks, heads, rows, keys),
            f32(heads * steps, rows),
            f32(key_count, 2 * heads + 8, rows),
            f32(keys, rows),
            bf16(iheads, rows, depth),
        ),
        scratch_shapes=[
            pltpu.VMEM(queries.shape, jnp.bfloat16),
            pltpu.VMEM(cache.shape, jnp.bfloat16),
            pltpu.VMEM(index_query.shape, jnp.bfloat16),
            pltpu.VMEM(index_keys.shape, jnp.bfloat16),
            pltpu.VMEM(weights.shape, jnp.float32),
            pltpu.VMEM((rows * (iheads + 8), depth), jnp.float32),
            pltpu.VMEM((rows, keys), jnp.float32),
            pltpu.VMEM((rows * heads, width), jnp.bfloat16),
            pltpu.VMEM((rows, LANES), jnp.float32),
            pltpu.VMEM((rows, LANES), jnp.float32),
            pltpu.SemaphoreType.DMA((steps + 4,)),
        ],
    )(*[in_hbm(x) for x in (queries, cache, index_query, index_keys, weights)])


def headsum_kernel(offsets, e_ref, tops_ref, got_ref, *outs):
    _, heads, rows, keys = e_ref.shape
    steps = tops_ref.shape[0] // heads
    near, _, near_stride, far_stride = position()

    tops = got_ref[:, 0:heads]
    top = jnp.max(tops, axis=0)
    total = jnp.sum(got_ref[:, heads : 2 * heads] * jnp.exp2((tops - top[None]) * SCORE2), axis=0)
    scale = (1.0 / MH) / total
    weights = []
    for h in range(heads):
        local = tops_ref[h * steps : (h + 1) * steps] - top[h : h + 1]
        weights.append(jnp.exp2(jnp.minimum(local * SCORE2, 0.0)) * scale[h : h + 1])
    weights = jnp.concatenate(weights + [jnp.zeros((LANES - heads * steps, rows), jnp.float32)], axis=0).T
    ltops = got_ref[:, 2 * heads : 2 * heads + 1]
    ltop = jnp.max(ltops, axis=0)
    lsum = jnp.sum(got_ref[:, 2 * heads + 1 : 2 * heads + 2] * jnp.exp(ltops - ltop[None]), axis=0)
    tail = jnp.concatenate([ltop, lsum, jnp.zeros((6, rows), jnp.float32)], axis=0)
    tail = jnp.concatenate([tail, jnp.zeros((8, keys - rows), jnp.float32)], axis=1)

    for i, d in enumerate(offsets):

        def body(k, carry):
            block = lax.rem(near + d, RING) * near_stride + k * far_stride
            columns = pltpu.roll(weights, LANES - lax.div(block, PART), 1)
            total = None
            for h in range(heads):
                term = e_ref[block, h].astype(jnp.float32) * columns[:, h * steps : h * steps + 1]
                total = term if total is None else total + term
            outs[i][pl.ds(pl.multiple_of(k * rows, rows), rows)] = total
            return carry

        lax.fori_loop(0, RING, body, 0)
        outs[i][RING * rows :] = tail


def head_sum(offsets, terms, tops, got):
    blocks, heads, rows, keys = terms.shape
    return call(
        functools.partial(headsum_kernel, offsets),
        "head_sum",
        24,
        in_specs=[VMEM] * 3,
        out_specs=[VMEM] * len(offsets),
        out_shape=[f32(blocks // RING * rows + 8, keys)] * len(offsets),
    )(terms, tops, got)


def merged_stats(tops, sums):
    top = tops[0]
    for other in tops[1:]:
        top = jnp.maximum(top, other)
    total = sums[0] * jnp.exp(tops[0] - top)
    for other, count in zip(tops[1:], sums[1:]):
        total = total + count * jnp.exp(other - top)
    return top, total


def partial_kernel(*refs):
    got, outs = refs[0:RING], refs[RING:]
    rows = outs[0].shape[0] - 8
    _, far, _, _ = position()
    last = RING * rows
    top, total = merged_stats([r[last : last + 1] for r in got], [r[last + 1 : last + 2] for r in got])
    for d in range(RING):
        place = pl.ds(pl.multiple_of(lax.rem(far + d, RING) * rows, rows), rows)
        outs[d][0:rows] = got[0][place] + got[1][place] + (got[2][place] + got[3][place])
        outs[d][rows:] = jnp.zeros_like(outs[d][rows:])
        outs[d][rows : rows + 1] = top
        outs[d][rows + 1 : rows + 2] = total


def partial_sum(got):
    height, keys = got[0].shape
    height = (height - 8) // RING + 8
    return call(
        partial_kernel,
        "partial_sum",
        in_specs=[VMEM] * RING,
        out_specs=[VMEM] * RING,
        out_shape=[f32(height, keys)] * RING,
    )(*got)


def active_kernel(qh_ref, k_ref, active_ref):
    heads, rows, _ = qh_ref.shape

    def step(i, carry):
        for j in range(GROUP):
            active_ref[i * GROUP + j] = jnp.maximum(dot(k_ref[...], qh_ref[i * GROUP + j], NT), 0.0)
        return carry

    lax.fori_loop(0, heads // GROUP, step, 0)


def active_products(qh, index_keys):
    heads, rows, _ = qh.shape
    return call(active_kernel, "active_products", 24, out_shape=f32(heads, index_keys.shape[0], rows))(qh, index_keys)


def dlogits_kernel(key_total, *refs):
    got = refs[0:RING]
    logits_ref, active_ref, k_ref, send_ref, turned = refs[RING:]
    heads, _, rows = active_ref.shape
    depth = k_ref.shape[1]
    keys = k_ref.shape[0]
    root = 1.0 / math.sqrt(depth)

    ltop, lsum = merged_stats(
        [r[rows : rows + 1, 0:rows] for r in got], [r[rows + 1 : rows + 2, 0:rows] for r in got]
    )
    target = got[0][0:rows] + got[1][0:rows] + (got[2][0:rows] + got[3][0:rows])
    soft = jnp.exp(logits_ref[...] - ltop) * (1.0 / lsum)
    for k in range(0, keys, rows):
        turned[k : k + rows] = key_total * (soft[k : k + rows] - target[:, k : k + rows].T)
        send_ref[0:rows, k : k + rows] = turned[k : k + rows].T
        send_ref[rows + heads // 2 :, k : k + rows] = k_ref[k : k + rows].astype(jnp.float32)

    def step(i, first, column):
        sums = []
        for j in range(GROUP):
            sums.append(jnp.sum(active_ref[i * GROUP + j] * turned[...], axis=0, keepdims=True) * root)
        place = pl.ds(pl.multiple_of(rows + first, GROUP), GROUP)
        send_ref[place, column : column + rows] = jnp.concatenate(sums, axis=0)

    half = heads // 2 // GROUP

    def low(i, carry):
        step(i, i * GROUP, 0)
        return carry

    def high(i, carry):
        step(i + half, i * GROUP, rows)
        return carry

    lax.fori_loop(0, half, low, 0)
    lax.fori_loop(0, half, high, 0)


def dlogits_of(got, logits, active, index_keys, key_total):
    heads, keys, rows = active.shape
    return call(
        functools.partial(dlogits_kernel, key_total),
        "dlogits",
        24,
        out_shape=f32(2 * rows + heads // 2, keys),
        scratch_shapes=[pltpu.VMEM((keys, rows), jnp.float32)],
    )(*got, logits, active, index_keys)


def keys_kernel(dlogits_ref, active_ref, qh_ref, w_ref, keys_ref, slopes, turned):
    heads, rows, depth = qh_ref.shape
    root = 1.0 / math.sqrt(depth)
    for k in range(0, turned.shape[0], rows):
        turned[k : k + rows] = dlogits_ref[0:rows, k : k + rows].T
    keys_ref[...] = jnp.zeros_like(keys_ref)

    def step(i, carry):
        weights = w_ref[pl.ds(i * GROUP, GROUP)] * root
        for j in range(GROUP):
            slope = jnp.where(active_ref[i * GROUP + j] > 0.0, turned[...] * weights[j : j + 1], 0.0)
            slopes[:, j * rows : (j + 1) * rows] = slope.astype(jnp.bfloat16)
        chunk = qh_ref[pl.ds(i * GROUP, GROUP)].reshape(GROUP * rows, depth)
        keys_ref[...] += dot(slopes[...], chunk, NN)
        return carry

    lax.fori_loop(0, heads // GROUP, step, 0)


def key_gradient(dlogits, active, qh, weights):
    heads, rows, depth = qh.shape
    keys = active.shape[1]
    return call(
        keys_kernel,
        "key_gradient",
        24,
        out_shape=f32(keys, depth),
        scratch_shapes=[pltpu.VMEM((keys, GROUP * rows), jnp.bfloat16), pltpu.VMEM((keys, rows), jnp.float32)],
    )(dlogits, active, qh, weights)


def query_kernel(offsets, pieces, *refs):
    ring, count = RING, len(offsets)
    got = refs[0:ring]
    qh_ref, w_ref = refs[ring : ring + 2]
    outs = refs[ring + 2 : ring + 2 + count]
    slopes, acc, near, dlogits = refs[ring + 2 + count :]
    heads, rows, depth = qh_ref.shape
    keys = got[0].shape[1]
    share = heads // (ring * ring)
    extra = heads // 2
    root = 1.0 / math.sqrt(depth)
    near_at, far_at, near_stride, far_stride = position()
    span = rows // pieces
    few = extra // pieces

    wsum = got[0][rows : rows + extra]
    for d in range(1, ring):
        wsum = wsum + got[d][rows : rows + extra]
    for d in range(ring):
        for k in range(0, keys, rows):
            near[d * keys + k : d * keys + k + rows] = got[d][rows + extra :, k : k + rows].astype(jnp.bfloat16)
        dlogits[:, d * keys : (d + 1) * keys] = got[d][0:rows] * root
    columns = jnp.concatenate([w_ref[...], jnp.zeros((LANES - heads, rows), jnp.float32)], axis=0).T

    for i, d in enumerate(offsets):
        first = (lax.rem(far_at + d, ring) * far_stride + near_at * near_stride) * share
        weights = pltpu.roll(columns, LANES - first, 1)
        queries = qh_ref[pl.ds(first, share)].reshape(share * rows, depth)
        for k in range(0, ring * keys, keys):
            products = dot(queries, near[k : k + keys], NT)
            for j in range(share):
                part = products[j * rows : (j + 1) * rows]
                slope = jnp.where(part > 0.0, dlogits[:, k : k + keys] * weights[:, j : j + 1], 0.0)
                slopes[j * rows : (j + 1) * rows, k : k + keys] = slope.astype(jnp.bfloat16)
        acc[...] = dot(slopes[...], near[...], NN)
        for z in range(pieces):
            for j in range(share):
                start = j * rows + z * span
                outs[i][z, pl.ds(j, span, stride=share), :] = acc[start : start + span]
            piece = wsum[z * few : (z + 1) * few]
            outs[i][z, share * span : share * span + few] = piece[:, 0:rows]
            outs[i][z, share * span + few :] = piece[:, rows : 2 * rows]


def query_gradient(offsets, got, qh, weights, pieces):
    keys = got[0].shape[1]
    heads, rows, depth = qh.shape
    share = heads // (RING * RING)
    tall = share * (rows // pieces) + heads // pieces
    return call(
        functools.partial(query_kernel, offsets, pieces),
        "query_gradient",
        24,
        in_specs=[VMEM] * (RING + 2),
        out_specs=[VMEM] * len(offsets),
        out_shape=[f32(pieces, tall, depth)] * len(offsets),
        scratch_shapes=[
            pltpu.VMEM((share * rows, RING * keys), jnp.bfloat16),
            pltpu.VMEM((share * rows, depth), jnp.float32),
            pltpu.VMEM((RING * keys, depth), jnp.bfloat16),
            pltpu.VMEM((rows, RING * keys), jnp.float32),
        ],
    )(*got, qh, weights)


def results_kernel(got_ref, query_ref, weight_ref):
    pieces, tall, depth = got_ref.shape
    span = query_ref.shape[1]
    few = (tall - span) // 2
    query_ref[...] = got_ref[:, 0:span]
    for z in range(pieces):
        weight_ref[z * few : (z + 1) * few] = got_ref[z, span : span + few]
        weight_ref[(pieces + z) * few : (pieces + z + 1) * few] = got_ref[z, span + few :]


def results(got, heads, span):
    pieces, _, depth = got.shape
    return call(
        results_kernel,
        "results",
        16,
        out_shape=(f32(pieces, span, depth), f32(heads, depth)),
    )(got)


def exchange(x, axis):
    return lax.all_to_all(x, axis, split_axis=0, concat_axis=0, tiled=True)


def shift(x, d, across):
    pairs = []
    for a in range(RING):
        for b in range(RING):
            for row in range(2):
                if (row == 1) != across:
                    there = (a + d) % RING * RING + b
                else:
                    there = a * RING + (b + d) % RING
                pairs.append(((a * RING + b) * 2 + row, there * 2 + row))
    return lax.ppermute(x, ("head", "row"), pairs)


def shards(mla_query, mla_cache, index_query, index_keys, index_weight):
    key_count = lax.axis_size("key")
    head_count = lax.axis_size("head")
    rows = mla_query.shape[0]
    keys, depth = index_keys.shape
    heads = index_query.shape[1]
    share = heads // head_count
    row_index = lax.axis_index("row")
    weights = index_weight.T
    queries = jnp.transpose(mla_query, (1, 2, 0))
    cache = jnp.swapaxes(mla_cache, 1, 2)
    terms, tops, send1, logits, qh = scores_and_logits(queries, cache, index_query, index_keys, weights, key_count)
    got1 = exchange(send1, "key")
    (far_two,) = head_sum((2,), terms, tops, got1)
    got1, _ = lax.optimization_barrier((got1, far_two))
    sides = head_sum((1, 3), terms, tops, got1)
    (own,) = head_sum((0,), terms, tops, got1)
    two = shift(far_two, 2, False)
    one = shift(sides[0], 1, False)
    three = shift(sides[1], 3, False)
    own, late = lax.optimization_barrier((own, qh))
    active = active_products(late, index_keys)
    got2, active = lax.optimization_barrier(([own, one, two, three], active))
    send2 = partial_sum(got2)
    two, one, three = [shift(send2[d], d, True) for d in (2, 1, 3)]
    got2 = [send2[0], one, two, three]
    key_total = float(keys * head_count * key_count)
    send3 = dlogits_of(got2, logits, active, index_keys, key_total)
    two, one, three = [shift(send3, d, False) for d in (2, 1, 3)]
    got3 = [send3, one, two, three]

    (far_two,) = query_gradient((2,), got3, qh, weights, key_count)
    got3, active, _ = lax.optimization_barrier((got3, active, far_two))
    sides = query_gradient((1, 3), got3, qh, weights, key_count)
    (own,) = query_gradient((0,), got3, qh, weights, key_count)
    two = shift(far_two, 2, True)
    one = shift(sides[0], 1, True)
    three = shift(sides[1], 3, True)
    active, _ = lax.optimization_barrier((active, own))
    keys_part = key_gradient(send3, active, qh, weights)
    two, keys_part = lax.optimization_barrier((two, keys_part))
    send4 = own + one + (two + three)

    half = keys // 2
    away = lax.dynamic_slice_in_dim(keys_part, (1 - row_index) * half, half, 0)
    near = lax.dynamic_slice_in_dim(keys_part, row_index * half, half, 0)
    key_grad = near + lax.ppermute(away, "row", [(0, 1), (1, 0)])

    got4 = jnp.sum(exchange(send4, "key"), axis=0)
    got5 = exchange(jnp.broadcast_to(got4[None], (key_count, *got4.shape)), "key")
    query_grad, weight_grad = results(got5, heads, share * (rows // key_count))
    return (query_grad.reshape(rows, share, depth), key_grad, weight_grad.T)


def solution(mesh):
    placed = (
        P("row", "head", None),
        P(None, "key", None),
        P("row", None, None),
        P(("head", "key"), None),
        P("row", None),
    )
    return jax.shard_map(
        shards,
        mesh=mesh,
        in_specs=placed,
        out_specs=(P("row", "head", None), P(("head", "key", "row"), None), P("row", None)),
        check_vma=False,
    )
```

```python
import functools
import math

import jax
import jax.numpy as jnp
from jax import lax
from jax.experimental import pallas as pl
from jax.experimental.pallas import tpu as pltpu
from jax.sharding import PartitionSpec as P

MH = 128
LOG2E = 1.4426950408889634
SCORE2 = LOG2E / math.sqrt(192.0)
LANES = 128
NT = (((1,), (1,)), ((), ()))
TN = (((0,), (0,)), ((), ()))
NN = (((1,), (0,)), ((), ()))


def dot(a, b, dims):
    return lax.dot_general(a, b, dims, preferred_element_type=jnp.float32)


def lane_iota(rows):
    return lax.broadcasted_iota(jnp.int32, (rows, LANES), 1)


RING = 4
PART = 4
GROUP = 8
VMEM = pl.BlockSpec(memory_space=pltpu.VMEM)
HBM = pl.BlockSpec(memory_space=pltpu.HBM)


def call(kernel, name, megabytes=32, **options):
    return pl.pallas_call(
        kernel,
        name=name,
        compiler_params=pltpu.CompilerParams(vmem_limit_bytes=megabytes << 20),
        **options,
    )


def in_hbm(x):
    return pltpu.with_memory_space_constraint(x, pltpu.HBM)


def f32(*shape):
    return jax.ShapeDtypeStruct(shape, jnp.float32)


def bf16(*shape):
    return jax.ShapeDtypeStruct(shape, jnp.bfloat16)


def position():
    head, first = lax.axis_index("head"), lax.axis_index("row") == 0
    x, y = lax.div(head, RING), lax.rem(head, RING)
    return jnp.where(first, y, x), jnp.where(first, x, y), jnp.where(first, 1, RING), jnp.where(first, RING, 1)


def scores_kernel(
    q_hbm, c_hbm, iq_hbm, k_hbm, w_hbm,
    e_ref, tops_ref, send_ref, logits_ref, qh_ref,
    q_ref, c_ref, iq_ref, k_ref, w_ref, wide, total_ref, queries_ref, tops, sums, sems,
):
    heads, width, rows = q_ref.shape
    blocks = c_ref.shape[0]
    steps = blocks // PART
    _, iheads, depth = iq_ref.shape
    keys = k_ref.shape[0]
    group = iheads
    pitch = wide.shape[0] // rows

    first = pltpu.make_async_copy(q_hbm, q_ref, sems.at[steps])
    first.start()

    def part_copy(step):
        span = pl.ds(step * PART, PART)
        return pltpu.make_async_copy(c_hbm.at[span], c_ref.at[span], sems.at[step])

    others = [(iq_hbm, iq_ref), (k_hbm, k_ref), (w_hbm, w_ref)]
    others = [pltpu.make_async_copy(src, dst, sems.at[steps + 1 + i]) for i, (src, dst) in enumerate(others)]
    for step in range(steps):
        part_copy(step).start()
    for copy in others:
        copy.start()

    tops[...] = jnp.zeros_like(tops)
    sums[...] = jnp.zeros_like(sums)
    first.wait()
    for h in range(heads):
        queries_ref[h * rows : (h + 1) * rows] = q_ref[h].T
    lane = lane_iota(rows)

    def score_step(step, carry):
        part_copy(step).wait()
        for h in range(0, heads, 2):
            queries = queries_ref[h * rows : (h + 2) * rows]
            scores = [dot(queries, c_ref[step * PART + j], NN) for j in range(PART)]
            top = scores[0]
            for score in scores[1:]:
                top = jnp.maximum(top, score)
            top = jnp.max(top, axis=1, keepdims=True)
            total = None
            for j, score in enumerate(scores):
                terms = jnp.exp2((score - top) * SCORE2)
                total = terms if total is None else total + terms
                e_ref[step * PART + j, h : h + 2] = terms.astype(jnp.bfloat16).reshape(2, rows, keys)
            total = jnp.sum(total, axis=1, keepdims=True)
            low, high = lane == h * steps + step, lane == (h + 1) * steps + step
            tops[...] = jnp.where(low, top[0:rows], jnp.where(high, top[rows:], tops[...]))
            sums[...] = jnp.where(low, total[0:rows], jnp.where(high, total[rows:], sums[...]))
        return carry

    lax.fori_loop(0, steps, score_step, 0)

    for copy in others:
        copy.wait()
    total_ref[...] = jnp.zeros_like(total_ref)
    for t in range(rows):
        wide[t * pitch : t * pitch + iheads] = iq_ref[t].astype(jnp.float32)
    columns = jnp.concatenate([w_ref[...], jnp.zeros((LANES - iheads, rows), jnp.float32)], axis=0).T

    def logit_step(step, carry):
        weights = pltpu.roll(columns, LANES - group * step, 1)
        for j in range(group):
            head = step * group + j
            qh_ref[head] = wide[pl.ds(head, rows, stride=pitch), :].astype(jnp.bfloat16)
        chunk = qh_ref[pl.ds(step * group, group)].reshape(group * rows, depth)
        products = dot(chunk, k_ref[...], NT)
        total = total_ref[...]
        for j in range(group):
            part = products[j * rows : (j + 1) * rows]
            total = total + jnp.maximum(part, 0.0) * weights[:, j : j + 1]
        total_ref[...] = total
        return carry

    lax.fori_loop(0, iheads // group, logit_step, 0)

    turned_tops = tops[...].T[0 : heads * steps]
    turned_sums = sums[...].T[0 : heads * steps]
    tops_ref[...] = turned_tops
    for k in range(0, keys, rows):
        logits_ref[k : k + rows] = total_ref[:, k : k + rows].T * (1.0 / math.sqrt(depth))
    logits = logits_ref[...]
    ltop = jnp.max(logits, axis=0, keepdims=True)
    lsum = jnp.sum(jnp.exp(logits - ltop), axis=0, keepdims=True)
    flat = []
    for h in range(heads):
        span = slice(h * steps, (h + 1) * steps)
        top = jnp.max(turned_tops[span], axis=0, keepdims=True)
        scaled = turned_sums[span] * jnp.exp2((turned_tops[span] - top) * SCORE2)
        flat.append((top, jnp.sum(scaled, axis=0, keepdims=True)))
    flat = jnp.concatenate([top for top, _ in flat] + [total for _, total in flat], axis=0)
    for z in range(send_ref.shape[0]):
        send_ref[z, 0 : 2 * heads] = flat
        send_ref[z, 2 * heads :] = jnp.zeros((8, rows), jnp.float32)
        send_ref[z, 2 * heads : 2 * heads + 1] = ltop
        send_ref[z, 2 * heads + 1 : 2 * heads + 2] = lsum


def scores_and_logits(queries, cache, index_query, index_keys, weights, key_count):
    heads, width, rows = queries.shape
    blocks, _, keys = cache.shape
    _, iheads, depth = index_query.shape
    steps = blocks // PART
    return call(
        scores_kernel,
        "scores_and_logits",
        32,
        in_specs=[HBM] * 5,
        out_specs=[VMEM] * 5,
        out_shape=(
            bf16(blocks, heads, rows, keys),
            f32(heads * steps, rows),
            f32(key_count, 2 * heads + 8, rows),
            f32(keys, rows),
            bf16(iheads, rows, depth),
        ),
        scratch_shapes=[
            pltpu.VMEM(queries.shape, jnp.bfloat16),
            pltpu.VMEM(cache.shape, jnp.bfloat16),
            pltpu.VMEM(index_query.shape, jnp.bfloat16),
            pltpu.VMEM(index_keys.shape, jnp.bfloat16),
            pltpu.VMEM(weights.shape, jnp.float32),
            pltpu.VMEM((rows * (iheads + 8), depth), jnp.float32),
            pltpu.VMEM((rows, keys), jnp.float32),
            pltpu.VMEM((rows * heads, width), jnp.bfloat16),
            pltpu.VMEM((rows, LANES), jnp.float32),
            pltpu.VMEM((rows, LANES), jnp.float32),
            pltpu.SemaphoreType.DMA((steps + 4,)),
        ],
    )(*[in_hbm(x) for x in (queries, cache, index_query, index_keys, weights)])


def headsum_kernel(offsets, e_ref, tops_ref, got_ref, *outs):
    _, heads, rows, keys = e_ref.shape
    steps = tops_ref.shape[0] // heads
    near, _, near_stride, far_stride = position()

    tops = got_ref[:, 0:heads]
    top = jnp.max(tops, axis=0)
    total = jnp.sum(got_ref[:, heads : 2 * heads] * jnp.exp2((tops - top[None]) * SCORE2), axis=0)
    scale = (1.0 / MH) / total
    weights = []
    for h in range(heads):
        local = tops_ref[h * steps : (h + 1) * steps] - top[h : h + 1]
        weights.append(jnp.exp2(jnp.minimum(local * SCORE2, 0.0)) * scale[h : h + 1])
    weights = jnp.concatenate(weights + [jnp.zeros((LANES - heads * steps, rows), jnp.float32)], axis=0).T
    ltops = got_ref[:, 2 * heads : 2 * heads + 1]
    ltop = jnp.max(ltops, axis=0)
    lsum = jnp.sum(got_ref[:, 2 * heads + 1 : 2 * heads + 2] * jnp.exp(ltops - ltop[None]), axis=0)
    tail = jnp.concatenate([ltop, lsum, jnp.zeros((6, rows), jnp.float32)], axis=0)
    tail = jnp.concatenate([tail, jnp.zeros((8, keys - rows), jnp.float32)], axis=1)

    for i, d in enumerate(offsets):

        def body(k, carry):
            block = lax.rem(near + d, RING) * near_stride + k * far_stride
            columns = pltpu.roll(weights, LANES - lax.div(block, PART), 1)
            total = None
            for h in range(heads):
                term = e_ref[block, h].astype(jnp.float32) * columns[:, h * steps : h * steps + 1]
                total = term if total is None else total + term
            outs[i][pl.ds(pl.multiple_of(k * rows, rows), rows)] = total
            return carry

        lax.fori_loop(0, RING, body, 0)
        outs[i][RING * rows :] = tail


def head_sum(offsets, terms, tops, got):
    blocks, heads, rows, keys = terms.shape
    return call(
        functools.partial(headsum_kernel, offsets),
        "head_sum",
        24,
        in_specs=[VMEM] * 3,
        out_specs=[VMEM] * len(offsets),
        out_shape=[f32(blocks // RING * rows + 8, keys)] * len(offsets),
    )(terms, tops, got)


def merged_stats(tops, sums):
    top = tops[0]
    for other in tops[1:]:
        top = jnp.maximum(top, other)
    total = sums[0] * jnp.exp(tops[0] - top)
    for other, count in zip(tops[1:], sums[1:]):
        total = total + count * jnp.exp(other - top)
    return top, total


def partial_kernel(*refs):
    got, outs = refs[0:RING], refs[RING:]
    rows = outs[0].shape[0] - 8
    _, far, _, _ = position()
    last = RING * rows
    top, total = merged_stats([r[last : last + 1] for r in got], [r[last + 1 : last + 2] for r in got])
    for d in range(RING):
        place = pl.ds(pl.multiple_of(lax.rem(far + d, RING) * rows, rows), rows)
        outs[d][0:rows] = got[0][place] + got[1][place] + (got[2][place] + got[3][place])
        outs[d][rows:] = jnp.zeros_like(outs[d][rows:])
        outs[d][rows : rows + 1] = top
        outs[d][rows + 1 : rows + 2] = total


def partial_sum(got):
    height, keys = got[0].shape
    height = (height - 8) // RING + 8
    return call(
        partial_kernel,
        "partial_sum",
        in_specs=[VMEM] * RING,
        out_specs=[VMEM] * RING,
        out_shape=[f32(height, keys)] * RING,
    )(*got)


def active_kernel(qh_ref, k_ref, active_ref):
    heads, rows, _ = qh_ref.shape

    def step(i, carry):
        for j in range(GROUP):
            active_ref[i * GROUP + j] = jnp.maximum(dot(k_ref[...], qh_ref[i * GROUP + j], NT), 0.0)
        return carry

    lax.fori_loop(0, heads // GROUP, step, 0)


def active_products(qh, index_keys):
    heads, rows, _ = qh.shape
    return call(active_kernel, "active_products", 24, out_shape=f32(heads, index_keys.shape[0], rows))(qh, index_keys)


def dlogits_kernel(key_total, *refs):
    got = refs[0:RING]
    logits_ref, active_ref, k_ref, send_ref, turned = refs[RING:]
    heads, _, rows = active_ref.shape
    depth = k_ref.shape[1]
    keys = k_ref.shape[0]
    root = 1.0 / math.sqrt(depth)

    ltop, lsum = merged_stats(
        [r[rows : rows + 1, 0:rows] for r in got], [r[rows + 1 : rows + 2, 0:rows] for r in got]
    )
    target = got[0][0:rows] + got[1][0:rows] + (got[2][0:rows] + got[3][0:rows])
    soft = jnp.exp(logits_ref[...] - ltop) * (1.0 / lsum)
    for k in range(0, keys, rows):
        turned[k : k + rows] = key_total * (soft[k : k + rows] - target[:, k : k + rows].T)
        send_ref[0:rows, k : k + rows] = turned[k : k + rows].T
        send_ref[rows + heads // 2 :, k : k + rows] = k_ref[k : k + rows].astype(jnp.float32)

    def step(i, first, column):
        sums = []
        for j in range(GROUP):
            sums.append(jnp.sum(active_ref[i * GROUP + j] * turned[...], axis=0, keepdims=True) * root)
        place = pl.ds(pl.multiple_of(rows + first, GROUP), GROUP)
        send_ref[place, column : column + rows] = jnp.concatenate(sums, axis=0)

    half = heads // 2 // GROUP

    def low(i, carry):
        step(i, i * GROUP, 0)
        return carry

    def high(i, carry):
        step(i + half, i * GROUP, rows)
        return carry

    lax.fori_loop(0, half, low, 0)
    lax.fori_loop(0, half, high, 0)


def dlogits_of(got, logits, active, index_keys, key_total):
    heads, keys, rows = active.shape
    return call(
        functools.partial(dlogits_kernel, key_total),
        "dlogits",
        24,
        out_shape=f32(2 * rows + heads // 2, keys),
        scratch_shapes=[pltpu.VMEM((keys, rows), jnp.float32)],
    )(*got, logits, active, index_keys)


def keys_kernel(dlogits_ref, active_ref, qh_ref, w_ref, keys_ref, slopes, turned):
    heads, rows, depth = qh_ref.shape
    root = 1.0 / math.sqrt(depth)
    for k in range(0, turned.shape[0], rows):
        turned[k : k + rows] = dlogits_ref[0:rows, k : k + rows].T
    keys_ref[...] = jnp.zeros_like(keys_ref)

    def step(i, carry):
        weights = w_ref[pl.ds(i * GROUP, GROUP)] * root
        for j in range(GROUP):
            slope = jnp.where(active_ref[i * GROUP + j] > 0.0, turned[...] * weights[j : j + 1], 0.0)
            slopes[:, j * rows : (j + 1) * rows] = slope.astype(jnp.bfloat16)
        chunk = qh_ref[pl.ds(i * GROUP, GROUP)].reshape(GROUP * rows, depth)
        keys_ref[...] += dot(slopes[...], chunk, NN)
        return carry

    lax.fori_loop(0, heads // GROUP, step, 0)


def key_gradient(dlogits, active, qh, weights):
    heads, rows, depth = qh.shape
    keys = active.shape[1]
    return call(
        keys_kernel,
        "key_gradient",
        24,
        out_shape=f32(keys, depth),
        scratch_shapes=[pltpu.VMEM((keys, GROUP * rows), jnp.bfloat16), pltpu.VMEM((keys, rows), jnp.float32)],
    )(dlogits, active, qh, weights)


def query_kernel(offsets, pieces, *refs):
    ring, count = RING, len(offsets)
    got = refs[0:ring]
    qh_ref, w_ref = refs[ring : ring + 2]
    outs = refs[ring + 2 : ring + 2 + count]
    slopes, acc, near, dlogits = refs[ring + 2 + count :]
    heads, rows, depth = qh_ref.shape
    keys = got[0].shape[1]
    share = heads // (ring * ring)
    extra = heads // 2
    root = 1.0 / math.sqrt(depth)
    near_at, far_at, near_stride, far_stride = position()
    span = rows // pieces
    few = extra // pieces

    wsum = got[0][rows : rows + extra]
    for d in range(1, ring):
        wsum = wsum + got[d][rows : rows + extra]
    for d in range(ring):
        for k in range(0, keys, rows):
            near[d * keys + k : d * keys + k + rows] = got[d][rows + extra :, k : k + rows].astype(jnp.bfloat16)
        dlogits[:, d * keys : (d + 1) * keys] = got[d][0:rows] * root
    columns = jnp.concatenate([w_ref[...], jnp.zeros((LANES - heads, rows), jnp.float32)], axis=0).T

    for i, d in enumerate(offsets):
        first = (lax.rem(far_at + d, ring) * far_stride + near_at * near_stride) * share
        weights = pltpu.roll(columns, LANES - first, 1)
        queries = qh_ref[pl.ds(first, share)].reshape(share * rows, depth)
        for k in range(0, ring * keys, keys):
            products = dot(queries, near[k : k + keys], NT)
            for j in range(share):
                part = products[j * rows : (j + 1) * rows]
                slope = jnp.where(part > 0.0, dlogits[:, k : k + keys] * weights[:, j : j + 1], 0.0)
                slopes[j * rows : (j + 1) * rows, k : k + keys] = slope.astype(jnp.bfloat16)
        acc[...] = dot(slopes[...], near[...], NN)
        for z in range(pieces):
            for j in range(share):
                start = j * rows + z * span
                outs[i][z, pl.ds(j, span, stride=share), :] = acc[start : start + span]
            piece = wsum[z * few : (z + 1) * few]
            outs[i][z, share * span : share * span + few] = piece[:, 0:rows]
            outs[i][z, share * span + few :] = piece[:, rows : 2 * rows]


def query_gradient(offsets, got, qh, weights, pieces):
    keys = got[0].shape[1]
    heads, rows, depth = qh.shape
    share = heads // (RING * RING)
    tall = share * (rows // pieces) + heads // pieces
    return call(
        functools.partial(query_kernel, offsets, pieces),
        "query_gradient",
        24,
        in_specs=[VMEM] * (RING + 2),
        out_specs=[VMEM] * len(offsets),
        out_shape=[f32(pieces, tall, depth)] * len(offsets),
        scratch_shapes=[
            pltpu.VMEM((share * rows, RING * keys), jnp.bfloat16),
            pltpu.VMEM((share * rows, depth), jnp.float32),
            pltpu.VMEM((RING * keys, depth), jnp.bfloat16),
            pltpu.VMEM((rows, RING * keys), jnp.float32),
        ],
    )(*got, qh, weights)


def results_kernel(got_ref, query_ref, weight_ref):
    pieces, tall, depth = got_ref.shape
    span = query_ref.shape[1]
    few = (tall - span) // 2
    query_ref[...] = got_ref[:, 0:span]
    for z in range(pieces):
        weight_ref[z * few : (z + 1) * few] = got_ref[z, span : span + few]
        weight_ref[(pieces + z) * few : (pieces + z + 1) * few] = got_ref[z, span + few :]


def results(got, heads, span):
    pieces, _, depth = got.shape
    return call(
        results_kernel,
        "results",
        16,
        out_shape=(f32(pieces, span, depth), f32(heads, depth)),
    )(got)


def exchange(x, axis):
    return lax.all_to_all(x, axis, split_axis=0, concat_axis=0, tiled=True)


def shift(x, d, across):
    pairs = []
    for a in range(RING):
        for b in range(RING):
            for row in range(2):
                if (row == 1) != across:
                    there = (a + d) % RING * RING + b
                else:
                    there = a * RING + (b + d) % RING
                pairs.append(((a * RING + b) * 2 + row, there * 2 + row))
    return lax.ppermute(x, ("head", "row"), pairs)


def shards(mla_query, mla_cache, index_query, index_keys, index_weight):
    key_count = lax.axis_size("key")
    head_count = lax.axis_size("head")
    rows = mla_query.shape[0]
    keys, depth = index_keys.shape
    heads = index_query.shape[1]
    share = heads // head_count
    row_index = lax.axis_index("row")
    weights = index_weight.T
    queries = jnp.transpose(mla_query, (1, 2, 0))
    cache = jnp.swapaxes(mla_cache, 1, 2)
    terms, tops, send1, logits, qh = scores_and_logits(queries, cache, index_query, index_keys, weights, key_count)
    got1 = exchange(send1, "key")
    (far_two,) = head_sum((2,), terms, tops, got1)
    got1, _ = lax.optimization_barrier((got1, far_two))
    sides = head_sum((1, 3), terms, tops, got1)
    (own,) = head_sum((0,), terms, tops, got1)
    two = shift(far_two, 2, False)
    one = shift(sides[0], 1, False)
    three = shift(sides[1], 3, False)
    own, late = lax.optimization_barrier((own, qh))
    active = active_products(late, index_keys)
    got2, active = lax.optimization_barrier(([own, one, two, three], active))
    send2 = partial_sum(got2)
    two, one, three = [shift(send2[d], d, True) for d in (2, 1, 3)]
    got2 = [send2[0], one, two, three]
    key_total = float(keys * head_count * key_count)
    send3 = dlogits_of(got2, logits, active, index_keys, key_total)
    two, one, three = [shift(send3, d, False) for d in (2, 1, 3)]
    got3 = [send3, one, two, three]

    (far_two,) = query_gradient((2,), got3, qh, weights, key_count)
    got3, active, _ = lax.optimization_barrier((got3, active, far_two))
    sides = query_gradient((1, 3), got3, qh, weights, key_count)
    (own,) = query_gradient((0,), got3, qh, weights, key_count)
    two = shift(far_two, 2, True)
    one = shift(sides[0], 1, True)
    three = shift(sides[1], 3, True)
    active, _ = lax.optimization_barrier((active, own))
    keys_part = key_gradient(send3, active, qh, weights)
    two, keys_part = lax.optimization_barrier((two, keys_part))
    send4 = own + one + (two + three)

    half = keys // 2
    away = lax.dynamic_slice_in_dim(keys_part, (1 - row_index) * half, half, 0)
    near = lax.dynamic_slice_in_dim(keys_part, row_index * half, half, 0)
    key_grad = near + lax.ppermute(away, "row", [(0, 1), (1, 0)])

    got4 = jnp.sum(exchange(send4, "key"), axis=0)
    got5 = exchange(jnp.broadcast_to(got4[None], (key_count, *got4.shape)), "key")
    query_grad, weight_grad = results(got5, heads, share * (rows // key_count))
    return (query_grad.reshape(rows, share, depth), key_grad, weight_grad.T)


def solution(mesh):
    placed = (
        P("row", "head", None),
        P(None, "key", None),
        P("row", None, None),
        P(("head", "key"), None),
        P("row", None),
    )
    return jax.shard_map(
        shards,
        mesh=mesh,
        in_specs=placed,
        out_specs=(P("row", "head", None), P(("head", "key", "row"), None), P("row", None)),
        check_vma=False,
    )
```

```python
import functools
import math

import jax
import jax.numpy as jnp
from jax import lax
from jax.experimental import pallas as pl
from jax.experimental.pallas import tpu as pltpu
from jax.sharding import PartitionSpec as P

MH = 128
LOG2E = 1.4426950408889634
SCORE2 = LOG2E / math.sqrt(192.0)
LANES = 128
NT = (((1,), (1,)), ((), ()))
TN = (((0,), (0,)), ((), ()))
NN = (((1,), (0,)), ((), ()))


def dot(a, b, dims):
    return lax.dot_general(a, b, dims, preferred_element_type=jnp.float32)


def lane_iota(rows):
    return lax.broadcasted_iota(jnp.int32, (rows, LANES), 1)


RING = 4
PART = 4
GROUP = 16
VMEM = pl.BlockSpec(memory_space=pltpu.VMEM)
HBM = pl.BlockSpec(memory_space=pltpu.HBM)


def call(kernel, name, megabytes=32, **options):
    return pl.pallas_call(
        kernel,
        name=name,
        compiler_params=pltpu.CompilerParams(vmem_limit_bytes=megabytes << 20),
        **options,
    )


def in_hbm(x):
    return pltpu.with_memory_space_constraint(x, pltpu.HBM)


def f32(*shape):
    return jax.ShapeDtypeStruct(shape, jnp.float32)


def bf16(*shape):
    return jax.ShapeDtypeStruct(shape, jnp.bfloat16)


def position():
    head, first = lax.axis_index("head"), lax.axis_index("row") == 0
    x, y = lax.div(head, RING), lax.rem(head, RING)
    return jnp.where(first, y, x), jnp.where(first, x, y), jnp.where(first, 1, RING), jnp.where(first, RING, 1)


def scores_kernel(
    q_hbm, c_hbm, iq_hbm, k_hbm, w_hbm,
    e_ref, tops_ref, send_ref, logits_ref, qh_ref,
    q_ref, c_ref, iq_ref, k_ref, w_ref, wide, total_ref, queries_ref, tops, sums, sems,
):
    heads, width, rows = q_ref.shape
    blocks = c_ref.shape[0]
    steps = blocks // PART
    _, iheads, depth = iq_ref.shape
    keys = k_ref.shape[0]
    group = iheads
    pitch = wide.shape[0] // rows

    first = pltpu.make_async_copy(q_hbm, q_ref, sems.at[steps])
    first.start()

    def part_copy(step):
        span = pl.ds(step * PART, PART)
        return pltpu.make_async_copy(c_hbm.at[span], c_ref.at[span], sems.at[step])

    others = [(iq_hbm, iq_ref), (k_hbm, k_ref), (w_hbm, w_ref)]
    others = [pltpu.make_async_copy(src, dst, sems.at[steps + 1 + i]) for i, (src, dst) in enumerate(others)]
    for step in range(steps):
        part_copy(step).start()
    for copy in others:
        copy.start()

    tops[...] = jnp.zeros_like(tops)
    sums[...] = jnp.zeros_like(sums)
    first.wait()
    for h in range(heads):
        queries_ref[h * rows : (h + 1) * rows] = q_ref[h].T
    lane = lane_iota(rows)

    def score_step(step, carry):
        part_copy(step).wait()
        for h in range(0, heads, 2):
            queries = queries_ref[h * rows : (h + 2) * rows]
            scores = [dot(queries, c_ref[step * PART + j], NN) for j in range(PART)]
            top = scores[0]
            for score in scores[1:]:
                top = jnp.maximum(top, score)
            top = jnp.max(top, axis=1, keepdims=True)
            total = None
            for j, score in enumerate(scores):
                terms = jnp.exp2((score - top) * SCORE2)
                total = terms if total is None else total + terms
                e_ref[step * PART + j, h : h + 2] = terms.astype(jnp.bfloat16).reshape(2, rows, keys)
            total = jnp.sum(total, axis=1, keepdims=True)
            low, high = lane == h * steps + step, lane == (h + 1) * steps + step
            tops[...] = jnp.where(low, top[0:rows], jnp.where(high, top[rows:], tops[...]))
            sums[...] = jnp.where(low, total[0:rows], jnp.where(high, total[rows:], sums[...]))
        return carry

    lax.fori_loop(0, steps, score_step, 0)

    for copy in others:
        copy.wait()
    total_ref[...] = jnp.zeros_like(total_ref)
    for t in range(rows):
        wide[t * pitch : t * pitch + iheads] = iq_ref[t].astype(jnp.float32)
    columns = jnp.concatenate([w_ref[...], jnp.zeros((LANES - iheads, rows), jnp.float32)], axis=0).T

    def logit_step(step, carry):
        weights = pltpu.roll(columns, LANES - group * step, 1)
        for j in range(group):
            head = step * group + j
            qh_ref[head] = wide[pl.ds(head, rows, stride=pitch), :].astype(jnp.bfloat16)
        chunk = qh_ref[pl.ds(step * group, group)].reshape(group * rows, depth)
        products = dot(chunk, k_ref[...], NT)
        total = total_ref[...]
        for j in range(group):
            part = products[j * rows : (j + 1) * rows]
            total = total + jnp.maximum(part, 0.0) * weights[:, j : j + 1]
        total_ref[...] = total
        return carry

    lax.fori_loop(0, iheads // group, logit_step, 0)

    turned_tops = tops[...].T[0 : heads * steps]
    turned_sums = sums[...].T[0 : heads * steps]
    tops_ref[...] = turned_tops
    for k in range(0, keys, rows):
        logits_ref[k : k + rows] = total_ref[:, k : k + rows].T * (1.0 / math.sqrt(depth))
    logits = logits_ref[...]
    ltop = jnp.max(logits, axis=0, keepdims=True)
    lsum = jnp.sum(jnp.exp(logits - ltop), axis=0, keepdims=True)
    flat = []
    for h in range(heads):
        span = slice(h * steps, (h + 1) * steps)
        top = jnp.max(turned_tops[span], axis=0, keepdims=True)
        scaled = turned_sums[span] * jnp.exp2((turned_tops[span] - top) * SCORE2)
        flat.append((top, jnp.sum(scaled, axis=0, keepdims=True)))
    flat = jnp.concatenate([top for top, _ in flat] + [total for _, total in flat], axis=0)
    for z in range(send_ref.shape[0]):
        send_ref[z, 0 : 2 * heads] = flat
        send_ref[z, 2 * heads :] = jnp.zeros((8, rows), jnp.float32)
        send_ref[z, 2 * heads : 2 * heads + 1] = ltop
        send_ref[z, 2 * heads + 1 : 2 * heads + 2] = lsum


def scores_and_logits(queries, cache, index_query, index_keys, weights, key_count):
    heads, width, rows = queries.shape
    blocks, _, keys = cache.shape
    _, iheads, depth = index_query.shape
    steps = blocks // PART
    return call(
        scores_kernel,
        "scores_and_logits",
        32,
        in_specs=[HBM] * 5,
        out_specs=[VMEM] * 5,
        out_shape=(
            bf16(blocks, heads, rows, keys),
            f32(heads * steps, rows),
            f32(key_count, 2 * heads + 8, rows),
            f32(keys, rows),
            bf16(iheads, rows, depth),
        ),
        scratch_shapes=[
            pltpu.VMEM(queries.shape, jnp.bfloat16),
            pltpu.VMEM(cache.shape, jnp.bfloat16),
            pltpu.VMEM(index_query.shape, jnp.bfloat16),
            pltpu.VMEM(index_keys.shape, jnp.bfloat16),
            pltpu.VMEM(weights.shape, jnp.float32),
            pltpu.VMEM((rows * (iheads + 8), depth), jnp.float32),
            pltpu.VMEM((rows, keys), jnp.float32),
            pltpu.VMEM((rows * heads, width), jnp.bfloat16),
            pltpu.VMEM((rows, LANES), jnp.float32),
            pltpu.VMEM((rows, LANES), jnp.float32),
            pltpu.SemaphoreType.DMA((steps + 4,)),
        ],
    )(*[in_hbm(x) for x in (queries, cache, index_query, index_keys, weights)])


def headsum_kernel(offsets, e_ref, tops_ref, got_ref, *outs):
    _, heads, rows, keys = e_ref.shape
    steps = tops_ref.shape[0] // heads
    near, _, near_stride, far_stride = position()

    tops = got_ref[:, 0:heads]
    top = jnp.max(tops, axis=0)
    total = jnp.sum(got_ref[:, heads : 2 * heads] * jnp.exp2((tops - top[None]) * SCORE2), axis=0)
    scale = (1.0 / MH) / total
    weights = []
    for h in range(heads):
        local = tops_ref[h * steps : (h + 1) * steps] - top[h : h + 1]
        weights.append(jnp.exp2(jnp.minimum(local * SCORE2, 0.0)) * scale[h : h + 1])
    weights = jnp.concatenate(weights + [jnp.zeros((LANES - heads * steps, rows), jnp.float32)], axis=0).T
    ltops = got_ref[:, 2 * heads : 2 * heads + 1]
    ltop = jnp.max(ltops, axis=0)
    lsum = jnp.sum(got_ref[:, 2 * heads + 1 : 2 * heads + 2] * jnp.exp(ltops - ltop[None]), axis=0)
    tail = jnp.concatenate([ltop, lsum, jnp.zeros((6, rows), jnp.float32)], axis=0)
    tail = jnp.concatenate([tail, jnp.zeros((8, keys - rows), jnp.float32)], axis=1)

    for i, d in enumerate(offsets):

        def body(k, carry):
            block = lax.rem(near + d, RING) * near_stride + k * far_stride
            columns = pltpu.roll(weights, LANES - lax.div(block, PART), 1)
            total = None
            for h in range(heads):
                term = e_ref[block, h].astype(jnp.float32) * columns[:, h * steps : h * steps + 1]
                total = term if total is None else total + term
            outs[i][pl.ds(pl.multiple_of(k * rows, rows), rows)] = total
            return carry

        lax.fori_loop(0, RING, body, 0)
        outs[i][RING * rows :] = tail


def head_sum(offsets, terms, tops, got):
    blocks, heads, rows, keys = terms.shape
    return call(
        functools.partial(headsum_kernel, offsets),
        "head_sum",
        24,
        in_specs=[VMEM] * 3,
        out_specs=[VMEM] * len(offsets),
        out_shape=[f32(blocks // RING * rows + 8, keys)] * len(offsets),
    )(terms, tops, got)


def merged_stats(tops, sums):
    top = tops[0]
    for other in tops[1:]:
        top = jnp.maximum(top, other)
    total = sums[0] * jnp.exp(tops[0] - top)
    for other, count in zip(tops[1:], sums[1:]):
        total = total + count * jnp.exp(other - top)
    return top, total


def partial_kernel(*refs):
    got, outs = refs[0:RING], refs[RING:]
    rows = outs[0].shape[0] - 8
    _, far, _, _ = position()
    last = RING * rows
    top, total = merged_stats([r[last : last + 1] for r in got], [r[last + 1 : last + 2] for r in got])
    for d in range(RING):
        place = pl.ds(pl.multiple_of(lax.rem(far + d, RING) * rows, rows), rows)
        outs[d][0:rows] = got[0][place] + got[1][place] + (got[2][place] + got[3][place])
        outs[d][rows:] = jnp.zeros_like(outs[d][rows:])
        outs[d][rows : rows + 1] = top
        outs[d][rows + 1 : rows + 2] = total


def partial_sum(got):
    height, keys = got[0].shape
    height = (height - 8) // RING + 8
    return call(
        partial_kernel,
        "partial_sum",
        in_specs=[VMEM] * RING,
        out_specs=[VMEM] * RING,
        out_shape=[f32(height, keys)] * RING,
    )(*got)


def active_kernel(qh_ref, k_ref, active_ref):
    heads, rows, _ = qh_ref.shape

    def step(i, carry):
        for j in range(GROUP):
            active_ref[i * GROUP + j] = jnp.maximum(dot(k_ref[...], qh_ref[i * GROUP + j], NT), 0.0)
        return carry

    lax.fori_loop(0, heads // GROUP, step, 0)


def active_products(qh, index_keys):
    heads, rows, _ = qh.shape
    return call(active_kernel, "active_products", 24, out_shape=f32(heads, index_keys.shape[0], rows))(qh, index_keys)


def dlogits_kernel(key_total, *refs):
    got = refs[0:RING]
    logits_ref, active_ref, k_ref, send_ref, turned = refs[RING:]
    heads, _, rows = active_ref.shape
    depth = k_ref.shape[1]
    keys = k_ref.shape[0]
    root = 1.0 / math.sqrt(depth)

    ltop, lsum = merged_stats(
        [r[rows : rows + 1, 0:rows] for r in got], [r[rows + 1 : rows + 2, 0:rows] for r in got]
    )
    target = got[0][0:rows] + got[1][0:rows] + (got[2][0:rows] + got[3][0:rows])
    soft = jnp.exp(logits_ref[...] - ltop) * (1.0 / lsum)
    for k in range(0, keys, rows):
        turned[k : k + rows] = key_total * (soft[k : k + rows] - target[:, k : k + rows].T)
        send_ref[0:rows, k : k + rows] = turned[k : k + rows].T
        send_ref[rows + heads // 2 :, k : k + rows] = k_ref[k : k + rows].astype(jnp.float32)

    def step(i, first, column):
        sums = []
        for j in range(GROUP):
            sums.append(jnp.sum(active_ref[i * GROUP + j] * turned[...], axis=0, keepdims=True) * root)
        place = pl.ds(pl.multiple_of(rows + first, GROUP), GROUP)
        send_ref[place, column : column + rows] = jnp.concatenate(sums, axis=0)

    half = heads // 2 // GROUP

    def low(i, carry):
        step(i, i * GROUP, 0)
        return carry

    def high(i, carry):
        step(i + half, i * GROUP, rows)
        return carry

    lax.fori_loop(0, half, low, 0)
    lax.fori_loop(0, half, high, 0)


def dlogits_of(got, logits, active, index_keys, key_total):
    heads, keys, rows = active.shape
    return call(
        functools.partial(dlogits_kernel, key_total),
        "dlogits",
        24,
        out_shape=f32(2 * rows + heads // 2, keys),
        scratch_shapes=[pltpu.VMEM((keys, rows), jnp.float32)],
    )(*got, logits, active, index_keys)


def keys_kernel(dlogits_ref, active_ref, qh_ref, w_ref, keys_ref, slopes, turned):
    heads, rows, depth = qh_ref.shape
    root = 1.0 / math.sqrt(depth)
    for k in range(0, turned.shape[0], rows):
        turned[k : k + rows] = dlogits_ref[0:rows, k : k + rows].T
    keys_ref[...] = jnp.zeros_like(keys_ref)

    def step(i, carry):
        weights = w_ref[pl.ds(i * GROUP, GROUP)] * root
        for j in range(GROUP):
            slope = jnp.where(active_ref[i * GROUP + j] > 0.0, turned[...] * weights[j : j + 1], 0.0)
            slopes[:, j * rows : (j + 1) * rows] = slope.astype(jnp.bfloat16)
        chunk = qh_ref[pl.ds(i * GROUP, GROUP)].reshape(GROUP * rows, depth)
        keys_ref[...] += dot(slopes[...], chunk, NN)
        return carry

    lax.fori_loop(0, heads // GROUP, step, 0)


def key_gradient(dlogits, active, qh, weights):
    heads, rows, depth = qh.shape
    keys = active.shape[1]
    return call(
        keys_kernel,
        "key_gradient",
        24,
        out_shape=f32(keys, depth),
        scratch_shapes=[pltpu.VMEM((keys, GROUP * rows), jnp.bfloat16), pltpu.VMEM((keys, rows), jnp.float32)],
    )(dlogits, active, qh, weights)


def query_kernel(offsets, pieces, *refs):
    ring, count = RING, len(offsets)
    got = refs[0:ring]
    qh_ref, w_ref = refs[ring : ring + 2]
    outs = refs[ring + 2 : ring + 2 + count]
    slopes, acc, near, dlogits = refs[ring + 2 + count :]
    heads, rows, depth = qh_ref.shape
    keys = got[0].shape[1]
    share = heads // (ring * ring)
    extra = heads // 2
    root = 1.0 / math.sqrt(depth)
    near_at, far_at, near_stride, far_stride = position()
    span = rows // pieces
    few = extra // pieces

    wsum = got[0][rows : rows + extra]
    for d in range(1, ring):
        wsum = wsum + got[d][rows : rows + extra]
    for d in range(ring):
        for k in range(0, keys, rows):
            near[d * keys + k : d * keys + k + rows] = got[d][rows + extra :, k : k + rows].astype(jnp.bfloat16)
        dlogits[:, d * keys : (d + 1) * keys] = got[d][0:rows] * root
    columns = jnp.concatenate([w_ref[...], jnp.zeros((LANES - heads, rows), jnp.float32)], axis=0).T

    for i, d in enumerate(offsets):
        first = (lax.rem(far_at + d, ring) * far_stride + near_at * near_stride) * share
        weights = pltpu.roll(columns, LANES - first, 1)
        queries = qh_ref[pl.ds(first, share)].reshape(share * rows, depth)
        for k in range(0, ring * keys, keys):
            products = dot(queries, near[k : k + keys], NT)
            for j in range(share):
                part = products[j * rows : (j + 1) * rows]
                slope = jnp.where(part > 0.0, dlogits[:, k : k + keys] * weights[:, j : j + 1], 0.0)
                slopes[j * rows : (j + 1) * rows, k : k + keys] = slope.astype(jnp.bfloat16)
        acc[...] = dot(slopes[...], near[...], NN)
        for z in range(pieces):
            for j in range(share):
                start = j * rows + z * span
                outs[i][z, pl.ds(j, span, stride=share), :] = acc[start : start + span]
            piece = wsum[z * few : (z + 1) * few]
            outs[i][z, share * span : share * span + few] = piece[:, 0:rows]
            outs[i][z, share * span + few :] = piece[:, rows : 2 * rows]


def query_gradient(offsets, got, qh, weights, pieces):
    keys = got[0].shape[1]
    heads, rows, depth = qh.shape
    share = heads // (RING * RING)
    tall = share * (rows // pieces) + heads // pieces
    return call(
        functools.partial(query_kernel, offsets, pieces),
        "query_gradient",
        24,
        in_specs=[VMEM] * (RING + 2),
        out_specs=[VMEM] * len(offsets),
        out_shape=[f32(pieces, tall, depth)] * len(offsets),
        scratch_shapes=[
            pltpu.VMEM((share * rows, RING * keys), jnp.bfloat16),
            pltpu.VMEM((share * rows, depth), jnp.float32),
            pltpu.VMEM((RING * keys, depth), jnp.bfloat16),
            pltpu.VMEM((rows, RING * keys), jnp.float32),
        ],
    )(*got, qh, weights)


def results_kernel(got_ref, query_ref, weight_ref):
    pieces, tall, depth = got_ref.shape
    span = query_ref.shape[1]
    few = (tall - span) // 2
    query_ref[...] = got_ref[:, 0:span]
    for z in range(pieces):
        weight_ref[z * few : (z + 1) * few] = got_ref[z, span : span + few]
        weight_ref[(pieces + z) * few : (pieces + z + 1) * few] = got_ref[z, span + few :]


def results(got, heads, span):
    pieces, _, depth = got.shape
    return call(
        results_kernel,
        "results",
        16,
        out_shape=(f32(pieces, span, depth), f32(heads, depth)),
    )(got)


def exchange(x, axis):
    return lax.all_to_all(x, axis, split_axis=0, concat_axis=0, tiled=True)


def shift(x, d, across):
    pairs = []
    for a in range(RING):
        for b in range(RING):
            for row in range(2):
                if (row == 1) != across:
                    there = (a + d) % RING * RING + b
                else:
                    there = a * RING + (b + d) % RING
                pairs.append(((a * RING + b) * 2 + row, there * 2 + row))
    return lax.ppermute(x, ("head", "row"), pairs)


def shards(mla_query, mla_cache, index_query, index_keys, index_weight):
    key_count = lax.axis_size("key")
    head_count = lax.axis_size("head")
    rows = mla_query.shape[0]
    keys, depth = index_keys.shape
    heads = index_query.shape[1]
    share = heads // head_count
    row_index = lax.axis_index("row")
    weights = index_weight.T
    queries = jnp.transpose(mla_query, (1, 2, 0))
    cache = jnp.swapaxes(mla_cache, 1, 2)
    terms, tops, send1, logits, qh = scores_and_logits(queries, cache, index_query, index_keys, weights, key_count)
    got1 = exchange(send1, "key")
    (far_two,) = head_sum((2,), terms, tops, got1)
    got1, _ = lax.optimization_barrier((got1, far_two))
    sides = head_sum((1, 3), terms, tops, got1)
    (own,) = head_sum((0,), terms, tops, got1)
    two = shift(far_two, 2, False)
    one = shift(sides[0], 1, False)
    three = shift(sides[1], 3, False)
    own, late = lax.optimization_barrier((own, qh))
    active = active_products(late, index_keys)
    got2, active = lax.optimization_barrier(([own, one, two, three], active))
    send2 = partial_sum(got2)
    two, one, three = [shift(send2[d], d, True) for d in (2, 1, 3)]
    got2 = [send2[0], one, two, three]
    key_total = float(keys * head_count * key_count)
    send3 = dlogits_of(got2, logits, active, index_keys, key_total)
    two, one, three = [shift(send3, d, False) for d in (2, 1, 3)]
    got3 = [send3, one, two, three]

    (far_two,) = query_gradient((2,), got3, qh, weights, key_count)
    got3, active, _ = lax.optimization_barrier((got3, active, far_two))
    sides = query_gradient((1, 3), got3, qh, weights, key_count)
    (own,) = query_gradient((0,), got3, qh, weights, key_count)
    two = shift(far_two, 2, True)
    one = shift(sides[0], 1, True)
    three = shift(sides[1], 3, True)
    active, _ = lax.optimization_barrier((active, own))
    keys_part = key_gradient(send3, active, qh, weights)
    two, keys_part = lax.optimization_barrier((two, keys_part))
    send4 = own + one + (two + three)

    half = keys // 2
    away = lax.dynamic_slice_in_dim(keys_part, (1 - row_index) * half, half, 0)
    near = lax.dynamic_slice_in_dim(keys_part, row_index * half, half, 0)
    key_grad = near + lax.ppermute(away, "row", [(0, 1), (1, 0)])

    got4 = jnp.sum(exchange(send4, "key"), axis=0)
    got5 = exchange(jnp.broadcast_to(got4[None], (key_count, *got4.shape)), "key")
    query_grad, weight_grad = results(got5, heads, share * (rows // key_count))
    return (query_grad.reshape(rows, share, depth), key_grad, weight_grad.T)


def solution(mesh):
    placed = (
        P("row", "head", None),
        P(None, "key", None),
        P("row", None, None),
        P(("head", "key"), None),
        P("row", None),
    )
    return jax.shard_map(
        shards,
        mesh=mesh,
        in_specs=placed,
        out_specs=(P("row", "head", None), P(("head", "key", "row"), None), P("row", None)),
        check_vma=False,
    )
```
